32 devices in a mesh: res: 2 (over core), dp: 16 (over z, y, x).
Axes of the slice: x: 2, y: 2, z: 4, core: 2. Of those that a mesh axis runs over, the one named last changes fastest.
Arguments:
- features: bfloat16 [2, 12544, 2048], P('res', 'dp'), may hold values from -6 to 6
- crop_counts: int32 [128], P('dp'), may hold values from 2 to 8, as said below
- crop_image: int32 [1024], P('dp'), may hold values from -1 to 127, as said below
- w_reduce: bfloat16 [2048, 512], replicated, may hold values from -0.125 to 0.125
- w_spatial: bfloat16 [4608, 512], replicated, may hold values from -0.09375 to 0.09375
- w_expand: bfloat16 [512, 2048], replicated, may hold values from -0.25 to 0.25
- w_hidden: bfloat16 [2048, 2048], replicated, may hold values from -0.125 to 0.125
- w_project: bfloat16 [2048, 128], replicated, may hold values from -0.125 to 0.125
- prototypes: bfloat16 [128, 3000], replicated, may hold values from -0.75 to 0.75
- norm_gain: float32 [5120], replicated, may hold values from 0.5 to 1.5
- norm_shift: float32 [5248], replicated, may hold values from -1.5 to 1.5
Outputs:
- loss: float32 [], replicated
- feature_grad: float32 [2, 12544, 2048], P('res', 'dp')
- reduce_grad: float32 [1048576], P(('res', 'dp'))
- spatial_grad: float32 [2359296], P(('res', 'dp'))
- expand_grad: float32 [1048576], P(('res', 'dp'))
- hidden_grad: float32 [4194304], P(('res', 'dp'))
- project_grad: float32 [262144], P(('res', 'dp'))
- prototype_grad: float32 [384000], replicated
- gain_grad: float32 [5120], replicated
- shift_grad: float32 [5248], replicated
The draws below stay inside these ranges and needn't reach their ends.
Inputs may be any that keep to these rules, and one draw needn't show every extreme that they name: `crop_counts`: each image has 2 to 8 small crops; some image has 8 and some has 2. `crop_image`: the 64 slots of dp index d hold images d * 8 to d * 8 + 7 in any order, image i in exactly crop_counts[i] of them; the other slots hold -1.
All inputs are finite; a program needn't handle non-finite values.
Results may differ from the reference program's by a relative error of at most 0.025.
Values sent between devices are 32-bit elements; how exact they have to be, the bound alone decides.
A program may use at most 192 MiB of HBM per device.

```python
import jax
import jax.numpy as jnp
from jax import lax

D = 2048
C = 512
H = 2048
PD = 128
PROTOS = 3000
IMG_DEV = 8
LSIDE = 7
SSIDE = 3
MOST = 8
SINK = 3
IMAGES = 128
ROWS = 784
ALL_ROWS = 12544
SLOT_DEV = 64
GAINS = 5120
SHIFTS = 5248
N_DP = 16


def crop_plan(key):
    plan_key = jax.random.fold_in(key, 4051)
    key_one, key_two, key_three = jax.random.split(plan_key, 3)
    fewer_crops = jnp.minimum(jax.random.randint(key_one, (IMAGES,), 0, MOST - 1), jax.random.randint(key_two, (IMAGES,), 0, MOST - 1))
    counts = (MOST - fewer_crops).at[0].set(MOST).at[1].set(2)
    groups = IMAGES // IMG_DEV
    per_image = counts.reshape(groups, IMG_DEV, 1)
    image_ids = jnp.arange(IMAGES, dtype=jnp.int32).reshape(groups, IMG_DEV, 1)
    position = jnp.arange(MOST, dtype=jnp.int32).reshape(1, 1, MOST)
    slot_table = jnp.where(position < per_image, image_ids, -1).reshape(groups, IMG_DEV * MOST)
    device_keys = jax.random.split(key_three, groups)
    orders = jax.vmap(lambda sub_key: jax.random.permutation(sub_key, IMG_DEV * MOST))(device_keys)
    slot_images = jnp.take_along_axis(slot_table, orders, axis=1).reshape(-1)
    return (counts.astype(jnp.int32), slot_images.astype(jnp.int32))


def draw_crop_counts(key, part):
    return crop_plan(key)[0]


def draw_crop_image(key, part):
    return crop_plan(key)[1]


def block_scale(own_key, dims, shards, least, largest):
    level = 1.0
    for dim, parts in shards:
        heights = jax.random.uniform(jax.random.fold_in(jax.random.fold_in(own_key, 6), dim), (parts,), jnp.float32, least / len(shards), largest / len(shards))
        level = level * jnp.repeat(jnp.exp(heights), dims[dim] // parts).reshape((-1,) + (1,) * (len(dims) - 1 - dim))
    return level


def noise(stream_key, dims, scale, reach, cuts=(), held_as=jnp.bfloat16):
    array = scale * jax.random.normal(stream_key, dims, jnp.float32)
    if cuts:
        array = array * block_scale(stream_key, dims, cuts, -0.22, 0.18)
    return jnp.clip(array, -reach, reach).astype(held_as)


def setup_inputs(seed: int = 0) -> dict:
    arg_keys = jax.random.split(jax.random.key(seed), 12)
    features = noise(arg_keys[0], (2, ALL_ROWS, D), 1.0, 6.0, ((0, 2), (1, 16)))
    crop_counts = draw_crop_counts(jax.random.fold_in(arg_keys[11], 71), 0)
    crop_image = draw_crop_image(jax.random.fold_in(arg_keys[11], 71), 0)
    w_reduce = noise(arg_keys[3], (D, C), D ** -0.5, 0.125)
    w_spatial = noise(arg_keys[4], (9 * C, C), (9 * C) ** -0.5, 0.09375)
    w_expand = noise(arg_keys[5], (C, D), C ** -0.5, 0.25)
    w_hidden = noise(arg_keys[6], (D, H), D ** -0.5, 0.125)
    w_project = noise(arg_keys[7], (H, PD), H ** -0.5, 0.125)
    prototypes = noise(arg_keys[8], (PD, PROTOS), (PD // 2) ** -0.5, 0.75)
    norm_gain = jnp.clip(1.0 + 0.1 * jax.random.normal(arg_keys[9], (GAINS,), jnp.float32), 0.5, 1.5)
    norm_shift = noise(arg_keys[10], (SHIFTS,), 0.3, 1.5, (), jnp.float32)
    return {"features": features, "crop_counts": crop_counts, "crop_image": crop_image, "w_reduce": w_reduce, "w_spatial": w_spatial, "w_expand": w_expand, "w_hidden": w_hidden, "w_project": w_project, "prototypes": prototypes, "norm_gain": norm_gain, "norm_shift": norm_shift}


@jax.custom_vjp
def low(v):
    return lax.optimization_barrier(v.astype(jnp.bfloat16)).astype(jnp.float32)

@jax.custom_vjp
def low_back(v):
    return v

def low_keep(v):
    return (low(v), None)

def low_pass(kept, grad):
    return (grad,)

def back_keep(v):
    return (v, None)

def back_low(kept, grad):
    return (low(grad),)
low.defvjp(low_keep, low_pass)
low_back.defvjp(back_keep, back_low)
HIGH = lax.Precision.HIGHEST
SOFTMAX_HEAT = 0.1
SHARPNESS = 0.05
EPS_NORM = 1e-05
EPS_UNIT = 1e-06

def product(left, right):
    return jnp.dot(left, right, precision=HIGH, preferred_element_type=jnp.float32)

def batch_norm(values, weight, gain_vec, shift_vec):
    row_total = jnp.sum(weight)
    mean_vec = lax.optimization_barrier(jnp.sum(values * weight, axis=0)) / row_total
    centred = values - mean_vec
    var_vec = lax.optimization_barrier(jnp.sum(weight * centred * centred, axis=0)) / row_total
    return centred * lax.rsqrt(var_vec + EPS_NORM) * gain_vec + shift_vec

def spatial_conv(acts, kernel, side):
    channels = acts.shape[-1]
    grid = acts.reshape(-1, side, side, channels)
    padded = jnp.pad(grid, ((0, 0), (1, 1), (1, 1), (0, 0)))
    pieces = [padded[:, tap_y:tap_y + side, tap_x:tap_x + side, :] for tap_y in range(3) for tap_x in range(3)]
    stacked = jnp.concatenate(pieces, axis=-1).reshape(-1, 9 * channels)
    return product(stacked, kernel)

def split_norms(vector, width, depth):
    return (vector[:width], vector[width:2 * width], vector[2 * width:2 * width + depth], vector[2 * width + depth:])

def tower(inputs, row_weight, crop_weight, side, params):
    w_reduce, w_spatial, w_expand, w_hidden, w_project, prototypes, norm_gain, norm_shift = params
    depth = w_reduce.shape[0]
    width = w_reduce.shape[1]
    hidden = w_hidden.shape[1]
    gain_one, gain_two, gain_three, gain_four = split_norms(norm_gain, width, depth)
    shift_one, shift_two, shift_three, shift_rest = split_norms(norm_shift, width, depth)
    shift_four = shift_rest[:hidden]
    head_bias = shift_rest[hidden:]
    conv_one = low_back(product(inputs, w_reduce))
    act_one = low(jax.nn.gelu(batch_norm(conv_one, row_weight, gain_one, shift_one)))
    conv_two = low_back(spatial_conv(act_one, w_spatial, side))
    act_two = low(jax.nn.gelu(batch_norm(conv_two, row_weight, gain_two, shift_two)))
    conv_three = low_back(product(act_two, w_expand))
    block_out = jax.nn.gelu(batch_norm(conv_three, row_weight, gain_three, shift_three) + inputs)
    pooled = low(lax.optimization_barrier(jnp.mean(block_out.reshape(-1, side * side, depth), axis=1)))
    head_one = low_back(product(pooled, w_hidden))
    act_four = low(jax.nn.gelu(batch_norm(head_one, crop_weight, gain_four, shift_four)))
    head_two = low_back(product(act_four, w_project)) + head_bias
    unit = low(head_two * lax.rsqrt(lax.optimization_barrier(jnp.sum(head_two * head_two, axis=1, keepdims=True)) + EPS_UNIT))
    return low_back(product(unit, prototypes))

def balanced_assign(view_crop_scores):
    table = jnp.exp(view_crop_scores / SHARPNESS)
    for sweep in range(SINK):
        table = table / lax.optimization_barrier(jnp.sum(table, axis=1, keepdims=True))
        table = table / lax.optimization_barrier(jnp.sum(table, axis=2, keepdims=True))
    return table

def arrange_layout(large_crop_scores):
    return large_crop_scores.reshape(N_DP, 2, IMG_DEV, PROTOS).transpose(1, 0, 2, 3).reshape(2, IMAGES, PROTOS)

def reference(features, crop_counts, crop_image, w_reduce, w_spatial, w_expand, w_hidden, w_project, prototypes, norm_gain, norm_shift):
    large_rows = features[0].astype(jnp.float32)
    slot_rows = SSIDE * SSIDE * SLOT_DEV
    small_rows = features[1].astype(jnp.float32).reshape(N_DP, ROWS, D)[:, :slot_rows].reshape(-1, D)
    live_slot = (crop_image >= 0).astype(jnp.float32)
    small_weight = jnp.repeat(live_slot, SSIDE * SSIDE)[:, None]
    large_weight = jnp.ones((ALL_ROWS, 1), jnp.float32)
    large_crop_weight = jnp.ones((2 * IMAGES, 1), jnp.float32)
    weights = (w_reduce.astype(jnp.float32), w_spatial.astype(jnp.float32), w_expand.astype(jnp.float32), w_hidden.astype(jnp.float32), w_project.astype(jnp.float32), prototypes.astype(jnp.float32), norm_gain.astype(jnp.float32), norm_shift.astype(jnp.float32))

    def forward(large_in, small_in, *params):
        large_crop_scores = tower(large_in, large_weight, large_crop_weight, LSIDE, params)
        small_scores = tower(small_in, small_weight, live_slot[:, None], SSIDE, params)
        return (large_crop_scores, small_scores)
    (large_crop_scores, small_scores), pull_net = jax.vjp(forward, large_rows, small_rows, *weights)
    cluster_codes = balanced_assign(arrange_layout(large_crop_scores))
    image_weight = 1.0 / (2.0 * (1.0 + crop_counts.astype(jnp.float32)))
    image_index = jnp.maximum(crop_image, 0).astype(jnp.int32)
    targets = (cluster_codes[0] + cluster_codes[1])[image_index]
    slot_weight = image_weight[image_index] * live_slot

    def objective(large_share, small_share):
        view_log_probability = jax.nn.log_softmax(arrange_layout(large_share) / SOFTMAX_HEAT, axis=-1)
        large_terms = -lax.optimization_barrier(jnp.sum(cluster_codes[0] * view_log_probability[1], axis=-1)) - lax.optimization_barrier(jnp.sum(cluster_codes[1] * view_log_probability[0], axis=-1))
        small_log_probability = jax.nn.log_softmax(small_share / SOFTMAX_HEAT, axis=-1)
        small_terms = -lax.optimization_barrier(jnp.sum(targets * small_log_probability, axis=-1)) * slot_weight
        return jnp.sum(image_weight * large_terms) + jnp.sum(small_terms)
    summed, pull_loss = jax.vjp(objective, large_crop_scores, small_scores)
    score_grads = pull_loss(jnp.ones_like(summed))
    grads = pull_net(score_grads)
    small_back = grads[1].reshape(N_DP, slot_rows, D)
    padding = jnp.zeros((N_DP, ROWS - slot_rows, D), small_back.dtype)
    small_full = jnp.concatenate([small_back, padding], axis=1).reshape(ALL_ROWS, D)
    feature_grad = jnp.stack([grads[0], small_full])
    loss = summed / IMAGES
    return (loss, feature_grad, grads[2].reshape(-1), grads[3].reshape(-1), grads[4].reshape(-1), grads[5].reshape(-1), grads[6].reshape(-1), grads[7].reshape(-1), grads[8], grads[9])
```

```python
import jax
import jax.numpy as jnp
from jax import lax
from jax.experimental import pallas as pl
from jax.experimental.pallas import tpu as pltpu
from jax.sharding import PartitionSpec as P

LSIDE = 7
SSIDE = 3
SINK = 3


HIGH = lax.Precision.HIGHEST
SOFTMAX_HEAT = 0.1
SHARPNESS = 0.05
EPS_NORM = 1e-05
EPS_UNIT = 1e-06


def combined_all(part, axis, combine):
    gathered = jax.tree.map(lambda a: lax.all_gather(a, axis), part)

    def take(source):
        return jax.tree.map(lambda a: lax.dynamic_index_in_dim(a, source, 0, False), gathered)

    return lax.fori_loop(
        1, lax.axis_size(axis), lambda source, state: combine(state, take(source)), take(0)
    )


def from_behind(value, axis, steps):
    count = lax.axis_size(axis)
    leading, last = (max(0, -steps), min(count, count - steps))
    return lax.ppermute(value, axis, [(source, source + steps) for source in range(leading, last)])


def row_contract(left, right):
    return lax.dot_general(
        left, right, (((0,), (0,)), ((), ())), preferred_element_type=jnp.float32
    )


def times_transposed(left, right):
    return lax.dot_general(
        left, right, (((1,), (1,)), ((), ())), preferred_element_type=jnp.float32
    )


def split_norms(vector, width, depth):
    return (
        vector[:width],
        vector[width : 2 * width],
        vector[2 * width : 2 * width + depth],
        vector[2 * width + depth :],
    )


def displaced(values, offset):
    if offset == 0:
        return values
    filler = jnp.zeros((abs(offset),) + values.shape[1:], values.dtype)
    if offset > 0:
        return jnp.concatenate([values[offset:], filler], axis=0)
    return jnp.concatenate([filler, values[:offset]], axis=0)


def tap_layout(row_count, big_crop):
    row_ids = jnp.arange(row_count)
    side_len = jnp.where(big_crop, LSIDE, SSIDE)
    pixel = row_ids % (side_len * side_len)
    line_ids = pixel // side_len
    column_ids = pixel % side_len
    layout = []
    for tap_y in (-1, 0, 1):
        for tap_x in (-1, 0, 1):
            inside = (
                (line_ids + tap_y >= 0)
                & (line_ids + tap_y < side_len)
                & (column_ids + tap_x >= 0)
                & (column_ids + tap_x < side_len)
            )
            layout.append((inside[:, None], tap_y * LSIDE + tap_x, tap_y * SSIDE + tap_x))
    return layout


def gather_taps(acts, layout, big_crop):
    pieces = []
    for inside, step_large, step_small in layout:
        moved_rows = jnp.where(big_crop, displaced(acts, step_large), displaced(acts, step_small))
        pieces.append(jnp.where(inside, moved_rows, jnp.zeros_like(moved_rows)))
    return jnp.concatenate(pieces, axis=1)


def scatter_taps(column_grad, layout, big_crop, channels):
    result = jnp.zeros((column_grad.shape[0], channels), jnp.float32)
    for tap_index, (inside, step_large, step_small) in enumerate(layout):
        piece = column_grad[:, tap_index * channels : (tap_index + 1) * channels]
        piece = jnp.where(inside, piece, jnp.zeros_like(piece))
        result = result + jnp.where(
            big_crop, displaced(piece, -step_large), displaced(piece, -step_small)
        )
    return result


def merge_moments(first_part, second_part):
    merged_count = first_part[0] + second_part[0]
    delta = second_part[1] - first_part[1]
    merged_mean = first_part[1] + delta * (second_part[0] / merged_count)
    merged_spread = (
        first_part[2]
        + second_part[2]
        + delta * delta * (first_part[0] * second_part[0] / merged_count)
    )
    return (merged_count, merged_mean, merged_spread)


def moments(values, weight):
    row_total = jnp.sum(weight)
    local_mean = jnp.sum(values * weight, axis=0) / row_total
    centred = values - local_mean
    local_spread = jnp.sum(weight * centred * centred, axis=0)
    whole_count, mean_vec, whole_spread = combined_all(
        (row_total, local_mean, local_spread), "dp", merge_moments
    )
    return (mean_vec, whole_spread / whole_count, whole_count)


def normalize(values, weight, gain_vec, shift_vec):
    mean_vec, var_vec, whole_count = moments(values, weight)
    scale_vec = lax.rsqrt(var_vec + EPS_NORM)
    centred = (values - mean_vec) * scale_vec
    return (centred * gain_vec + shift_vec, (centred, scale_vec, whole_count))


def normalize_back(upstream, weight, gain_vec, saved_stats):
    centred, scale_vec, whole_count = saved_stats
    upstream = upstream * weight
    local_first = jnp.sum(upstream, axis=0)
    local_second = jnp.sum(upstream * centred, axis=0)
    whole_first, whole_second = lax.psum((local_first, local_second), "dp")
    result = (
        gain_vec
        * scale_vec
        * (upstream - weight * (whole_first + centred * whole_second) / whole_count)
    )
    return (result, local_second, local_first)


def gelu_back(before, upstream):
    return jax.vjp(jax.nn.gelu, before)[1](upstream)[0]


def spread_rows(crop_grad, crop_total, area):
    depth = crop_grad.shape[1]
    widened = jnp.broadcast_to(crop_grad[:crop_total, None, :], (crop_total, area, depth))
    return widened.reshape(crop_total * area, depth) / area


def body(
    features,
    crop_counts,
    crop_image,
    w_reduce,
    w_spatial,
    w_expand,
    w_hidden,
    w_project,
    prototypes,
    norm_gain,
    norm_shift,
):
    inputs = features[0]
    row_count = inputs.shape[0]
    depth = w_reduce.shape[0]
    width = w_reduce.shape[1]
    hidden = w_hidden.shape[1]
    slot_count = crop_image.shape[0]
    image_count = crop_counts.shape[0]
    image_total = image_count * lax.axis_size("dp")
    big_crop = lax.axis_index("res") == 0
    first_image = lax.axis_index("dp") * image_count
    live_slot = (crop_image >= 0).astype(jnp.float32)
    slot_rows = SSIDE * SSIDE * slot_count
    live_rows = jnp.concatenate(
        [jnp.repeat(live_slot, SSIDE * SSIDE), jnp.zeros((row_count - slot_rows,), jnp.float32)]
    )
    row_weight = jnp.where(big_crop, jnp.ones_like(live_rows), live_rows)[:, None]
    large_crops = (jnp.arange(slot_count) < 2 * image_count).astype(jnp.float32)
    crop_weight = jnp.where(big_crop, large_crops, live_slot)[:, None]
    gain_one, gain_two, gain_three, gain_four = split_norms(norm_gain, width, depth)
    shift_one, shift_two, shift_three, shift_rest = split_norms(norm_shift, width, depth)
    shift_four = shift_rest[:hidden]
    head_bias = shift_rest[hidden:]
    layout = tap_layout(row_count, big_crop)
    conv_one = jnp.dot(inputs, w_reduce, preferred_element_type=jnp.float32)
    norm_one, saved_one = normalize(conv_one, row_weight, gain_one, shift_one)
    act_one = jax.nn.gelu(norm_one).astype(jnp.bfloat16)
    columns = gather_taps(act_one, layout, big_crop)
    conv_two = jnp.dot(columns, w_spatial, preferred_element_type=jnp.float32)
    norm_two, saved_two = normalize(conv_two, row_weight, gain_two, shift_two)
    act_two = jax.nn.gelu(norm_two).astype(jnp.bfloat16)
    conv_three = jnp.dot(act_two, w_expand, preferred_element_type=jnp.float32)
    norm_three, saved_three = normalize(conv_three, row_weight, gain_three, shift_three)
    joined = norm_three + inputs.astype(jnp.float32)
    block_out = jax.nn.gelu(joined)
    large_pool = jnp.mean(block_out.reshape(2 * image_count, LSIDE * LSIDE, depth), axis=1)
    large_pool = jnp.concatenate(
        [large_pool, jnp.zeros((slot_count - 2 * image_count, depth), jnp.float32)], axis=0
    )
    small_pool = jnp.mean(block_out[:slot_rows].reshape(slot_count, SSIDE * SSIDE, depth), axis=1)
    pooled = jnp.where(big_crop, large_pool, small_pool).astype(jnp.bfloat16)
    head_one = jnp.dot(pooled, w_hidden, preferred_element_type=jnp.float32)
    norm_four, saved_four = normalize(head_one, crop_weight, gain_four, shift_four)
    act_four = jax.nn.gelu(norm_four).astype(jnp.bfloat16)
    head_two = jnp.dot(act_four, w_project, preferred_element_type=jnp.float32) + head_bias
    unit, unit_back = jax.vjp(
        lambda vec: vec * lax.rsqrt(jnp.sum(vec * vec, axis=1, keepdims=True) + EPS_UNIT), head_two
    )
    unit_low = unit.astype(jnp.bfloat16)
    scores = jnp.dot(unit_low, prototypes, preferred_element_type=jnp.float32)
    table = jnp.exp(scores[: 2 * image_count].reshape(2, image_count, -1) / SHARPNESS)
    for sweep in range(SINK):
        column_total = lax.psum(jnp.sum(table, axis=1), "dp")
        table = table / column_total[:, None, :]
        table = table / jnp.sum(table, axis=2, keepdims=True)
    own_codes = table
    far_codes = from_behind(own_codes, "res", 1)
    weight_image = 1.0 / (2.0 * (1.0 + crop_counts.astype(jnp.float32)))
    onehot = ((crop_image - first_image)[:, None] == jnp.arange(image_count)[None, :]).astype(
        jnp.float32
    )
    slot_scale = jnp.dot(onehot, weight_image, precision=HIGH) * live_slot
    small_targets = jnp.dot(onehot, far_codes[0] + far_codes[1], precision=HIGH)

    def partial_loss(scores_by_row):
        log_probability = jax.nn.log_softmax(scores_by_row / SOFTMAX_HEAT, axis=-1)
        view_zero = log_probability[:image_count]
        view_one = log_probability[image_count : 2 * image_count]
        large_share = -jnp.sum(
            weight_image
            * (
                jnp.sum(own_codes[0] * view_one, axis=-1)
                + jnp.sum(own_codes[1] * view_zero, axis=-1)
            )
        )
        small_share = -jnp.sum(slot_scale * jnp.sum(small_targets * log_probability, axis=-1))
        return jnp.where(big_crop, large_share, small_share)

    local_total, total_back = jax.vjp(partial_loss, scores)
    whole_total = lax.psum(local_total, ("res", "dp"))
    loss = whole_total / image_total
    score_grad = total_back(jnp.ones_like(local_total))[0].astype(jnp.bfloat16)
    proto_grad = row_contract(unit_low, score_grad)
    unit_grad = times_transposed(score_grad, prototypes)
    head_two_grad = unit_back(unit_grad)[0]
    bias_grad = jnp.sum(head_two_grad, axis=0)
    head_two_low = head_two_grad.astype(jnp.bfloat16)
    project_grad = row_contract(act_four, head_two_low)
    act_four_grad = times_transposed(head_two_low, w_project)
    head_one_grad, gain_four_grad, shift_four_grad = normalize_back(
        gelu_back(norm_four, act_four_grad), crop_weight, gain_four, saved_four
    )
    head_one_low = head_one_grad.astype(jnp.bfloat16)
    hidden_grad = row_contract(pooled, head_one_low)
    pooled_grad = times_transposed(head_one_low, w_hidden)
    large_spread = spread_rows(pooled_grad, 2 * image_count, LSIDE * LSIDE)
    small_spread = jnp.concatenate(
        [
            spread_rows(pooled_grad, slot_count, SSIDE * SSIDE),
            jnp.zeros((row_count - slot_rows, depth), jnp.float32),
        ],
        axis=0,
    )
    out_grad = jnp.where(big_crop, large_spread, small_spread)
    joined_grad = gelu_back(joined, out_grad)
    three_grad, gain_three_grad, shift_three_grad = normalize_back(
        joined_grad, row_weight, gain_three, saved_three
    )
    three_low = three_grad.astype(jnp.bfloat16)
    expand_grad = row_contract(act_two, three_low)
    act_two_grad = times_transposed(three_low, w_expand)
    two_grad, gain_two_grad, shift_two_grad = normalize_back(
        gelu_back(norm_two, act_two_grad), row_weight, gain_two, saved_two
    )
    two_low = two_grad.astype(jnp.bfloat16)
    spatial_grad = row_contract(columns, two_low)
    column_grad = times_transposed(two_low, w_spatial)
    act_one_grad = scatter_taps(column_grad, layout, big_crop, width)
    one_grad, gain_one_grad, shift_one_grad = normalize_back(
        gelu_back(norm_one, act_one_grad), row_weight, gain_one, saved_one
    )
    one_low = one_grad.astype(jnp.bfloat16)
    reduce_grad = row_contract(inputs, one_low)
    input_grad = (joined_grad + times_transposed(one_low, w_reduce)) * row_weight
    weight_terms = (
        reduce_grad.reshape(-1),
        spatial_grad.reshape(-1),
        expand_grad.reshape(-1),
        hidden_grad.reshape(-1),
        project_grad.reshape(-1),
    )
    summed = (
        lax.psum_scatter(weight_terms[0], ("res", "dp"), scatter_dimension=0, tiled=True),
        lax.psum_scatter(weight_terms[1], ("res", "dp"), scatter_dimension=0, tiled=True),
        lax.psum_scatter(weight_terms[2], ("res", "dp"), scatter_dimension=0, tiled=True),
        lax.psum_scatter(weight_terms[3], ("res", "dp"), scatter_dimension=0, tiled=True),
        lax.psum_scatter(weight_terms[4], ("res", "dp"), scatter_dimension=0, tiled=True),
    )
    gain_local = jnp.concatenate([gain_one_grad, gain_two_grad, gain_three_grad, gain_four_grad])
    shift_local = jnp.concatenate(
        [shift_one_grad, shift_two_grad, shift_three_grad, shift_four_grad, bias_grad]
    )
    gain_total, shift_total, proto_total = lax.psum(
        (gain_local, shift_local, proto_grad.reshape(-1)), ("res", "dp")
    )
    return (
        loss,
        input_grad[None],
        summed[0],
        summed[1],
        summed[2],
        summed[3],
        summed[4],
        proto_total,
        gain_total,
        shift_total,
    )


MESH = pl.DeviceIdType.MESH
BF = jnp.bfloat16
F32 = jnp.float32
GROUP = 16
ROWS = 784
WIDTH = 512
DEPTH = 2048
HIDDEN = 2048
FEATS = 128
SLOTS = 64
IMAGES = 8
PROTOS = 3000
PADDED = 3072
LANES = 128
EDGE = 16
STRIPE = 112
TANH_IN = 0.7978845608
TANH_CUBE = 0.044715

X_COUNT, X_ONE, X_TWO, X_THREE, X_FOUR = 0, 1, 2, 3, 7
X_FOUR_BACK, X_EXTRA, X_THREE_BACK, X_TWO_BACK, X_ONE_BACK, EXCHANGES = 11, 15, 16, 20, 21, 22


def mm(left, right):
    return jnp.dot(left, right, preferred_element_type=F32)


def mm_t(left, right):
    return lax.dot_general(left, right, (((1,), (1,)), ((), ())), preferred_element_type=F32)


def t_mm(left, right):
    return lax.dot_general(left, right, (((0,), (0,)), ((), ())), preferred_element_type=F32)


def gelu(v):
    return 0.5 * v * (1.0 + jnp.tanh(TANH_IN * (v + TANH_CUBE * (v * v * v))))


def gelu_slope(v):
    square = v * v
    t = jnp.tanh(TANH_IN * (v + TANH_CUBE * (v * square)))
    return 0.5 * (1.0 + t) + 0.5 * v * (1.0 - t * t) * (
        TANH_IN * (1.0 + (3.0 * TANH_CUBE) * square)
    )


def two_parts(v):
    high = v.astype(BF)
    return high, (v - high.astype(F32)).astype(BF)


def at(start, size):
    return pl.ds(pl.multiple_of(start, size if size % 8 == 0 else 8), size)


def lanes(index, width=LANES):
    if isinstance(index, int):
        return slice(index * width, (index + 1) * width)
    return pl.ds(pl.multiple_of(index * width, width), width)


def tower_kernel(
    feat,
    crop_row,
    count_row,
    w_reduce,
    w_spatial,
    w_expand,
    w_hidden,
    w_project,
    protos,
    gain,
    shift,
    loss_out,
    feature_out,
    reduce_out,
    spatial_out,
    expand_out,
    hidden_out,
    project_out,
    proto_out,
    gain_out,
    shift_out,
    F,
    WR,
    WS,
    WE,
    WH,
    WP,
    PR,
    C1,
    C2,
    C3,
    DJ,
    DA,
    APAD,
    COLS,
    A2,
    A1T,
    PO,
    H1,
    A4,
    DA4,
    DH1,
    DP,
    SC,
    TG,
    DS,
    TAB,
    Q,
    RACC,
    RINV,
    UNITS,
    UOWN,
    RW,
    CW,
    LINE,
    COL,
    PT,
    P,
    PRM1,
    PRM2,
    PRM3,
    PRM4,
    MSG,
    RECV,
    OUTT,
    load_sem,
    send_sem,
    recv_sem,
    unit_sem,
    out_sem,
    far_sem,
    FAR,
):
    r = lax.axis_index("res")
    d = lax.axis_index("dp")
    big = r == 0
    area = jnp.where(big, LSIDE * LSIDE, SSIDE * SSIDE)
    area_f = area.astype(F32)
    side_f = jnp.where(big, float(LSIDE), float(SSIDE))
    area_inv = jnp.where(big, 1.0 / (LSIDE * LSIDE), 1.0 / (SSIDE * SSIDE))
    side_inv = jnp.where(big, 1.0 / LSIDE, 1.0 / SSIDE)

    loads = [
        pltpu.make_async_copy(source, target, load_sem.at[index])
        for index, (source, target) in enumerate(
            [
                (feat.at[0], F),
                (w_reduce, WR),
                (w_spatial, WS),
                (w_expand, WE),
                (w_hidden, WH),
                (w_project, WP),
                (protos, PR),
            ]
        )
    ]
    for load in loads:
        load.start()

    barrier = pltpu.get_barrier_semaphore()

    @pl.loop(1, GROUP)
    def _(k):
        pl.semaphore_signal(
            barrier, inc=1, device_id=(r, lax.rem(d + k, GROUP)), device_id_type=MESH
        )

    pl.semaphore_signal(barrier, inc=1, device_id=(1 - r, d), device_id_type=MESH)

    slot_of = lax.broadcasted_iota(jnp.int32, (ROWS, SLOTS), 1)
    row_of = lax.broadcasted_iota(jnp.int32, (ROWS, SLOTS), 0)
    inside = ((row_of >= slot_of * area) & (row_of < slot_of * area + area)).astype(F32)
    lane_ids = lax.broadcasted_iota(jnp.int32, (1, SLOTS), 1)
    crop_ids = crop_row[...]
    live = jnp.where(big, (lane_ids < 2 * IMAGES).astype(F32), (crop_ids >= 0).astype(F32))
    RW[...] = jnp.broadcast_to(jnp.sum(inside * live, axis=1, keepdims=True), (ROWS, LANES))
    PT[...] = inside.astype(BF)
    slot_row = lax.broadcasted_iota(jnp.int32, (SLOTS, ROWS), 0)
    pixel_lane = lax.broadcasted_iota(jnp.int32, (SLOTS, ROWS), 1)
    P[...] = (
        ((pixel_lane >= slot_row * area) & (pixel_lane < slot_row * area + area))
        .astype(F32)
        .astype(BF)
    )
    square_row = lax.broadcasted_iota(jnp.int32, (SLOTS, SLOTS), 0)
    square_lane = lax.broadcasted_iota(jnp.int32, (SLOTS, SLOTS), 1)
    eye = (square_row == square_lane).astype(F32)
    CW[...] = jnp.broadcast_to(jnp.sum(eye * live, axis=1, keepdims=True), (SLOTS, LANES))
    live_total = jnp.sum(live, axis=1, keepdims=True)
    own_crops = jnp.broadcast_to(live_total, (1, LANES))
    own_rows = own_crops * area_f
    row_f = lax.broadcasted_iota(jnp.int32, (ROWS, LANES), 0).astype(F32)
    pixel = row_f - jnp.floor((row_f + 0.5) * area_inv) * area_f
    line = jnp.floor((pixel + 0.5) * side_inv)
    LINE[...] = line
    COL[...] = pixel - line * side_f
    APAD[0:EDGE, :] = jnp.zeros((EDGE, WIDTH), F32)
    APAD[EDGE + ROWS :, :] = jnp.zeros((EDGE, WIDTH), F32)
    for prm, base, blocks in ((PRM1, 0, 4), (PRM2, 4, 4), (PRM3, 8, 16), (PRM4, 24, 16)):
        for q in range(blocks):
            prm[q, 2:3, :] = gain[base + q : base + q + 1, :]
            prm[q, 3:4, :] = shift[base + q : base + q + 1, :]
    MSG[X_COUNT] = jnp.broadcast_to(own_rows, (8, LANES))

    pl.semaphore_wait(barrier, GROUP)

    def announce(x):
        @pl.loop(1, GROUP)
        def _(k):
            pltpu.make_async_remote_copy(
                MSG.at[x],
                RECV.at[x, d],
                send_sem.at[x],
                recv_sem.at[x],
                device_id=(r, lax.rem(d + k, GROUP)),
                device_id_type=MESH,
            ).start()

        RECV[x, d] = MSG[x]

    def collect(x):
        others = RECV.at[x, pl.ds(0, GROUP - 1)]
        pltpu.make_async_copy(others, others, recv_sem.at[x]).wait()
        pltpu.make_async_copy(others, others, send_sem.at[x]).wait()

    announce(X_COUNT)

    def local_moments(values, rows, first_lane, weight, own, x):
        for q in range(4):
            v = values[rows, first_lane + q * LANES : first_lane + (q + 1) * LANES]
            w = weight[...]
            total = jnp.sum(v * w, axis=0, keepdims=True)
            centred = (v - total / own) * w
            MSG[x, q : q + 1, :] = total
            MSG[x, 4 + q : 5 + q, :] = jnp.sum(centred * centred, axis=0, keepdims=True)

    def whole_moments(x, counts, prm, first):
        whole = jnp.sum(counts, axis=0, keepdims=True)
        each = counts[:, None, :]
        sums = RECV[x, :, 0:4, :]
        spreads = RECV[x, :, 4:8, :]
        mean = jnp.sum(sums, axis=0) / whole
        off = sums / each - mean[None]
        var = jnp.sum(spreads + each * off * off, axis=0) / whole
        scale = lax.rsqrt(var + EPS_NORM)
        for q in range(4):
            prm[first + q, 0:1, :] = mean[q : q + 1]
            prm[first + q, 1:2, :] = scale[q : q + 1]

    def whole_back(x, whole, prm, first, place):
        ones = jnp.sum(RECV[x, :, 0:4, :], axis=0)
        twos = jnp.sum(RECV[x, :, 4:8, :], axis=0)
        for q in range(4):
            prm[first + q, 4:5, :] = ones[q : q + 1] / whole
            prm[first + q, 5:6, :] = twos[q : q + 1] / whole
        FAR[0, pl.ds(place, 4), :] = twos
        FAR[0, pl.ds(48 + place, 4), :] = ones

    def norm_terms(v, prm, index):
        centred = (v - prm[index, 0:1, :]) * prm[index, 1:2, :]
        return centred, centred * prm[index, 2:3, :] + prm[index, 3:4, :]

    def back_through(du, centred, weight, prm, index):
        inner = du - weight * (prm[index, 4:5, :] + centred * prm[index, 5:6, :])
        return prm[index, 2:3, :] * prm[index, 1:2, :] * inner

    def spread_taps(sign):
        def for_side(side):
            @pl.loop(0, ROWS // STRIPE)
            def _(s):
                base = pl.multiple_of(s * STRIPE, STRIPE)
                rows = pl.ds(base, STRIPE)
                window = pl.ds(base, STRIPE + 2 * EDGE)
                for tap in range(9):
                    dy, dx = sign * (tap // 3 - 1), sign * (tap % 3 - 1)
                    y = LINE[rows, :] + float(dy)
                    x = COL[rows, :] + float(dx)
                    keep = (y >= 0.0) & (y < float(side)) & (x >= 0.0) & (x < float(side))
                    start = EDGE + dy * side + dx
                    for q in range(4):
                        moved = APAD[window, lanes(q)][start : start + STRIPE]
                        COLS[rows, tap * WIDTH + q * LANES : tap * WIDTH + (q + 1) * LANES] = (
                            jnp.where(keep, moved, 0.0).astype(BF)
                        )

        @pl.when(big)
        def _():
            for_side(LSIDE)

        @pl.when(jnp.logical_not(big))
        def _():
            for_side(SSIDE)

    loads[0].wait()
    loads[1].wait()
    C1[...] = mm(F[...], WR[...])
    every = pl.ds(0, ROWS)
    local_moments(C1, every, 0, RW, own_rows, X_ONE)
    announce(X_ONE)
    collect(X_COUNT)
    row_counts = RECV[X_COUNT, :, 0, :]
    crop_counts = row_counts * area_inv
    whole_rows = jnp.sum(row_counts, axis=0, keepdims=True)
    whole_crops = jnp.sum(crop_counts, axis=0, keepdims=True)
    collect(X_ONE)
    whole_moments(X_ONE, row_counts, PRM1, 0)
    for q in range(4):
        _, before = norm_terms(C1[:, lanes(q)], PRM1, q)
        act = gelu(before)
        APAD[EDGE : EDGE + ROWS, lanes(q)] = act
        A1T[lanes(q), :] = act.astype(BF).T
    spread_taps(1)
    loads[2].wait()

    @pl.loop(0, 2)
    def _(h):
        C2[:, lanes(h, 256)] = mm(COLS[...], WS[:, lanes(h, 256)])

    local_moments(C2, every, 0, RW, own_rows, X_TWO)
    announce(X_TWO)
    collect(X_TWO)
    whole_moments(X_TWO, row_counts, PRM2, 0)
    for q in range(4):
        _, before = norm_terms(C2[:, lanes(q)], PRM2, q)
        A2[:, lanes(q)] = gelu(before).astype(BF)
    loads[3].wait()

    @pl.loop(0, 4)
    def _(j):
        rows = at(j * ROWS, ROWS)
        C3[rows, :] = mm(A2[...], WE[:, lanes(j, WIDTH)])
        local_moments(C3, rows, 0, RW, own_rows, X_THREE + j)
        announce(X_THREE + j)

    @pl.loop(0, 4)
    def _(j):
        collect(X_THREE + j)
        whole_moments(X_THREE + j, row_counts, PRM3, 4 * j)
        rows = at(j * ROWS, ROWS)
        for q in range(4):
            _, before = norm_terms(C3[rows, lanes(q)], PRM3, 4 * j + q)
            joined = before + F[:, lanes(4 * j + q)].astype(F32)
            high, low = two_parts(gelu(joined))
            pooled = (mm(P[...], high) + mm(P[...], low)) * area_inv
            PO[:, lanes(4 * j + q)] = pooled.astype(BF)

    loads[4].wait()

    @pl.loop(0, 4)
    def _(j):
        H1[j] = mm(PO[...], WH[:, lanes(j, WIDTH)])
        local_moments(H1.at[j], pl.ds(0, SLOTS), 0, CW, own_crops, X_FOUR + j)
        announce(X_FOUR + j)

    @pl.loop(0, 4)
    def _(j):
        collect(X_FOUR + j)
        whole_moments(X_FOUR + j, crop_counts, PRM4, 4 * j)
        for q in range(4):
            _, before = norm_terms(H1[j, :, lanes(q)], PRM4, 4 * j + q)
            A4[:, lanes(4 * j + q)] = gelu(before).astype(BF)

    loads[5].wait()
    loads[6].wait()
    head_two = mm(A4[...], WP[...]) + shift[40:41, :]
    length_inv = lax.rsqrt(jnp.sum(head_two * head_two, axis=1, keepdims=True) + EPS_UNIT)
    unit = head_two * length_inv
    unit_low = unit.astype(BF)
    UOWN[...] = unit_low[0 : 2 * IMAGES].astype(F32)

    def unit_copy(k):
        return pltpu.make_async_remote_copy(
            UOWN,
            UNITS.at[d],
            unit_sem.at[0],
            unit_sem.at[1],
            device_id=(r, lax.rem(d + k, GROUP)),
            device_id_type=MESH,
        )

    forward_units = pltpu.make_async_remote_copy(
        UNITS, UNITS, unit_sem.at[2], unit_sem.at[3], device_id=(1 - r, d), device_id_type=MESH
    )

    @pl.when(big)
    def _():
        @pl.loop(1, GROUP)
        def _(k):
            unit_copy(k).start()

        UNITS[d] = UOWN[...]

    SC[...] = mm(unit_low, PR[...])

    @pl.when(big)
    def _():
        others = UNITS.at[pl.ds(0, GROUP - 1)]
        pltpu.make_async_copy(others, others, unit_sem.at[1]).wait()
        pltpu.make_async_copy(others, others, unit_sem.at[0]).wait()
        forward_units.start()

    @pl.when(jnp.logical_not(big))
    def _():
        forward_units.wait_recv()

    chunk = 512
    chunks = PADDED // chunk
    images = GROUP * IMAGES
    chunk_lane = lax.broadcasted_iota(jnp.int32, (1, chunk), 1)

    @pl.loop(0, 2)
    def _(v):
        view = UNITS[:, pl.ds(pl.multiple_of(v * IMAGES, IMAGES), IMAGES), :]
        view = view.reshape(images, FEATS).astype(BF)

        def sweep(first):
            RACC[...] = jnp.zeros_like(RACC)

            @pl.loop(0, chunks)
            def _(c):
                columns = lanes(c, chunk)
                valid = (chunk_lane + c * chunk) < PROTOS
                if first:
                    table = jnp.exp(mm(view, PR[:, columns]) / SHARPNESS)
                else:
                    table = TAB[:, columns] * jnp.concatenate([RINV[...]] * 4, axis=1)
                total = jnp.sum(table, axis=0, keepdims=True)
                table = table * jnp.where(valid, 1.0 / total, 0.0)
                TAB[:, columns] = table
                RACC[...] += (
                    table[:, 0:128] + table[:, 128:256] + table[:, 256:384] + table[:, 384:512]
                )

            RINV[...] = jnp.broadcast_to(
                1.0 / jnp.sum(RACC[...], axis=1, keepdims=True), (images, LANES)
            )

        for number in range(SINK):
            sweep(number == 0)
        own = pl.ds(pl.multiple_of(d * IMAGES, IMAGES), IMAGES)
        row_inv = RINV[own, :][:, 0:1]
        Q[pl.ds(pl.multiple_of(v * IMAGES, IMAGES), IMAGES), :] = TAB[own, :] * row_inv

    ident_f = jnp.sum(eye * crop_ids.astype(F32), axis=1, keepdims=True)
    pick_lane = lax.broadcasted_iota(jnp.int32, (SLOTS, 2 * IMAGES), 1)
    pick_row = lax.broadcasted_iota(jnp.int32, (SLOTS, 2 * IMAGES), 0)
    image_lane = jnp.where(pick_lane < IMAGES, pick_lane, pick_lane - IMAGES)
    first_image = (d * IMAGES).astype(F32)
    crossed = (pick_row < 2 * IMAGES) & (jnp.abs(pick_row - pick_lane) == IMAGES)
    matched = ident_f == image_lane.astype(F32) + first_image
    picked = jnp.where(big, crossed.astype(F32), matched.astype(F32))
    image_weight = 1.0 / (2.0 * (1.0 + count_row[...].astype(F32)))
    picked = picked * jnp.concatenate([image_weight, image_weight], axis=1)
    TG[...] = jnp.dot(picked, Q[...], precision=HIGH, preferred_element_type=F32)
    valid_all = lax.broadcasted_iota(jnp.int32, (1, PADDED), 1) < PROTOS
    loss_rows = []
    for s in range(4):
        rows = slice(16 * s, 16 * s + 16)
        target = TG[rows, :]
        logit = jnp.where(valid_all, SC[rows, :] / SOFTMAX_HEAT, -1e30)
        shifted = logit - jnp.max(logit, axis=1, keepdims=True)
        raised = jnp.exp(shifted)
        total = jnp.sum(raised, axis=1, keepdims=True)
        loss_rows.append(jnp.sum(target * (shifted - jnp.log(total)), axis=1, keepdims=True))
        mass = jnp.sum(target, axis=1, keepdims=True)
        DS[rows, :] = ((raised * (mass / total) - target) / SOFTMAX_HEAT).astype(BF)
    loss_local = -jnp.sum(
        loss_rows[0] + loss_rows[1] + loss_rows[2] + loss_rows[3], axis=0, keepdims=True
    )

    OUTP = t_mm(unit_low, DS[...])
    PROTO_BUF = TAB
    PROTO_BUF[...] = OUTP
    proto_copy = pltpu.make_async_copy(PROTO_BUF, proto_out, out_sem.at[2])
    proto_copy.start()
    unit_grad = mm_t(DS[...], PR[...])
    along = jnp.sum(unit * unit_grad, axis=1, keepdims=True)
    head_two_grad = (unit_grad - unit * along) * length_inv
    bias_grad = jnp.sum(head_two_grad, axis=0, keepdims=True)
    MSG[X_EXTRA] = jnp.concatenate(
        [bias_grad, jnp.broadcast_to(loss_local, (1, LANES)), jnp.zeros((6, LANES), F32)], axis=0
    )
    announce(X_EXTRA)
    head_two_low = head_two_grad.astype(BF)

    @pl.loop(0, 4)
    def _(j):
        DA4[j] = mm_t(head_two_low, WP[at(j * WIDTH, WIDTH), :])
        for q in range(4):
            centred, before = norm_terms(H1[j, :, lanes(q)], PRM4, 4 * j + q)
            du = DA4[j, :, lanes(q)] * gelu_slope(before) * CW[...]
            DA4[j, :, lanes(q)] = du
            MSG[X_FOUR_BACK + j, q : q + 1, :] = jnp.sum(du, axis=0, keepdims=True)
            MSG[X_FOUR_BACK + j, 4 + q : 5 + q, :] = jnp.sum(du * centred, axis=0, keepdims=True)
        announce(X_FOUR_BACK + j)

    project_buf = OUTT.at[0]
    for j in range(4):
        project_buf[:, lanes(j)] = t_mm(A4[:, lanes(j, WIDTH)], head_two_low)
    project_copies = [
        pltpu.make_async_copy(
            project_buf.at[:, lanes(j)], project_out.at[pl.ds(j * WIDTH, WIDTH), :], out_sem.at[0]
        )
        for j in range(4)
    ]
    for copy in project_copies:
        copy.start()

    @pl.loop(0, 4)
    def _(j):
        collect(X_FOUR_BACK + j)
        whole_back(X_FOUR_BACK + j, whole_crops, PRM4, 4 * j, 24 + 4 * j)
        for q in range(4):
            centred, _ = norm_terms(H1[j, :, lanes(q)], PRM4, 4 * j + q)
            DH1[:, lanes(4 * j + q)] = back_through(
                DA4[j, :, lanes(q)], centred, CW[...], PRM4, 4 * j + q
            ).astype(BF)

    @pl.loop(0, 4)
    def _(j):
        DP[j] = mm_t(DH1[...], WH[at(j * WIDTH, WIDTH), :]) * area_inv

    @pl.loop(0, 4)
    def _(j):
        rows = at(j * ROWS, ROWS)
        for q in range(4):
            high, low = two_parts(DP[j, :, lanes(q)])
            out_grad = mm(PT[...], high) + mm(PT[...], low)
            centred, before = norm_terms(C3[rows, lanes(q)], PRM3, 4 * j + q)
            joined = before + F[:, lanes(4 * j + q)].astype(F32)
            du = out_grad * gelu_slope(joined)
            DJ[rows, lanes(q)] = du
            MSG[X_THREE_BACK + j, q : q + 1, :] = jnp.sum(du, axis=0, keepdims=True)
            MSG[X_THREE_BACK + j, 4 + q : 5 + q, :] = jnp.sum(du * centred, axis=0, keepdims=True)
        announce(X_THREE_BACK + j)

    pltpu.make_async_copy(project_buf, project_buf, out_sem.at[0]).wait()

    def send_tile(slot, target, first):
        copy = pltpu.make_async_copy(OUTT.at[slot], target, out_sem.at[slot])
        if not isinstance(first, bool):

            @pl.when(jnp.logical_not(first))
            def _():
                copy.wait()
        elif not first:
            copy.wait()
        return copy

    @pl.loop(0, 16)
    def _(tile):
        slot = lax.rem(tile, 2)
        i = tile // 4
        j = lax.rem(tile, 4)
        target = hidden_out.at[at(i * WIDTH, WIDTH), lanes(j, WIDTH)]
        copy = send_tile(slot, target, tile < 2)
        OUTT[slot] = t_mm(PO[:, lanes(i, WIDTH)], DH1[:, lanes(j, WIDTH)])
        copy.start()

    @pl.loop(0, 4)
    def _(j):
        collect(X_THREE_BACK + j)
        whole_back(X_THREE_BACK + j, whole_rows, PRM3, 4 * j, 8 + 4 * j)
        rows = at(j * ROWS, ROWS)
        for q in range(4):
            centred, _ = norm_terms(C3[rows, lanes(q)], PRM3, 4 * j + q)
            COLS[:, lanes(4 * j + q)] = back_through(
                DJ[rows, lanes(q)], centred, RW[...], PRM3, 4 * j + q
            ).astype(BF)

    @pl.loop(0, 2)
    def _(h):
        DA[:, lanes(h, 256)] = mm_t(COLS[:, 0:DEPTH], WE[at(h * 256, 256), :])

    for q in range(4):
        centred, before = norm_terms(C2[:, lanes(q)], PRM2, q)
        du = DA[:, lanes(q)] * gelu_slope(before) * RW[...]
        DA[:, lanes(q)] = du
        MSG[X_TWO_BACK, q : q + 1, :] = jnp.sum(du, axis=0, keepdims=True)
        MSG[X_TWO_BACK, 4 + q : 5 + q, :] = jnp.sum(du * centred, axis=0, keepdims=True)
    announce(X_TWO_BACK)

    @pl.loop(0, 4)
    def _(j):
        slot = lax.rem(j, 2)
        copy = send_tile(slot, expand_out.at[:, lanes(j, WIDTH)], False)
        OUTT[slot] = t_mm(A2[...], COLS[:, lanes(j, WIDTH)])
        copy.start()

    collect(X_TWO_BACK)
    whole_back(X_TWO_BACK, whole_rows, PRM2, 0, 4)
    for q in range(4):
        centred, _ = norm_terms(C2[:, lanes(q)], PRM2, q)
        APAD[EDGE : EDGE + ROWS, lanes(q)] = back_through(
            DA[:, lanes(q)], centred, RW[...], PRM2, q
        )
    spread_taps(-1)

    @pl.loop(0, 2)
    def _(h):
        total = mm_t(COLS[:, 0:WIDTH], WS[at(h * 256, 256), :])
        for tap in range(1, 9):
            total += mm_t(
                COLS[:, tap * WIDTH : (tap + 1) * WIDTH], WS[at(tap * WIDTH + h * 256, 256), :]
            )
        DA[:, lanes(h, 256)] = total

    for q in range(4):
        centred, before = norm_terms(C1[:, lanes(q)], PRM1, q)
        du = DA[:, lanes(q)] * gelu_slope(before) * RW[...]
        DA[:, lanes(q)] = du
        MSG[X_ONE_BACK, q : q + 1, :] = jnp.sum(du, axis=0, keepdims=True)
        MSG[X_ONE_BACK, 4 + q : 5 + q, :] = jnp.sum(du * centred, axis=0, keepdims=True)
    announce(X_ONE_BACK)

    @pl.loop(0, 9)
    def _(tap):
        slot = lax.rem(tap, 2)
        copy = send_tile(slot, spatial_out.at[at(tap * WIDTH, WIDTH), :], False)
        OUTT[slot] = mm(A1T[...], COLS[:, lanes(tap, WIDTH)])
        copy.start()

    collect(X_ONE_BACK)
    whole_back(X_ONE_BACK, whole_rows, PRM1, 0, 0)
    collect(X_EXTRA)
    extra = jnp.sum(RECV[X_EXTRA], axis=0)
    FAR[0, 88:96, :] = extra
    far = pltpu.make_async_remote_copy(
        FAR.at[0],
        FAR.at[1],
        far_sem.at[0],
        far_sem.at[1],
        device_id=(1 - r, d),
        device_id_type=MESH,
    )
    far.start()
    for q in range(4):
        centred, _ = norm_terms(C1[:, lanes(q)], PRM1, q)
        A2[:, lanes(q)] = back_through(DA[:, lanes(q)], centred, RW[...], PRM1, q).astype(BF)

    @pl.loop(0, 4)
    def _(j):
        rows = at(j * ROWS, ROWS)
        grad = mm_t(A2[...], WR[at(j * WIDTH, WIDTH), :])
        for q in range(4):
            DJ[rows, lanes(q)] = (DJ[rows, lanes(q)] + grad[:, lanes(q)]) * RW[...]
        pltpu.make_async_copy(
            DJ.at[rows, :], feature_out.at[0, :, lanes(j, WIDTH)], out_sem.at[3]
        ).start()

    @pl.loop(0, 4)
    def _(j):
        slot = lax.rem(j + 1, 2)
        copy = send_tile(slot, reduce_out.at[at(j * WIDTH, WIDTH), :], False)
        OUTT[slot] = t_mm(F[:, lanes(j, WIDTH)], A2[...])
        copy.start()

    far.wait()
    both = jnp.where(big, FAR[0], FAR[1]) + jnp.where(big, FAR[1], FAR[0])
    gain_out[...] = both[0:40]
    shift_out[0:40, :] = both[48:88]
    shift_out[40:41, :] = both[88:89]
    loss_out[...] = jnp.broadcast_to(both[89:90], (8, LANES)) / float(GROUP * IMAGES)

    @pl.when(big)
    def _():
        forward_units.wait_send()

    proto_copy.wait()
    for slot in range(2):
        pltpu.make_async_copy(
            OUTT.at[slot], reduce_out.at[pl.ds(0, WIDTH), :], out_sem.at[slot]
        ).wait()
    pltpu.make_async_copy(feature_out.at[0], feature_out.at[0], out_sem.at[3]).wait()


def tower(
    features,
    crop_counts,
    crop_image,
    w_reduce,
    w_spatial,
    w_expand,
    w_hidden,
    w_project,
    prototypes,
    norm_gain,
    norm_shift,
):
    protos = jnp.pad(prototypes, ((0, 0), (0, PADDED - PROTOS)))
    anywhere = pl.BlockSpec(memory_space=pl.ANY)
    inside = pl.BlockSpec(memory_space=pltpu.VMEM)

    def vm(*shape, dtype=F32):
        return pltpu.VMEM(shape, dtype)

    dma = pltpu.SemaphoreType.DMA

    def shaped(*shape):
        return jax.ShapeDtypeStruct(shape, F32)

    return pl.pallas_call(
        tower_kernel,
        out_shape=(
            shaped(8, LANES),
            shaped(1, ROWS, DEPTH),
            shaped(DEPTH, WIDTH),
            shaped(9 * WIDTH, WIDTH),
            shaped(WIDTH, DEPTH),
            shaped(DEPTH, HIDDEN),
            shaped(HIDDEN, FEATS),
            shaped(FEATS, PADDED),
            shaped(40, LANES),
            shaped(41, LANES),
        ),
        in_specs=[anywhere, inside, inside] + [anywhere] * 6 + [inside, inside],
        out_specs=(inside,) + (anywhere,) * 7 + (inside, inside),
        scratch_shapes=[
            vm(ROWS, DEPTH, dtype=BF),
            vm(DEPTH, WIDTH, dtype=BF),
            vm(9 * WIDTH, WIDTH, dtype=BF),
            vm(WIDTH, DEPTH, dtype=BF),
            vm(DEPTH, HIDDEN, dtype=BF),
            vm(HIDDEN, FEATS, dtype=BF),
            vm(FEATS, PADDED, dtype=BF),
            vm(ROWS, WIDTH),
            vm(ROWS, WIDTH),
            vm(4 * ROWS, WIDTH),
            vm(4 * ROWS, WIDTH),
            vm(ROWS, WIDTH),
            vm(ROWS + 2 * EDGE, WIDTH),
            vm(ROWS, 9 * WIDTH, dtype=BF),
            vm(ROWS, WIDTH, dtype=BF),
            vm(WIDTH, ROWS, dtype=BF),
            vm(SLOTS, DEPTH, dtype=BF),
            vm(4, SLOTS, WIDTH),
            vm(SLOTS, HIDDEN, dtype=BF),
            vm(4, SLOTS, WIDTH),
            vm(SLOTS, HIDDEN, dtype=BF),
            vm(4, SLOTS, WIDTH),
            vm(SLOTS, PADDED),
            vm(SLOTS, PADDED),
            vm(SLOTS, PADDED, dtype=BF),
            vm(GROUP * IMAGES, PADDED),
            vm(2 * IMAGES, PADDED),
            vm(GROUP * IMAGES, LANES),
            vm(GROUP * IMAGES, LANES),
            vm(GROUP, 2 * IMAGES, FEATS),
            vm(2 * IMAGES, FEATS),
            vm(ROWS, LANES),
            vm(SLOTS, LANES),
            vm(ROWS, LANES),
            vm(ROWS, LANES),
            vm(ROWS, SLOTS, dtype=BF),
            vm(SLOTS, ROWS, dtype=BF),
            vm(4, 8, LANES),
            vm(4, 8, LANES),
            vm(16, 8, LANES),
            vm(16, 8, LANES),
            vm(EXCHANGES, 8, LANES),
            vm(EXCHANGES, GROUP, 8, LANES),
            vm(2, WIDTH, WIDTH),
            dma((7,)),
            dma((EXCHANGES,)),
            dma((EXCHANGES,)),
            dma((4,)),
            dma((4,)),
            dma((2,)),
            vm(2, 96, LANES),
        ],
        compiler_params=pltpu.CompilerParams(
            collective_id=0, has_side_effects=True, vmem_limit_bytes=62 << 20
        ),
    )(
        features,
        crop_image.reshape(1, SLOTS),
        crop_counts.reshape(1, IMAGES),
        w_reduce,
        w_spatial,
        w_expand,
        w_hidden,
        w_project,
        protos,
        norm_gain.reshape(40, LANES),
        norm_shift.reshape(41, LANES),
    )


def fused_body(*arrays):
    loss, feature_grad, reduce, spatial, expand, hidden, project, proto, gain, shift = tower(*arrays)

    def scattered(grad):
        return lax.psum_scatter(
            grad.reshape(-1), ("res", "dp"), scatter_dimension=0, tiled=True
        )

    return (
        loss[0, 0],
        feature_grad,
        scattered(reduce),
        scattered(spatial),
        scattered(expand),
        scattered(hidden),
        scattered(project),
        lax.psum(proto[:, :PROTOS].reshape(-1), ("res", "dp")),
        gain.reshape(-1),
        shift.reshape(-1),
    )


def solution(mesh):
    return jax.shard_map(
        fused_body if mesh.shape["dp"] == GROUP else body,
        mesh=mesh,
        in_specs=(P("res", "dp", None), P("dp"), P("dp"), P(), P(), P(), P(), P(), P(), P(), P()),
        out_specs=(
            P(),
            P("res", "dp", None),
            P(("res", "dp")),
            P(("res", "dp")),
            P(("res", "dp")),
            P(("res", "dp")),
            P(("res", "dp")),
            P(),
            P(),
            P(),
        ),
        check_vma=False,
    )
```

```python
import jax
import jax.numpy as jnp
from jax import lax
from jax.experimental import pallas as pl
from jax.experimental.pallas import tpu as pltpu
from jax.sharding import PartitionSpec as P

LSIDE = 7
SSIDE = 3
SINK = 3


HIGH = lax.Precision.HIGHEST
SOFTMAX_HEAT = 0.1
SHARPNESS = 0.05
EPS_NORM = 1e-05
EPS_UNIT = 1e-06


def combined_all(part, axis, combine):
    gathered = jax.tree.map(lambda a: lax.all_gather(a, axis), part)

    def take(source):
        return jax.tree.map(lambda a: lax.dynamic_index_in_dim(a, source, 0, False), gathered)

    return lax.fori_loop(
        1, lax.axis_size(axis), lambda source, state: combine(state, take(source)), take(0)
    )


def from_behind(value, axis, steps):
    count = lax.axis_size(axis)
    leading, last = (max(0, -steps), min(count, count - steps))
    return lax.ppermute(value, axis, [(source, source + steps) for source in range(leading, last)])


def row_contract(left, right):
    return lax.dot_general(
        left, right, (((0,), (0,)), ((), ())), preferred_element_type=jnp.float32
    )


def times_transposed(left, right):
    return lax.dot_general(
        left, right, (((1,), (1,)), ((), ())), preferred_element_type=jnp.float32
    )


def split_norms(vector, width, depth):
    return (
        vector[:width],
        vector[width : 2 * width],
        vector[2 * width : 2 * width + depth],
        vector[2 * width + depth :],
    )


def displaced(values, offset):
    if offset == 0:
        return values
    filler = jnp.zeros((abs(offset),) + values.shape[1:], values.dtype)
    if offset > 0:
        return jnp.concatenate([values[offset:], filler], axis=0)
    return jnp.concatenate([filler, values[:offset]], axis=0)


def tap_layout(row_count, big_crop):
    row_ids = jnp.arange(row_count)
    side_len = jnp.where(big_crop, LSIDE, SSIDE)
    pixel = row_ids % (side_len * side_len)
    line_ids = pixel // side_len
    column_ids = pixel % side_len
    layout = []
    for tap_y in (-1, 0, 1):
        for tap_x in (-1, 0, 1):
            inside = (
                (line_ids + tap_y >= 0)
                & (line_ids + tap_y < side_len)
                & (column_ids + tap_x >= 0)
                & (column_ids + tap_x < side_len)
            )
            layout.append((inside[:, None], tap_y * LSIDE + tap_x, tap_y * SSIDE + tap_x))
    return layout


def gather_taps(acts, layout, big_crop):
    pieces = []
    for inside, step_large, step_small in layout:
        moved_rows = jnp.where(big_crop, displaced(acts, step_large), displaced(acts, step_small))
        pieces.append(jnp.where(inside, moved_rows, jnp.zeros_like(moved_rows)))
    return jnp.concatenate(pieces, axis=1)


def scatter_taps(column_grad, layout, big_crop, channels):
    result = jnp.zeros((column_grad.shape[0], channels), jnp.float32)
    for tap_index, (inside, step_large, step_small) in enumerate(layout):
        piece = column_grad[:, tap_index * channels : (tap_index + 1) * channels]
        piece = jnp.where(inside, piece, jnp.zeros_like(piece))
        result = result + jnp.where(
            big_crop, displaced(piece, -step_large), displaced(piece, -step_small)
        )
    return result


def merge_moments(first_part, second_part):
    merged_count = first_part[0] + second_part[0]
    delta = second_part[1] - first_part[1]
    merged_mean = first_part[1] + delta * (second_part[0] / merged_count)
    merged_spread = (
        first_part[2]
        + second_part[2]
        + delta * delta * (first_part[0] * second_part[0] / merged_count)
    )
    return (merged_count, merged_mean, merged_spread)


def moments(values, weight):
    row_total = jnp.sum(weight)
    local_mean = jnp.sum(values * weight, axis=0) / row_total
    centred = values - local_mean
    local_spread = jnp.sum(weight * centred * centred, axis=0)
    whole_count, mean_vec, whole_spread = combined_all(
        (row_total, local_mean, local_spread), "dp", merge_moments
    )
    return (mean_vec, whole_spread / whole_count, whole_count)


def normalize(values, weight, gain_vec, shift_vec):
    mean_vec, var_vec, whole_count = moments(values, weight)
    scale_vec = lax.rsqrt(var_vec + EPS_NORM)
    centred = (values - mean_vec) * scale_vec
    return (centred * gain_vec + shift_vec, (centred, scale_vec, whole_count))


def normalize_back(upstream, weight, gain_vec, saved_stats):
    centred, scale_vec, whole_count = saved_stats
    upstream = upstream * weight
    local_first = jnp.sum(upstream, axis=0)
    local_second = jnp.sum(upstream * centred, axis=0)
    whole_first, whole_second = lax.psum((local_first, local_second), "dp")
    result = (
        gain_vec
        * scale_vec
        * (upstream - weight * (whole_first + centred * whole_second) / whole_count)
    )
    return (result, local_second, local_first)


def gelu_back(before, upstream):
    return jax.vjp(jax.nn.gelu, before)[1](upstream)[0]


def spread_rows(crop_grad, crop_total, area):
    depth = crop_grad.shape[1]
    widened = jnp.broadcast_to(crop_grad[:crop_total, None, :], (crop_total, area, depth))
    return widened.reshape(crop_total * area, depth) / area


def body(
    features,
    crop_counts,
    crop_image,
    w_reduce,
    w_spatial,
    w_expand,
    w_hidden,
    w_project,
    prototypes,
    norm_gain,
    norm_shift,
):
    inputs = features[0]
    row_count = inputs.shape[0]
    depth = w_reduce.shape[0]
    width = w_reduce.shape[1]
    hidden = w_hidden.shape[1]
    slot_count = crop_image.shape[0]
    image_count = crop_counts.shape[0]
    image_total = image_count * lax.axis_size("dp")
    big_crop = lax.axis_index("res") == 0
    first_image = lax.axis_index("dp") * image_count
    live_slot = (crop_image >= 0).astype(jnp.float32)
    slot_rows = SSIDE * SSIDE * slot_count
    live_rows = jnp.concatenate(
        [jnp.repeat(live_slot, SSIDE * SSIDE), jnp.zeros((row_count - slot_rows,), jnp.float32)]
    )
    row_weight = jnp.where(big_crop, jnp.ones_like(live_rows), live_rows)[:, None]
    large_crops = (jnp.arange(slot_count) < 2 * image_count).astype(jnp.float32)
    crop_weight = jnp.where(big_crop, large_crops, live_slot)[:, None]
    gain_one, gain_two, gain_three, gain_four = split_norms(norm_gain, width, depth)
    shift_one, shift_two, shift_three, shift_rest = split_norms(norm_shift, width, depth)
    shift_four = shift_rest[:hidden]
    head_bias = shift_rest[hidden:]
    layout = tap_layout(row_count, big_crop)
    conv_one = jnp.dot(inputs, w_reduce, preferred_element_type=jnp.float32)
    norm_one, saved_one = normalize(conv_one, row_weight, gain_one, shift_one)
    act_one = jax.nn.gelu(norm_one).astype(jnp.bfloat16)
    columns = gather_taps(act_one, layout, big_crop)
    conv_two = jnp.dot(columns, w_spatial, preferred_element_type=jnp.float32)
    norm_two, saved_two = normalize(conv_two, row_weight, gain_two, shift_two)
    act_two = jax.nn.gelu(norm_two).astype(jnp.bfloat16)
    conv_three = jnp.dot(act_two, w_expand, preferred_element_type=jnp.float32)
    norm_three, saved_three = normalize(conv_three, row_weight, gain_three, shift_three)
    joined = norm_three + inputs.astype(jnp.float32)
    block_out = jax.nn.gelu(joined)
    large_pool = jnp.mean(block_out.reshape(2 * image_count, LSIDE * LSIDE, depth), axis=1)
    large_pool = jnp.concatenate(
        [large_pool, jnp.zeros((slot_count - 2 * image_count, depth), jnp.float32)], axis=0
    )
    small_pool = jnp.mean(block_out[:slot_rows].reshape(slot_count, SSIDE * SSIDE, depth), axis=1)
    pooled = jnp.where(big_crop, large_pool, small_pool).astype(jnp.bfloat16)
    head_one = jnp.dot(pooled, w_hidden, preferred_element_type=jnp.float32)
    norm_four, saved_four = normalize(head_one, crop_weight, gain_four, shift_four)
    act_four = jax.nn.gelu(norm_four).astype(jnp.bfloat16)
    head_two = jnp.dot(act_four, w_project, preferred_element_type=jnp.float32) + head_bias
    unit, unit_back = jax.vjp(
        lambda vec: vec * lax.rsqrt(jnp.sum(vec * vec, axis=1, keepdims=True) + EPS_UNIT), head_two
    )
    unit_low = unit.astype(jnp.bfloat16)
    scores = jnp.dot(unit_low, prototypes, preferred_element_type=jnp.float32)
    table = jnp.exp(scores[: 2 * image_count].reshape(2, image_count, -1) / SHARPNESS)
    for sweep in range(SINK):
        column_total = lax.psum(jnp.sum(table, axis=1), "dp")
        table = table / column_total[:, None, :]
        table = table / jnp.sum(table, axis=2, keepdims=True)
    own_codes = table
    far_codes = from_behind(own_codes, "res", 1)
    weight_image = 1.0 / (2.0 * (1.0 + crop_counts.astype(jnp.float32)))
    onehot = ((crop_image - first_image)[:, None] == jnp.arange(image_count)[None, :]).astype(
        jnp.float32
    )
    slot_scale = jnp.dot(onehot, weight_image, precision=HIGH) * live_slot
    small_targets = jnp.dot(onehot, far_codes[0] + far_codes[1], precision=HIGH)

    def partial_loss(scores_by_row):
        log_probability = jax.nn.log_softmax(scores_by_row / SOFTMAX_HEAT, axis=-1)
        view_zero = log_probability[:image_count]
        view_one = log_probability[image_count : 2 * image_count]
        large_share = -jnp.sum(
            weight_image
            * (
                jnp.sum(own_codes[0] * view_one, axis=-1)
                + jnp.sum(own_codes[1] * view_zero, axis=-1)
            )
        )
        small_share = -jnp.sum(slot_scale * jnp.sum(small_targets * log_probability, axis=-1))
        return jnp.where(big_crop, large_share, small_share)

    local_total, total_back = jax.vjp(partial_loss, scores)
    whole_total = lax.psum(local_total, ("res", "dp"))
    loss = whole_total / image_total
    score_grad = total_back(jnp.ones_like(local_total))[0].astype(jnp.bfloat16)
    proto_grad = row_contract(unit_low, score_grad)
    unit_grad = times_transposed(score_grad, prototypes)
    head_two_grad = unit_back(unit_grad)[0]
    bias_grad = jnp.sum(head_two_grad, axis=0)
    head_two_low = head_two_grad.astype(jnp.bfloat16)
    project_grad = row_contract(act_four, head_two_low)
    act_four_grad = times_transposed(head_two_low, w_project)
    head_one_grad, gain_four_grad, shift_four_grad = normalize_back(
        gelu_back(norm_four, act_four_grad), crop_weight, gain_four, saved_four
    )
    head_one_low = head_one_grad.astype(jnp.bfloat16)
    hidden_grad = row_contract(pooled, head_one_low)
    pooled_grad = times_transposed(head_one_low, w_hidden)
    large_spread = spread_rows(pooled_grad, 2 * image_count, LSIDE * LSIDE)
    small_spread = jnp.concatenate(
        [
            spread_rows(pooled_grad, slot_count, SSIDE * SSIDE),
            jnp.zeros((row_count - slot_rows, depth), jnp.float32),
        ],
        axis=0,
    )
    out_grad = jnp.where(big_crop, large_spread, small_spread)
    joined_grad = gelu_back(joined, out_grad)
    three_grad, gain_three_grad, shift_three_grad = normalize_back(
        joined_grad, row_weight, gain_three, saved_three
    )
    three_low = three_grad.astype(jnp.bfloat16)
    expand_grad = row_contract(act_two, three_low)
    act_two_grad = times_transposed(three_low, w_expand)
    two_grad, gain_two_grad, shift_two_grad = normalize_back(
        gelu_back(norm_two, act_two_grad), row_weight, gain_two, saved_two
    )
    two_low = two_grad.astype(jnp.bfloat16)
    spatial_grad = row_contract(columns, two_low)
    column_grad = times_transposed(two_low, w_spatial)
    act_one_grad = scatter_taps(column_grad, layout, big_crop, width)
    one_grad, gain_one_grad, shift_one_grad = normalize_back(
        gelu_back(norm_one, act_one_grad), row_weight, gain_one, saved_one
    )
    one_low = one_grad.astype(jnp.bfloat16)
    reduce_grad = row_contract(inputs, one_low)
    input_grad = (joined_grad + times_transposed(one_low, w_reduce)) * row_weight
    weight_terms = (
        reduce_grad.reshape(-1),
        spatial_grad.reshape(-1),
        expand_grad.reshape(-1),
        hidden_grad.reshape(-1),
        project_grad.reshape(-1),
    )
    summed = (
        lax.psum_scatter(weight_terms[0], ("res", "dp"), scatter_dimension=0, tiled=True),
        lax.psum_scatter(weight_terms[1], ("res", "dp"), scatter_dimension=0, tiled=True),
        lax.psum_scatter(weight_terms[2], ("res", "dp"), scatter_dimension=0, tiled=True),
        lax.psum_scatter(weight_terms[3], ("res", "dp"), scatter_dimension=0, tiled=True),
        lax.psum_scatter(weight_terms[4], ("res", "dp"), scatter_dimension=0, tiled=True),
    )
    gain_local = jnp.concatenate([gain_one_grad, gain_two_grad, gain_three_grad, gain_four_grad])
    shift_local = jnp.concatenate(
        [shift_one_grad, shift_two_grad, shift_three_grad, shift_four_grad, bias_grad]
    )
    gain_total, shift_total, proto_total = lax.psum(
        (gain_local, shift_local, proto_grad.reshape(-1)), ("res", "dp")
    )
    return (
        loss,
        input_grad[None],
        summed[0],
        summed[1],
        summed[2],
        summed[3],
        summed[4],
        proto_total,
        gain_total,
        shift_total,
    )


MESH = pl.DeviceIdType.MESH
BF = jnp.bfloat16
F32 = jnp.float32
GROUP = 16
ROWS = 784
WIDTH = 512
DEPTH = 2048
HIDDEN = 2048
FEATS = 128
SLOTS = 64
IMAGES = 8
PROTOS = 3000
PADDED = 3072
LANES = 128
EDGE = 16
STRIPE = 112
TANH_IN = 0.7978845608
TANH_CUBE = 0.044715

X_COUNT, X_ONE, X_TWO, X_THREE, X_FOUR = 0, 1, 2, 3, 7
X_FOUR_BACK, X_EXTRA, X_THREE_BACK, X_TWO_BACK, X_ONE_BACK, EXCHANGES = 11, 15, 16, 20, 21, 22
SPATIAL_HALF = 2304
PROTO_HALF = 1536


def mm(left, right):
    return jnp.dot(left, right, preferred_element_type=F32)


def mm_t(left, right):
    return lax.dot_general(left, right, (((1,), (1,)), ((), ())), preferred_element_type=F32)


def t_mm(left, right):
    return lax.dot_general(left, right, (((0,), (0,)), ((), ())), preferred_element_type=F32)


def gelu(v):
    return 0.5 * v * (1.0 + jnp.tanh(TANH_IN * (v + TANH_CUBE * (v * v * v))))


def gelu_slope(v):
    square = v * v
    t = jnp.tanh(TANH_IN * (v + TANH_CUBE * (v * square)))
    return 0.5 * (1.0 + t) + 0.5 * v * (1.0 - t * t) * (
        TANH_IN * (1.0 + (3.0 * TANH_CUBE) * square)
    )


def two_parts(v):
    high = v.astype(BF)
    return high, (v - high.astype(F32)).astype(BF)


def at(start, size):
    return pl.ds(pl.multiple_of(start, size if size % 8 == 0 else 8), size)


def lanes(index, width=LANES):
    if isinstance(index, int):
        return slice(index * width, (index + 1) * width)
    return pl.ds(pl.multiple_of(index * width, width), width)


def tower_kernel(
    feat,
    crop_row,
    count_row,
    w_reduce,
    w_spatial,
    w_expand,
    w_hidden,
    w_project,
    protos,
    gain,
    shift,
    loss_out,
    feature_out,
    reduce_out,
    spatial_out,
    expand_out,
    hidden_out,
    project_out,
    proto_out,
    gain_out,
    shift_out,
    PG,
    RB_S,
    RB_R,
    RB_E,
    RB_P,
    F,
    WR,
    WS,
    WE,
    WHB,
    WHC,
    WP,
    PR,
    C1,
    C2,
    C3,
    DJ,
    APAD,
    COLS,
    A2,
    A1T,
    PO,
    H1,
    A4,
    DA4,
    DH1,
    DS,
    UL,
    POF,
    D2F,
    D2A,
    TAB,
    Q,
    RACC,
    RINV,
    UNITS,
    UOWN,
    RW,
    CW,
    LINE,
    COL,
    PT,
    P,
    PRM1,
    PRM2,
    PRM3,
    PRM4,
    MSG,
    RECV,
    FAR,
    OUT,
    RC_E,
    RC_P,
    OUT_P,
    STG,
    STGE,
    HACC,
    HREC,
    HAL,
    PACC,
    PREC,
    PIN,
    load_sem,
    send_sem,
    recv_sem,
    unit_sem,
    out_sem,
    far_sem,
    wh_sem,
    rs_send,
    rs_recv,
    stage_sem,
    gather_send,
    gather_recv,
    core_send,
    core_recv,
    row_sem,
    free_sem,
):
    r = lax.axis_index("res")
    d = lax.axis_index("dp")
    big = r == 0
    area = jnp.where(big, LSIDE * LSIDE, SSIDE * SSIDE)
    area_f = area.astype(F32)
    side_f = jnp.where(big, float(LSIDE), float(SSIDE))
    area_inv = jnp.where(big, 1.0 / (LSIDE * LSIDE), 1.0 / (SSIDE * SSIDE))
    side_inv = jnp.where(big, 1.0 / LSIDE, 1.0 / SSIDE)

    loads = [
        pltpu.make_async_copy(source, target, load_sem.at[index])
        for index, (source, target) in enumerate(
            [
                (feat.at[0], F),
                (w_reduce, WR),
                (w_spatial, WS),
                (w_expand, WE),
                (w_hidden.at[:, pl.ds(pl.multiple_of(d * LANES, LANES), LANES)], WHC),
                (w_project, WP),
                (protos, PR),
            ]
        )
    ]
    for load in loads:
        load.start()

    def hidden_load(k, slot):
        return pltpu.make_async_copy(
            w_hidden.at[:, lanes(k, 256)], WHB.at[slot], wh_sem.at[slot]
        )

    for k in range(2):
        hidden_load(k, k).start()

    barrier = pltpu.get_barrier_semaphore()

    @pl.loop(1, GROUP)
    def _(k):
        pl.semaphore_signal(
            barrier, inc=1, device_id=(r, lax.rem(d + k, GROUP)), device_id_type=MESH
        )

    pl.semaphore_signal(barrier, inc=1, device_id=(1 - r, d), device_id_type=MESH)

    slot_of = lax.broadcasted_iota(jnp.int32, (ROWS, SLOTS), 1)
    row_of = lax.broadcasted_iota(jnp.int32, (ROWS, SLOTS), 0)
    inside = ((row_of >= slot_of * area) & (row_of < slot_of * area + area)).astype(F32)
    lane_ids = lax.broadcasted_iota(jnp.int32, (1, SLOTS), 1)
    crop_ids = crop_row[...]
    live = jnp.where(big, (lane_ids < 2 * IMAGES).astype(F32), (crop_ids >= 0).astype(F32))
    RW[...] = jnp.broadcast_to(jnp.sum(inside * live, axis=1, keepdims=True), (ROWS, LANES))
    PT[...] = inside.astype(BF)
    slot_row = lax.broadcasted_iota(jnp.int32, (SLOTS, ROWS), 0)
    pixel_lane = lax.broadcasted_iota(jnp.int32, (SLOTS, ROWS), 1)
    P[...] = (
        ((pixel_lane >= slot_row * area) & (pixel_lane < slot_row * area + area))
        .astype(F32)
        .astype(BF)
    )
    square_row = lax.broadcasted_iota(jnp.int32, (SLOTS, SLOTS), 0)
    square_lane = lax.broadcasted_iota(jnp.int32, (SLOTS, SLOTS), 1)
    eye = (square_row == square_lane).astype(F32)
    CW[...] = jnp.broadcast_to(jnp.sum(eye * live, axis=1, keepdims=True), (SLOTS, LANES))
    live_total = jnp.sum(live, axis=1, keepdims=True)
    own_crops = jnp.broadcast_to(live_total, (1, LANES))
    own_rows = own_crops * area_f
    row_f = lax.broadcasted_iota(jnp.int32, (ROWS, LANES), 0).astype(F32)
    pixel = row_f - jnp.floor((row_f + 0.5) * area_inv) * area_f
    line = jnp.floor((pixel + 0.5) * side_inv)
    LINE[...] = line
    COL[...] = pixel - line * side_f
    APAD[0:EDGE, :] = jnp.zeros((EDGE, WIDTH), F32)
    APAD[EDGE + ROWS :, :] = jnp.zeros((EDGE, WIDTH), F32)
    for prm, base, blocks in ((PRM1, 0, 4), (PRM2, 4, 4), (PRM3, 8, 16), (PRM4, 24, 16)):
        for q in range(blocks):
            prm[q, 2:3, :] = gain[base + q : base + q + 1, :]
            prm[q, 3:4, :] = shift[base + q : base + q + 1, :]
    MSG[X_COUNT] = jnp.broadcast_to(own_rows, (8, LANES))

    pl.semaphore_wait(barrier, GROUP)

    def announce(x):
        @pl.loop(1, GROUP)
        def _(k):
            pltpu.make_async_remote_copy(
                MSG.at[x],
                RECV.at[x, d],
                send_sem.at[x],
                recv_sem.at[x],
                device_id=(r, lax.rem(d + k, GROUP)),
                device_id_type=MESH,
            ).start()

        RECV[x, d] = MSG[x]

    def collect(x):
        others = RECV.at[x, pl.ds(0, GROUP - 1)]
        pltpu.make_async_copy(others, others, recv_sem.at[x]).wait()
        pltpu.make_async_copy(others, others, send_sem.at[x]).wait()

    announce(X_COUNT)

    place = {1: lax.rem(d, 2), 2: lax.rem(d // 2, 2), 4: lax.rem(d // 4, 2), 8: d // 8}

    def partner(bit):
        return (r, d + bit * (1 - 2 * place[bit]))

    def block_of(order, stage, j, flip):
        index = 0
        for t, bit in enumerate(order):
            if t < stage:
                index = index + bit * place[bit]
            elif t == stage:
                index = index + bit * ((1 - place[bit]) if flip else place[bit])
            else:
                index = index + bit * ((j >> (t - stage - 1)) & 1)
        return index

    class Strip:
        def __init__(self, own, base, depth, columns, landing, staging, order, number):
            self.own, self.base, self.depth, self.columns = own, base, depth, columns
            self.landing, self.staging, self.order, self.number = landing, staging, order, number

        def block(self, index):
            start = pl.multiple_of(self.base + index * self.depth, 16)
            return self.own.at[pl.ds(start, self.depth), self.columns]

        def rows(self, stage):
            first = 16 - (16 >> stage)
            return first * self.depth, (8 >> stage) * self.depth

        def start(self, stage):
            first, _ = self.rows(stage)
            for j in range(8 >> stage):
                pltpu.make_async_remote_copy(
                    self.block(block_of(self.order, stage, j, True)),
                    self.landing.at[pl.ds(first + j * self.depth, self.depth), :],
                    rs_send.at[self.number, stage],
                    rs_recv.at[self.number, stage],
                    device_id=partner(self.order[stage]),
                    device_id_type=MESH,
                ).start()

        def landed(self, stage):
            first, size = self.rows(stage)
            return self.landing.at[pl.ds(first, size), :]

        def fetch(self, stage, slot):
            area = self.landed(stage)
            pltpu.make_async_copy(area, area, rs_recv.at[self.number, stage]).wait()
            _, size = self.rows(stage)
            copy = pltpu.make_async_copy(
                area, self.staging.at[slot, pl.ds(0, size), :], stage_sem.at[slot]
            )
            copy.start()
            return copy

        def fold(self, stage, slot):
            for j in range(8 >> stage):
                target = self.block(block_of(self.order, stage, j, False))
                target[...] += self.staging[slot, j * self.depth : (j + 1) * self.depth, :]

        def close(self):
            for stage in range(4):
                area = self.landed(stage)
                pltpu.make_async_copy(area, area, rs_send.at[self.number, stage]).wait()

    def advance(steps):
        copies = [steps[0][0].fetch(steps[0][1], 0)]
        for k, (strip, stage) in enumerate(steps):
            if k + 1 < len(steps):
                copies.append(steps[k + 1][0].fetch(steps[k + 1][1], (k + 1) % 2))
            copies[k].wait()
            strip.fold(stage, k % 2)
            if stage < 3:
                strip.start(stage + 1)

    order_a, order_b, order_c = (1, 2, 4, 8), (2, 1, 4, 8), (4, 1, 2, 8)
    orders = (order_a, order_b, order_b, order_c)
    spatial_strips = [
        Strip(C3, 0, 144, lanes(q), RB_S.at[q], STG, orders[q], q) for q in range(4)
    ]
    reduce_strips = [
        Strip(C3, SPATIAL_HALF, 64, lanes(q), RB_R.at[q], STG, orders[q], 4 + q) for q in range(4)
    ]
    expand_strips = [
        Strip(RC_E, 256 * q, 16, slice(0, WIDTH), RB_E.at[q], STGE, orders[q], 8 + q)
        for q in range(4)
    ]
    proto_strip = Strip(RC_P, 0, 96, slice(0, LANES), RB_P, STG, order_c, 12)

    def gathered_block(order, stage, j):
        index = 0
        for t, bit in enumerate(order):
            if t < stage:
                index = index + bit * ((j >> t) & 1)
            else:
                index = index + bit * place[bit]
        return index

    def gather_start(ref, base, depth, columns, order, stage, number):
        for j in range(1 << stage):
            start = pl.multiple_of(base + gathered_block(order, stage, j) * depth, 16)
            area = ref.at[pl.ds(start, depth), columns]
            pltpu.make_async_remote_copy(
                area,
                area,
                gather_send.at[number, stage],
                gather_recv.at[number, stage],
                device_id=partner(order[stage]),
                device_id_type=MESH,
            ).start()

    def gather_wait(ref, depth, columns, stage, number, sems):
        area = ref.at[pl.ds(0, depth << stage), columns]
        pltpu.make_async_copy(area, area, sems.at[number, stage]).wait()

    pooled_parts = (
        (slice(0, 640), (8, 4, 2, 1)),
        (slice(640, 1536), (8, 4, 1, 2)),
        (slice(1536, 2048), (8, 2, 1, 4)),
    )

    def by_size(action):
        @pl.when(big)
        def _():
            action(2 * IMAGES)

        @pl.when(jnp.logical_not(big))
        def _():
            action(SLOTS)

    def pooled_gather(stage):
        def action(depth):
            for number, (columns, order) in enumerate(pooled_parts):
                gather_start(PG, 0, depth, columns, order, stage, number)

        by_size(action)

    def pooled_arrived(stage):
        def action(depth):
            for number, (columns, order) in enumerate(pooled_parts):
                gather_wait(PG, depth, columns, stage, number, gather_recv)

        by_size(action)

    def core_copy(source, target, sent, landed):
        return pltpu.make_async_remote_copy(
            source,
            target,
            core_send.at[sent],
            core_recv.at[landed],
            device_id=(1 - r, d),
            device_id_type=MESH,
        )

    def half_tile(index):
        return pl.ds(pl.multiple_of(index * 256, 256), 256)

    def local_moments(values, rows, first_lane, weight, own, x):
        for q in range(4):
            v = values[rows, first_lane + q * LANES : first_lane + (q + 1) * LANES]
            w = weight[...]
            total = jnp.sum(v * w, axis=0, keepdims=True)
            centred = (v - total / own) * w
            MSG[x, q : q + 1, :] = total
            MSG[x, 4 + q : 5 + q, :] = jnp.sum(centred * centred, axis=0, keepdims=True)

    def whole_moments(x, counts, prm, first):
        whole = jnp.sum(counts, axis=0, keepdims=True)
        each = counts[:, None, :]
        sums = RECV[x, :, 0:4, :]
        spreads = RECV[x, :, 4:8, :]
        mean = jnp.sum(sums, axis=0) / whole
        off = sums / each - mean[None]
        var = jnp.sum(spreads + each * off * off, axis=0) / whole
        scale = lax.rsqrt(var + EPS_NORM)
        for q in range(4):
            prm[first + q, 0:1, :] = mean[q : q + 1]
            prm[first + q, 1:2, :] = scale[q : q + 1]

    def whole_back(x, whole, prm, first, place):
        ones = jnp.sum(RECV[x, :, 0:4, :], axis=0)
        twos = jnp.sum(RECV[x, :, 4:8, :], axis=0)
        for q in range(4):
            prm[first + q, 4:5, :] = ones[q : q + 1] / whole
            prm[first + q, 5:6, :] = twos[q : q + 1] / whole
        FAR[0, pl.ds(place, 4), :] = twos
        FAR[0, pl.ds(48 + place, 4), :] = ones

    def norm_terms(v, prm, index):
        centred = (v - prm[index, 0:1, :]) * prm[index, 1:2, :]
        return centred, centred * prm[index, 2:3, :] + prm[index, 3:4, :]

    def back_through(du, centred, weight, prm, index):
        inner = du - weight * (prm[index, 4:5, :] + centred * prm[index, 5:6, :])
        return prm[index, 2:3, :] * prm[index, 1:2, :] * inner

    def spread_taps(sign):
        def for_side(side):
            @pl.loop(0, ROWS // STRIPE)
            def _(s):
                base = pl.multiple_of(s * STRIPE, STRIPE)
                rows = pl.ds(base, STRIPE)
                window = pl.ds(base, STRIPE + 2 * EDGE)
                for tap in range(9):
                    dy, dx = sign * (tap // 3 - 1), sign * (tap % 3 - 1)
                    y = LINE[rows, :] + float(dy)
                    x = COL[rows, :] + float(dx)
                    keep = (y >= 0.0) & (y < float(side)) & (x >= 0.0) & (x < float(side))
                    start = EDGE + dy * side + dx
                    for q in range(4):
                        moved = APAD[window, lanes(q)][start : start + STRIPE]
                        COLS[rows, tap * WIDTH + q * LANES : tap * WIDTH + (q + 1) * LANES] = (
                            jnp.where(keep, moved, 0.0).astype(BF)
                        )

        @pl.when(big)
        def _():
            for_side(LSIDE)

        @pl.when(jnp.logical_not(big))
        def _():
            for_side(SSIDE)

    loads[0].wait()
    loads[1].wait()
    C1[...] = mm(F[...], WR[...])
    every = pl.ds(0, ROWS)
    local_moments(C1, every, 0, RW, own_rows, X_ONE)
    announce(X_ONE)
    collect(X_COUNT)
    row_counts = RECV[X_COUNT, :, 0, :]
    crop_counts = row_counts * area_inv
    whole_rows = jnp.sum(row_counts, axis=0, keepdims=True)
    whole_crops = jnp.sum(crop_counts, axis=0, keepdims=True)
    collect(X_ONE)
    whole_moments(X_ONE, row_counts, PRM1, 0)
    for q in range(4):
        _, before = norm_terms(C1[:, lanes(q)], PRM1, q)
        act = gelu(before)
        APAD[EDGE : EDGE + ROWS, lanes(q)] = act
        A1T[lanes(q), :] = act.astype(BF).T
    spread_taps(1)
    loads[2].wait()

    @pl.loop(0, 2)
    def _(h):
        C2[:, lanes(h, 256)] = mm(COLS[...], WS[:, lanes(h, 256)])

    local_moments(C2, every, 0, RW, own_rows, X_TWO)
    announce(X_TWO)
    collect(X_TWO)
    whole_moments(X_TWO, row_counts, PRM2, 0)
    for q in range(4):
        _, before = norm_terms(C2[:, lanes(q)], PRM2, q)
        A2[:, lanes(q)] = gelu(before).astype(BF)
    loads[3].wait()

    @pl.loop(0, 4)
    def _(j):
        rows = at(j * ROWS, ROWS)
        C3[rows, :] = mm(A2[...], WE[:, lanes(j, WIDTH)])
        local_moments(C3, rows, 0, RW, own_rows, X_THREE + j)
        announce(X_THREE + j)

    @pl.loop(0, 4)
    def _(j):
        collect(X_THREE + j)
        whole_moments(X_THREE + j, row_counts, PRM3, 4 * j)
        rows = at(j * ROWS, ROWS)
        for q in range(4):
            _, before = norm_terms(C3[rows, lanes(q)], PRM3, 4 * j + q)
            joined = before + F[:, lanes(4 * j + q)].astype(F32)
            high, low = two_parts(gelu(joined))
            pooled = (mm(P[...], high) + mm(P[...], low)) * area_inv
            pooled_low = pooled.astype(BF)
            PO[:, lanes(4 * j + q)] = pooled_low
            POF[:, lanes(4 * j + q)] = pooled_low.astype(F32) * CW[...]

    def keep_pooled(depth):
        copy = pltpu.make_async_copy(
            POF.at[pl.ds(0, depth), :],
            PG.at[pl.ds(pl.multiple_of(d * depth, 16), depth), :],
            row_sem.at[0],
        )
        copy.start()
        copy.wait()

    by_size(keep_pooled)
    pooled_gather(0)

    @pl.loop(0, 4)
    def _(j):
        for half in range(2):
            k = 2 * j + half
            hidden_load(k, half).wait()
            H1[j, :, half * 256 : half * 256 + 256] = mm(PO[...], WHB[half])
            hidden_load(lax.rem(k + 2, 8), half).start()
        local_moments(H1.at[j], pl.ds(0, SLOTS), 0, CW, own_crops, X_FOUR + j)
        announce(X_FOUR + j)

    @pl.loop(0, 4)
    def _(j):
        collect(X_FOUR + j)
        whole_moments(X_FOUR + j, crop_counts, PRM4, 4 * j)
        for q in range(4):
            _, before = norm_terms(H1[j, :, lanes(q)], PRM4, 4 * j + q)
            A4[:, lanes(4 * j + q)] = gelu(before).astype(BF)

    pooled_arrived(0)
    pooled_gather(1)
    loads[5].wait()
    loads[6].wait()
    head_two = mm(A4[...], WP[...]) + shift[40:41, :]
    length_inv = lax.rsqrt(jnp.sum(head_two * head_two, axis=1, keepdims=True) + EPS_UNIT)
    unit = head_two * length_inv
    unit_low = unit.astype(BF)
    UOWN[...] = unit_low[0 : 2 * IMAGES].astype(F32)
    UL[...] = unit_low

    def unit_copy(k):
        return pltpu.make_async_remote_copy(
            UOWN,
            UNITS.at[d],
            unit_sem.at[0],
            unit_sem.at[1],
            device_id=(r, lax.rem(d + k, GROUP)),
            device_id_type=MESH,
        )

    forward_units = pltpu.make_async_remote_copy(
        UNITS, UNITS, unit_sem.at[2], unit_sem.at[3], device_id=(1 - r, d), device_id_type=MESH
    )

    @pl.when(big)
    def _():
        @pl.loop(1, GROUP)
        def _(k):
            unit_copy(k).start()

        UNITS[d] = UOWN[...]

    @pl.when(big)
    def _():
        others = UNITS.at[pl.ds(0, GROUP - 1)]
        pltpu.make_async_copy(others, others, unit_sem.at[1]).wait()
        pltpu.make_async_copy(others, others, unit_sem.at[0]).wait()
        forward_units.start()

    @pl.when(jnp.logical_not(big))
    def _():
        forward_units.wait_recv()

    pooled_arrived(1)
    pooled_gather(2)

    chunk = 512
    chunks = PADDED // chunk
    images = GROUP * IMAGES
    chunk_lane = lax.broadcasted_iota(jnp.int32, (1, chunk), 1)

    @pl.loop(0, 2)
    def _(v):
        view = UNITS[:, pl.ds(pl.multiple_of(v * IMAGES, IMAGES), IMAGES), :]
        view = view.reshape(images, FEATS).astype(BF)

        def sweep(first):
            RACC[...] = jnp.zeros_like(RACC)

            @pl.loop(0, chunks)
            def _(c):
                columns = lanes(c, chunk)
                valid = (chunk_lane + c * chunk) < PROTOS
                if first:
                    raised = jnp.exp(mm(view, PR[:, columns]) / SHARPNESS)
                for q in range(chunk // LANES):
                    tile = pl.ds(pl.multiple_of(c * chunk + q * LANES, LANES), images)
                    if first:
                        table = raised[:, lanes(q)]
                    else:
                        table = TAB[tile, :] * RINV[...]
                    total = jnp.sum(table, axis=0, keepdims=True)
                    table = table * jnp.where(valid[:, lanes(q)], 1.0 / total, 0.0)
                    TAB[tile, :] = table
                    RACC[...] += table

            RINV[...] = jnp.broadcast_to(
                1.0 / jnp.sum(RACC[...], axis=1, keepdims=True), (images, LANES)
            )

        for number in range(SINK):
            sweep(number == 0)
        row_inv = RINV[pl.ds(pl.multiple_of(d * IMAGES, IMAGES), IMAGES), :]
        for c in range(PADDED // LANES):
            own = pl.ds(pl.multiple_of(c * LANES + d * IMAGES, IMAGES), IMAGES)
            Q[pl.ds(pl.multiple_of(v * IMAGES, IMAGES), IMAGES), lanes(c)] = TAB[own, :] * row_inv

    ident_f = jnp.sum(eye * crop_ids.astype(F32), axis=1, keepdims=True)
    pick_lane = lax.broadcasted_iota(jnp.int32, (SLOTS, 2 * IMAGES), 1)
    pick_row = lax.broadcasted_iota(jnp.int32, (SLOTS, 2 * IMAGES), 0)
    image_lane = jnp.where(pick_lane < IMAGES, pick_lane, pick_lane - IMAGES)
    first_image = (d * IMAGES).astype(F32)
    crossed = (pick_row < 2 * IMAGES) & (jnp.abs(pick_row - pick_lane) == IMAGES)
    matched = ident_f == image_lane.astype(F32) + first_image
    picked = jnp.where(big, crossed.astype(F32), matched.astype(F32))
    image_weight = 1.0 / (2.0 * (1.0 + count_row[...].astype(F32)))
    picked = picked * jnp.concatenate([image_weight, image_weight], axis=1)
    valid_all = lax.broadcasted_iota(jnp.int32, (1, PADDED), 1) < PROTOS
    loss_rows = []
    for s in range(4):
        rows = slice(16 * s, 16 * s + 16)
        target = jnp.dot(picked[rows], Q[...], precision=HIGH, preferred_element_type=F32)
        logit = jnp.where(valid_all, mm(UL[rows, :], PR[...]) / SOFTMAX_HEAT, -1e30)
        shifted = logit - jnp.max(logit, axis=1, keepdims=True)
        raised = jnp.exp(shifted)
        total = jnp.sum(raised, axis=1, keepdims=True)
        loss_rows.append(jnp.sum(target * (shifted - jnp.log(total)), axis=1, keepdims=True))
        mass = jnp.sum(target, axis=1, keepdims=True)
        DS[rows, :] = ((raised * (mass / total) - target) / SOFTMAX_HEAT).astype(BF)
    loss_local = -jnp.sum(
        loss_rows[0] + loss_rows[1] + loss_rows[2] + loss_rows[3], axis=0, keepdims=True
    )

    def proto_half(which):
        return t_mm(DS[:, pl.ds(pl.multiple_of(which * PROTO_HALF, LANES), PROTO_HALF)], UL[...])

    OUT_P[...] = proto_half(1 - r)
    proto_swap = core_copy(OUT_P, RC_P, 4, 17)
    proto_swap.start()
    unit_grad = mm_t(DS[...], PR[...])
    along = jnp.sum(unit * unit_grad, axis=1, keepdims=True)
    head_two_grad = (unit_grad - unit * along) * length_inv
    bias_grad = jnp.sum(head_two_grad, axis=0, keepdims=True)
    MSG[X_EXTRA] = jnp.concatenate(
        [bias_grad, jnp.broadcast_to(loss_local, (1, LANES)), jnp.zeros((6, LANES), F32)], axis=0
    )
    announce(X_EXTRA)
    head_two_low = head_two_grad.astype(BF)

    @pl.loop(0, 4)
    def _(j):
        DA4[j] = mm_t(head_two_low, WP[at(j * WIDTH, WIDTH), :])
        for q in range(4):
            centred, before = norm_terms(H1[j, :, lanes(q)], PRM4, 4 * j + q)
            du = DA4[j, :, lanes(q)] * gelu_slope(before) * CW[...]
            DA4[j, :, lanes(q)] = du
            MSG[X_FOUR_BACK + j, q : q + 1, :] = jnp.sum(du, axis=0, keepdims=True)
            MSG[X_FOUR_BACK + j, 4 + q : 5 + q, :] = jnp.sum(du * centred, axis=0, keepdims=True)
        announce(X_FOUR_BACK + j)

    D2F[...] = head_two_low.astype(F32)

    def share_rows(depth):
        own = pl.ds(pl.multiple_of(d * depth, 16), depth)

        @pl.loop(1, GROUP)
        def _(k):
            pltpu.make_async_remote_copy(
                D2F.at[pl.ds(0, depth), :],
                D2A.at[own, :],
                row_sem.at[1],
                row_sem.at[2],
                device_id=(r, lax.rem(d + k, GROUP)),
                device_id_type=MESH,
            ).start()

        D2A[own, :] = D2F[0:depth, :]

    by_size(share_rows)
    proto_own = proto_half(r)
    proto_swap.wait_recv()
    RC_P[...] += proto_own
    proto_strip.start(0)

    @pl.loop(0, 4)
    def _(j):
        collect(X_FOUR_BACK + j)
        whole_back(X_FOUR_BACK + j, whole_crops, PRM4, 4 * j, 24 + 4 * j)
        for q in range(4):
            centred, _ = norm_terms(H1[j, :, lanes(q)], PRM4, 4 * j + q)
            DH1[:, lanes(4 * j + q)] = back_through(
                DA4[j, :, lanes(q)], centred, CW[...], PRM4, 4 * j + q
            ).astype(BF)

    pooled_arrived(2)
    pooled_gather(3)
    DP = H1
    for j in range(4):
        DP[j] = jnp.zeros((SLOTS, WIDTH), F32)

    @pl.loop(0, 4)
    def _(i):
        for half in range(2):
            k = 2 * i + half
            hidden_load(k, half).wait()
            back = mm_t(DH1[:, lanes(k, 256)], WHB[half])
            for j in range(4):
                DP[j] += back[:, lanes(j, WIDTH)]

            @pl.when(k + 2 < 8)
            def _():
                hidden_load(k + 2, half).start()

    @pl.loop(0, 4)
    def _(j):
        rows = at(j * ROWS, ROWS)
        for q in range(4):
            high, low = two_parts(DP[j, :, lanes(q)] * area_inv)
            out_grad = mm(PT[...], high) + mm(PT[...], low)
            centred, before = norm_terms(C3[rows, lanes(q)], PRM3, 4 * j + q)
            joined = before + F[:, lanes(4 * j + q)].astype(F32)
            du = out_grad * gelu_slope(joined)
            DJ[rows, lanes(q)] = du
            MSG[X_THREE_BACK + j, q : q + 1, :] = jnp.sum(du, axis=0, keepdims=True)
            MSG[X_THREE_BACK + j, 4 + q : 5 + q, :] = jnp.sum(du * centred, axis=0, keepdims=True)
        announce(X_THREE_BACK + j)

    advance([(proto_strip, 0)])

    @pl.loop(0, 4)
    def _(j):
        collect(X_THREE_BACK + j)
        whole_back(X_THREE_BACK + j, whole_rows, PRM3, 4 * j, 8 + 4 * j)
        rows = at(j * ROWS, ROWS)
        for q in range(4):
            centred, _ = norm_terms(C3[rows, lanes(q)], PRM3, 4 * j + q)
            COLS[:, lanes(4 * j + q)] = back_through(
                DJ[rows, lanes(q)], centred, RW[...], PRM3, 4 * j + q
            ).astype(BF)

    pl.semaphore_signal(free_sem, inc=1, device_id=(1 - r, d), device_id_type=MESH)
    centre = pl.ds(EDGE, ROWS)

    @pl.loop(0, 2)
    def _(h):
        APAD[centre, lanes(h, 256)] = mm_t(COLS[:, 0:DEPTH], WE[at(h * 256, 256), :])

    def through_gelu(values, prm, x):
        for q in range(4):
            centred, before = norm_terms(values[:, lanes(q)], prm, q)
            du = APAD[centre, lanes(q)] * gelu_slope(before) * RW[...]
            APAD[centre, lanes(q)] = du
            MSG[x, q : q + 1, :] = jnp.sum(du, axis=0, keepdims=True)
            MSG[x, 4 + q : 5 + q, :] = jnp.sum(du * centred, axis=0, keepdims=True)
        announce(x)

    through_gelu(C2, PRM2, X_TWO_BACK)

    @pl.loop(0, 4)
    def _(j):
        OUT[half_tile(j), :] = t_mm(A2[:, half_tile(1 - r)], COLS[:, lanes(j, WIDTH)])
        core_copy(OUT.at[half_tile(j), :], RC_E.at[half_tile(j), :], j, j).start()

    @pl.loop(0, 4)
    def _(j):
        own = t_mm(A2[:, half_tile(r)], COLS[:, lanes(j, WIDTH)])
        tile = RC_E.at[half_tile(j), :]
        core_copy(tile, tile, j, j).wait_recv()
        tile[...] += own

    for strip in expand_strips:
        strip.start(0)
    collect(X_TWO_BACK)
    whole_back(X_TWO_BACK, whole_rows, PRM2, 0, 4)
    for q in range(4):
        centred, _ = norm_terms(C2[:, lanes(q)], PRM2, q)
        APAD[centre, lanes(q)] = back_through(APAD[centre, lanes(q)], centred, RW[...], PRM2, q)
    spread_taps(-1)

    @pl.loop(0, 2)
    def _(h):
        total = mm_t(COLS[:, 0:WIDTH], WS[at(h * 256, 256), :])
        for tap in range(1, 9):
            total += mm_t(
                COLS[:, tap * WIDTH : (tap + 1) * WIDTH], WS[at(tap * WIDTH + h * 256, 256), :]
            )
        APAD[centre, lanes(h, 256)] = total

    through_gelu(C1, PRM1, X_ONE_BACK)
    advance([(proto_strip, 1)])

    def half_tap(which, m):
        g = 9 * which + m
        return mm(A1T[half_tile(lax.rem(g, 2)), :], COLS[:, lanes(g // 2, WIDTH)])

    pl.semaphore_wait(free_sem, 1)

    def ring(slot):
        tile = OUT.at[half_tile(slot), :]
        return tile, core_copy(tile, tile, slot, 0)

    def add_half_tap(m):
        own = half_tap(r, m)
        tile = C3.at[half_tile(m), :]
        core_copy(tile, tile, 0, 4 + m).wait_recv()
        tile[...] += own

    @pl.loop(0, 9)
    def _(m):
        slot = lax.rem(m, 4)
        tile, last = ring(slot)
        last.wait_send()
        tile[...] = half_tap(1 - r, m)
        core_copy(tile, C3.at[half_tile(m), :], slot, 4 + m).start()

        @pl.when(m >= 2)
        def _():
            add_half_tap(m - 2)

    add_half_tap(7)
    add_half_tap(8)
    for strip in spatial_strips:
        strip.start(0)

    collect(X_ONE_BACK)
    whole_back(X_ONE_BACK, whole_rows, PRM1, 0, 0)
    for q in range(4):
        centred, _ = norm_terms(C1[:, lanes(q)], PRM1, q)
        A2[:, lanes(q)] = back_through(APAD[centre, lanes(q)], centred, RW[...], PRM1, q).astype(BF)

    def reduce_tile(which, j):
        columns = pl.ds(pl.multiple_of(which * 1024 + j * 256, 256), 256)
        return t_mm(F[:, columns], A2[...])

    def reduce_rows(j):
        return C3.at[pl.ds(pl.multiple_of(SPATIAL_HALF + j * 256, 256), 256), :]

    @pl.loop(0, 4)
    def _(j):
        slot = lax.rem(j + 1, 4)
        tile, last = ring(slot)
        last.wait_send()
        tile[...] = reduce_tile(1 - r, j)
        core_copy(tile, reduce_rows(j), slot, 13 + j).start()

    @pl.loop(0, 4)
    def _(j):
        own = reduce_tile(r, j)
        tile = reduce_rows(j)
        core_copy(tile, tile, 0, 13 + j).wait_recv()
        tile[...] += own

    for strip in reduce_strips:
        strip.start(0)

    collect(X_EXTRA)
    extra = jnp.sum(RECV[X_EXTRA], axis=0)
    FAR[0, 88:96, :] = extra
    far = pltpu.make_async_remote_copy(
        FAR.at[0],
        FAR.at[1],
        far_sem.at[0],
        far_sem.at[1],
        device_id=(1 - r, d),
        device_id_type=MESH,
    )
    far.start()

    def wave(strips, stage):
        return [(strip, stage) for strip in strips]

    advance(wave(expand_strips, 0))

    @pl.loop(0, 4)
    def _(j):
        rows = at(j * ROWS, ROWS)
        grad = mm_t(A2[...], WR[at(j * WIDTH, WIDTH), :])
        for q in range(4):
            DJ[rows, lanes(q)] = (DJ[rows, lanes(q)] + grad[:, lanes(q)]) * RW[...]
        pltpu.make_async_copy(
            DJ.at[rows, :], feature_out.at[0, :, lanes(j, WIDTH)], out_sem.at[0]
        ).start()

    advance(wave(expand_strips, 1))
    advance(wave(spatial_strips, 0))

    pooled_arrived(3)

    def rows_in(depth):
        area = D2A.at[pl.ds(0, (GROUP - 1) * depth), :]
        pltpu.make_async_copy(area, area, row_sem.at[2]).wait()
        pltpu.make_async_copy(area, area, row_sem.at[1]).wait()

    by_size(rows_in)
    loads[4].wait()
    for slot in range(4):
        ring(slot)[1].wait_send()
    CH = OUT
    HACC[...] = jnp.zeros_like(HACC)
    PACC[...] = jnp.zeros_like(PACC)
    unit_rows = pl.ds(pl.multiple_of(d * LANES, LANES), LANES)

    @pl.loop(0, jnp.where(big, 1, 4))
    def _(c):
        rows = half_tile(c)
        for j in range(4):
            pltpu.make_async_copy(
                PG.at[rows, lanes(j, WIDTH)], CH.at[pl.ds(256 * j, 256), :], out_sem.at[1]
            ).start()
        pltpu.make_async_copy(CH, CH, out_sem.at[1]).wait()
        head = mm(CH[0:256, :].astype(BF), WHC[0:WIDTH, :])
        for j in range(1, 4):
            head += mm(CH[256 * j : 256 * j + 256, :].astype(BF), WHC[WIDTH * j : WIDTH * j + WIDTH, :])
        centred, before = norm_terms(head, PRM4, d)
        low_rows = D2A[rows, :].astype(BF)
        du = mm_t(low_rows, WP[unit_rows, :]) * gelu_slope(before)
        dh = back_through(du, centred, 1.0, PRM4, d).astype(BF)
        PACC[...] += t_mm(gelu(before).astype(BF), low_rows)
        for j in range(4):
            HACC[WIDTH * j : WIDTH * j + WIDTH, :] += t_mm(
                CH[256 * j : 256 * j + 256, :].astype(BF), dh
            )

    def hidden_half(which):
        return HACC.at[pl.ds(pl.multiple_of(which * 1024, 1024), 1024), :]

    hidden_swap = core_copy(hidden_half(1 - r), HREC, 5, 18)
    hidden_swap.start()
    project_swap = core_copy(PACC, PREC, 6, 19)
    project_swap.start()
    advance([(proto_strip, 2)])
    hidden_swap.wait_recv()
    hidden_half(r)[...] += HREC[...]

    @pl.loop(1, GROUP)
    def _(k):
        to = lax.rem(d + k, GROUP)
        pltpu.make_async_remote_copy(
            HACC.at[pl.ds(pl.multiple_of(r * 1024 + to * 64, 64), 64), :],
            HAL.at[d],
            row_sem.at[3],
            row_sem.at[4],
            device_id=(r, to),
            device_id_type=MESH,
        ).start()

    HAL[d] = HACC[pl.ds(pl.multiple_of(r * 1024 + d * 64, 64), 64), :]

    project_swap.wait()
    PACC[...] = jnp.where(big, PACC[...], PREC[...]) + jnp.where(big, PREC[...], PACC[...])
    serves = (d // 8) == r
    first_owner = lax.rem(2 * d, GROUP)
    for half in range(2):
        owner = first_owner + half
        part = PACC.at[pl.ds(64 * half, 64), :]
        local = owner == d

        @pl.when(serves & jnp.logical_not(local))
        def _():
            pltpu.make_async_remote_copy(
                part, PIN, core_send.at[7 + half], row_sem.at[5],
                device_id=(r, owner), device_id_type=MESH,
            ).start()

        @pl.when(serves & local)
        def _():
            PIN[...] = part[...]

    chip_of_own = (r * GROUP + d) // 2
    from_self = chip_of_own == d

    advance(wave(reduce_strips, 0))
    advance(wave(expand_strips, 2))
    advance(wave(spatial_strips, 1))
    advance([(proto_strip, 3)])
    proto_own_rows = pl.ds(pl.multiple_of(r * PROTO_HALF + d * 96, 16), 96)
    TAB[proto_own_rows, :] = RC_P[pl.ds(pl.multiple_of(d * 96, 16), 96), :]
    proto_order = (8, 2, 1, 4)
    every_lane = slice(0, LANES)

    def proto_gather(stage):
        gather_start(TAB, r * PROTO_HALF, 96, every_lane, proto_order, stage, 3)

    def proto_arrived(stage):
        gather_wait(TAB, 96, every_lane, stage, 3, gather_recv)

    proto_gather(0)
    advance(wave(reduce_strips, 1))
    proto_arrived(0)
    proto_gather(1)
    advance(wave(expand_strips, 3))
    advance(wave(spatial_strips, 2))
    proto_arrived(1)
    proto_gather(2)
    advance(wave(reduce_strips, 2))
    proto_arrived(2)
    proto_gather(3)
    for j in range(4):
        for q in range(4):
            expand_out[pl.ds(4 * j + q, 16, stride=16), :] = RC_E[
                pl.ds(pl.multiple_of(256 * j + d * 16, 16), 16), lanes(q)
            ]
    far.wait()
    both = jnp.where(big, FAR[0], FAR[1]) + jnp.where(big, FAR[1], FAR[0])
    gain_out[...] = both[0:40]
    shift_out[0:40, :] = both[48:88]
    shift_out[40:41, :] = both[88:89]
    loss_out[...] = jnp.broadcast_to(both[89:90], (8, LANES)) / float(GROUP * IMAGES)
    arrived = HAL.at[pl.ds(0, GROUP - 1)]
    pltpu.make_async_copy(arrived, arrived, row_sem.at[4]).wait()
    pltpu.make_async_copy(arrived, arrived, row_sem.at[3]).wait()
    for source in range(GROUP):
        hidden_out[pl.ds(source, 64, stride=16), :] = HAL[source]

    @pl.when(jnp.logical_not(from_self))
    def _():
        pltpu.make_async_copy(PIN, PIN, row_sem.at[5]).wait()

    project_out[...] = PIN[...]
    for half in range(2):

        @pl.when(serves & jnp.logical_not(first_owner + half == d))
        def _():
            pltpu.make_async_copy(PIN, PIN, core_send.at[7 + half]).wait()

    proto_arrived(3)
    proto_part = TAB.at[pl.ds(pl.multiple_of(r * PROTO_HALF, LANES), PROTO_HALF), :]
    proto_far = core_copy(proto_part, proto_part, 9, 20)
    proto_far.start()
    advance(wave(spatial_strips, 3))
    for q in range(4):
        spatial_out[pl.ds(q, 144, stride=4), :] = C3[
            pl.ds(pl.multiple_of(d * 144, 16), 144), lanes(q)
        ]
    proto_far.wait()
    for m in range(6):
        for q in range(4):
            chunk_rows = pl.ds((4 * m + q) * LANES, LANES)
            CH[LANES * m : LANES * m + LANES, lanes(q)] = TAB[chunk_rows, :].T
        pltpu.make_async_copy(
            CH.at[pl.ds(LANES * m, LANES), :], proto_out.at[:, lanes(m, WIDTH)], out_sem.at[2]
        ).start()
    advance(wave(reduce_strips, 3))
    for q in range(4):
        reduce_out[pl.ds(q, 64, stride=4), :] = C3[
            pl.ds(pl.multiple_of(SPATIAL_HALF + d * 64, 16), 64), lanes(q)
        ]

    @pl.when(big)
    def _():
        forward_units.wait_send()

    hidden_swap.wait_send()
    proto_swap.wait_send()
    for stage in range(4):

        def pooled_sent(depth):
            for number, (columns, _) in enumerate(pooled_parts):
                gather_wait(PG, depth, columns, stage, number, gather_send)

        by_size(pooled_sent)
        gather_wait(TAB, 96, every_lane, stage, 3, gather_send)
    for strip in spatial_strips + reduce_strips + expand_strips + [proto_strip]:
        strip.close()
    pltpu.make_async_copy(feature_out.at[0], feature_out.at[0], out_sem.at[0]).wait()
    pltpu.make_async_copy(proto_out, proto_out, out_sem.at[2]).wait()


def tower(
    features,
    crop_counts,
    crop_image,
    w_reduce,
    w_spatial,
    w_expand,
    w_hidden,
    w_project,
    prototypes,
    norm_gain,
    norm_shift,
):
    protos = jnp.pad(prototypes, ((0, 0), (0, PADDED - PROTOS)))
    anywhere = pl.BlockSpec(memory_space=pl.ANY)
    inside = pl.BlockSpec(memory_space=pltpu.VMEM)
    in_hbm = pl.BlockSpec(memory_space=pltpu.HBM)

    def vm(*shape, dtype=F32):
        return pltpu.VMEM(shape, dtype)

    dma = pltpu.SemaphoreType.DMA

    def shaped(*shape):
        return jax.ShapeDtypeStruct(shape, F32)

    return pl.pallas_call(
        tower_kernel,
        out_shape=(
            shaped(8, LANES),
            shaped(1, ROWS, DEPTH),
            shaped(256, LANES),
            shaped(576, LANES),
            shaped(256, LANES),
            shaped(1024, LANES),
            shaped(64, LANES),
            shaped(FEATS, PADDED),
            shaped(40, LANES),
            shaped(41, LANES),
            shaped(GROUP * SLOTS, DEPTH),
            shaped(4, 15 * 144, LANES),
            shaped(4, 15 * 64, LANES),
            shaped(4, 15 * 16, WIDTH),
            shaped(15 * 96, LANES),
        ),
        in_specs=[anywhere, inside, inside] + [anywhere] * 6 + [inside, inside],
        out_specs=(
            (inside, anywhere) + (inside,) * 5 + (anywhere, inside, inside) + (in_hbm,) * 5
        ),
        scratch_shapes=[
            vm(ROWS, DEPTH, dtype=BF),
            vm(DEPTH, WIDTH, dtype=BF),
            vm(9 * WIDTH, WIDTH, dtype=BF),
            vm(WIDTH, DEPTH, dtype=BF),
            vm(2, DEPTH, 256, dtype=BF),
            vm(DEPTH, LANES, dtype=BF),
            vm(HIDDEN, FEATS, dtype=BF),
            vm(FEATS, PADDED, dtype=BF),
            vm(ROWS, WIDTH),
            vm(ROWS, WIDTH),
            vm(SPATIAL_HALF + 1024, WIDTH),
            vm(4 * ROWS, WIDTH),
            vm(ROWS + 2 * EDGE, WIDTH),
            vm(ROWS, 9 * WIDTH, dtype=BF),
            vm(ROWS, WIDTH, dtype=BF),
            vm(WIDTH, ROWS, dtype=BF),
            vm(SLOTS, DEPTH, dtype=BF),
            vm(4, SLOTS, WIDTH),
            vm(SLOTS, HIDDEN, dtype=BF),
            vm(4, SLOTS, WIDTH),
            vm(SLOTS, HIDDEN, dtype=BF),
            vm(SLOTS, PADDED, dtype=BF),
            vm(SLOTS, FEATS, dtype=BF),
            vm(SLOTS, DEPTH),
            vm(SLOTS, FEATS),
            vm(GROUP * SLOTS, FEATS),
            vm(PADDED, GROUP * IMAGES),
            vm(2 * IMAGES, PADDED),
            vm(GROUP * IMAGES, LANES),
            vm(GROUP * IMAGES, LANES),
            vm(GROUP, 2 * IMAGES, FEATS),
            vm(2 * IMAGES, FEATS),
            vm(ROWS, LANES),
            vm(SLOTS, LANES),
            vm(ROWS, LANES),
            vm(ROWS, LANES),
            vm(ROWS, SLOTS, dtype=BF),
            vm(SLOTS, ROWS, dtype=BF),
            vm(4, 8, LANES),
            vm(4, 8, LANES),
            vm(16, 8, LANES),
            vm(16, 8, LANES),
            vm(EXCHANGES, 8, LANES),
            vm(EXCHANGES, GROUP, 8, LANES),
            vm(2, 96, LANES),
            vm(1024, WIDTH),
            vm(1024, WIDTH),
            vm(PROTO_HALF, LANES),
            vm(PROTO_HALF, LANES),
            vm(2, 8 * 144, LANES),
            vm(2, 8 * 16, WIDTH),
            vm(DEPTH, LANES),
            vm(1024, LANES),
            vm(GROUP, 64, LANES),
            vm(LANES, LANES),
            vm(LANES, LANES),
            vm(64, LANES),
            dma((7,)),
            dma((EXCHANGES,)),
            dma((EXCHANGES,)),
            dma((4,)),
            dma((4,)),
            dma((2,)),
            dma((2,)),
            dma((13, 4)),
            dma((13, 4)),
            dma((2,)),
            dma((4, 4)),
            dma((4, 4)),
            dma((10,)),
            dma((21,)),
            dma((6,)),
            pltpu.SemaphoreType.REGULAR,
        ],
        compiler_params=pltpu.CompilerParams(
            collective_id=0, has_side_effects=True, vmem_limit_bytes=63 << 20
        ),
    )(
        features,
        crop_image.reshape(1, SLOTS),
        crop_counts.reshape(1, IMAGES),
        w_reduce,
        w_spatial,
        w_expand,
        w_hidden,
        w_project,
        protos,
        norm_gain.reshape(40, LANES),
        norm_shift.reshape(41, LANES),
    )


def fused_body(*arrays):
    loss, feature, reduce, spatial, expand, hidden, project, proto, gain, shift = tower(*arrays)[:10]
    return (
        loss[0, 0],
        feature,
        reduce.reshape(-1),
        spatial.reshape(-1),
        expand.reshape(-1),
        hidden.reshape(-1),
        project.reshape(-1),
        proto[:, :PROTOS].reshape(-1),
        gain.reshape(-1),
        shift.reshape(-1),
    )


def solution(mesh):
    return jax.shard_map(
        fused_body if mesh.shape["dp"] == GROUP else body,
        mesh=mesh,
        in_specs=(P("res", "dp", None), P("dp"), P("dp"), P(), P(), P(), P(), P(), P(), P(), P()),
        out_specs=(
            P(),
            P("res", "dp", None),
            P(("res", "dp")),
            P(("res", "dp")),
            P(("res", "dp")),
            P(("res", "dp")),
            P(("res", "dp")),
            P(),
            P(),
            P(),
        ),
        check_vma=False,
    )
```

```python
import jax
import jax.numpy as jnp
from jax import lax
from jax.experimental import pallas as pl
from jax.experimental.pallas import tpu as pltpu
from jax.sharding import PartitionSpec as P

LSIDE = 7
SSIDE = 3
SINK = 3


HIGH = lax.Precision.HIGHEST
SOFTMAX_HEAT = 0.1
SHARPNESS = 0.05
EPS_NORM = 1e-05
EPS_UNIT = 1e-06


def combined_all(part, axis, combine):
    gathered = jax.tree.map(lambda a: lax.all_gather(a, axis), part)

    def take(source):
        return jax.tree.map(lambda a: lax.dynamic_index_in_dim(a, source, 0, False), gathered)

    return lax.fori_loop(
        1, lax.axis_size(axis), lambda source, state: combine(state, take(source)), take(0)
    )


def from_behind(value, axis, steps):
    count = lax.axis_size(axis)
    leading, last = (max(0, -steps), min(count, count - steps))
    return lax.ppermute(value, axis, [(source, source + steps) for source in range(leading, last)])


def row_contract(left, right):
    return lax.dot_general(
        left, right, (((0,), (0,)), ((), ())), preferred_element_type=jnp.float32
    )


def times_transposed(left, right):
    return lax.dot_general(
        left, right, (((1,), (1,)), ((), ())), preferred_element_type=jnp.float32
    )


def split_norms(vector, width, depth):
    return (
        vector[:width],
        vector[width : 2 * width],
        vector[2 * width : 2 * width + depth],
        vector[2 * width + depth :],
    )


def displaced(values, offset):
    if offset == 0:
        return values
    filler = jnp.zeros((abs(offset),) + values.shape[1:], values.dtype)
    if offset > 0:
        return jnp.concatenate([values[offset:], filler], axis=0)
    return jnp.concatenate([filler, values[:offset]], axis=0)


def tap_layout(row_count, big_crop):
    row_ids = jnp.arange(row_count)
    side_len = jnp.where(big_crop, LSIDE, SSIDE)
    pixel = row_ids % (side_len * side_len)
    line_ids = pixel // side_len
    column_ids = pixel % side_len
    layout = []
    for tap_y in (-1, 0, 1):
        for tap_x in (-1, 0, 1):
            inside = (
                (line_ids + tap_y >= 0)
                & (line_ids + tap_y < side_len)
                & (column_ids + tap_x >= 0)
                & (column_ids + tap_x < side_len)
            )
            layout.append((inside[:, None], tap_y * LSIDE + tap_x, tap_y * SSIDE + tap_x))
    return layout


def gather_taps(acts, layout, big_crop):
    pieces = []
    for inside, step_large, step_small in layout:
        moved_rows = jnp.where(big_crop, displaced(acts, step_large), displaced(acts, step_small))
        pieces.append(jnp.where(inside, moved_rows, jnp.zeros_like(moved_rows)))
    return jnp.concatenate(pieces, axis=1)


def scatter_taps(column_grad, layout, big_crop, channels):
    result = jnp.zeros((column_grad.shape[0], channels), jnp.float32)
    for tap_index, (inside, step_large, step_small) in enumerate(layout):
        piece = column_grad[:, tap_index * channels : (tap_index + 1) * channels]
        piece = jnp.where(inside, piece, jnp.zeros_like(piece))
        result = result + jnp.where(
            big_crop, displaced(piece, -step_large), displaced(piece, -step_small)
        )
    return result


def merge_moments(first_part, second_part):
    merged_count = first_part[0] + second_part[0]
    delta = second_part[1] - first_part[1]
    merged_mean = first_part[1] + delta * (second_part[0] / merged_count)
    merged_spread = (
        first_part[2]
        + second_part[2]
        + delta * delta * (first_part[0] * second_part[0] / merged_count)
    )
    return (merged_count, merged_mean, merged_spread)


def moments(values, weight):
    row_total = jnp.sum(weight)
    local_mean = jnp.sum(values * weight, axis=0) / row_total
    centred = values - local_mean
    local_spread = jnp.sum(weight * centred * centred, axis=0)
    whole_count, mean_vec, whole_spread = combined_all(
        (row_total, local_mean, local_spread), "dp", merge_moments
    )
    return (mean_vec, whole_spread / whole_count, whole_count)


def normalize(values, weight, gain_vec, shift_vec):
    mean_vec, var_vec, whole_count = moments(values, weight)
    scale_vec = lax.rsqrt(var_vec + EPS_NORM)
    centred = (values - mean_vec) * scale_vec
    return (centred * gain_vec + shift_vec, (centred, scale_vec, whole_count))


def normalize_back(upstream, weight, gain_vec, saved_stats):
    centred, scale_vec, whole_count = saved_stats
    upstream = upstream * weight
    local_first = jnp.sum(upstream, axis=0)
    local_second = jnp.sum(upstream * centred, axis=0)
    whole_first, whole_second = lax.psum((local_first, local_second), "dp")
    result = (
        gain_vec
        * scale_vec
        * (upstream - weight * (whole_first + centred * whole_second) / whole_count)
    )
    return (result, local_second, local_first)


def gelu_back(before, upstream):
    return jax.vjp(jax.nn.gelu, before)[1](upstream)[0]


def spread_rows(crop_grad, crop_total, area):
    depth = crop_grad.shape[1]
    widened = jnp.broadcast_to(crop_grad[:crop_total, None, :], (crop_total, area, depth))
    return widened.reshape(crop_total * area, depth) / area


def body(
    features,
    crop_counts,
    crop_image,
    w_reduce,
    w_spatial,
    w_expand,
    w_hidden,
    w_project,
    prototypes,
    norm_gain,
    norm_shift,
):
    inputs = features[0]
    row_count = inputs.shape[0]
    depth = w_reduce.shape[0]
    width = w_reduce.shape[1]
    hidden = w_hidden.shape[1]
    slot_count = crop_image.shape[0]
    image_count = crop_counts.shape[0]
    image_total = image_count * lax.axis_size("dp")
    big_crop = lax.axis_index("res") == 0
    first_image = lax.axis_index("dp") * image_count
    live_slot = (crop_image >= 0).astype(jnp.float32)
    slot_rows = SSIDE * SSIDE * slot_count
    live_rows = jnp.concatenate(
        [jnp.repeat(live_slot, SSIDE * SSIDE), jnp.zeros((row_count - slot_rows,), jnp.float32)]
    )
    row_weight = jnp.where(big_crop, jnp.ones_like(live_rows), live_rows)[:, None]
    large_crops = (jnp.arange(slot_count) < 2 * image_count).astype(jnp.float32)
    crop_weight = jnp.where(big_crop, large_crops, live_slot)[:, None]
    gain_one, gain_two, gain_three, gain_four = split_norms(norm_gain, width, depth)
    shift_one, shift_two, shift_three, shift_rest = split_norms(norm_shift, width, depth)
    shift_four = shift_rest[:hidden]
    head_bias = shift_rest[hidden:]
    layout = tap_layout(row_count, big_crop)
    conv_one = jnp.dot(inputs, w_reduce, preferred_element_type=jnp.float32)
    norm_one, saved_one = normalize(conv_one, row_weight, gain_one, shift_one)
    act_one = jax.nn.gelu(norm_one).astype(jnp.bfloat16)
    columns = gather_taps(act_one, layout, big_crop)
    conv_two = jnp.dot(columns, w_spatial, preferred_element_type=jnp.float32)
    norm_two, saved_two = normalize(conv_two, row_weight, gain_two, shift_two)
    act_two = jax.nn.gelu(norm_two).astype(jnp.bfloat16)
    conv_three = jnp.dot(act_two, w_expand, preferred_element_type=jnp.float32)
    norm_three, saved_three = normalize(conv_three, row_weight, gain_three, shift_three)
    joined = norm_three + inputs.astype(jnp.float32)
    block_out = jax.nn.gelu(joined)
    large_pool = jnp.mean(block_out.reshape(2 * image_count, LSIDE * LSIDE, depth), axis=1)
    large_pool = jnp.concatenate(
        [large_pool, jnp.zeros((slot_count - 2 * image_count, depth), jnp.float32)], axis=0
    )
    small_pool = jnp.mean(block_out[:slot_rows].reshape(slot_count, SSIDE * SSIDE, depth), axis=1)
    pooled = jnp.where(big_crop, large_pool, small_pool).astype(jnp.bfloat16)
    head_one = jnp.dot(pooled, w_hidden, preferred_element_type=jnp.float32)
    norm_four, saved_four = normalize(head_one, crop_weight, gain_four, shift_four)
    act_four = jax.nn.gelu(norm_four).astype(jnp.bfloat16)
    head_two = jnp.dot(act_four, w_project, preferred_element_type=jnp.float32) + head_bias
    unit, unit_back = jax.vjp(
        lambda vec: vec * lax.rsqrt(jnp.sum(vec * vec, axis=1, keepdims=True) + EPS_UNIT), head_two
    )
    unit_low = unit.astype(jnp.bfloat16)
    scores = jnp.dot(unit_low, prototypes, preferred_element_type=jnp.float32)
    table = jnp.exp(scores[: 2 * image_count].reshape(2, image_count, -1) / SHARPNESS)
    for sweep in range(SINK):
        column_total = lax.psum(jnp.sum(table, axis=1), "dp")
        table = table / column_total[:, None, :]
        table = table / jnp.sum(table, axis=2, keepdims=True)
    own_codes = table
    far_codes = from_behind(own_codes, "res", 1)
    weight_image = 1.0 / (2.0 * (1.0 + crop_counts.astype(jnp.float32)))
    onehot = ((crop_image - first_image)[:, None] == jnp.arange(image_count)[None, :]).astype(
        jnp.float32
    )
    slot_scale = jnp.dot(onehot, weight_image, precision=HIGH) * live_slot
    small_targets = jnp.dot(onehot, far_codes[0] + far_codes[1], precision=HIGH)

    def partial_loss(scores_by_row):
        log_probability = jax.nn.log_softmax(scores_by_row / SOFTMAX_HEAT, axis=-1)
        view_zero = log_probability[:image_count]
        view_one = log_probability[image_count : 2 * image_count]
        large_share = -jnp.sum(
            weight_image
            * (
                jnp.sum(own_codes[0] * view_one, axis=-1)
                + jnp.sum(own_codes[1] * view_zero, axis=-1)
            )
        )
        small_share = -jnp.sum(slot_scale * jnp.sum(small_targets * log_probability, axis=-1))
        return jnp.where(big_crop, large_share, small_share)

    local_total, total_back = jax.vjp(partial_loss, scores)
    whole_total = lax.psum(local_total, ("res", "dp"))
    loss = whole_total / image_total
    score_grad = total_back(jnp.ones_like(local_total))[0].astype(jnp.bfloat16)
    proto_grad = row_contract(unit_low, score_grad)
    unit_grad = times_transposed(score_grad, prototypes)
    head_two_grad = unit_back(unit_grad)[0]
    bias_grad = jnp.sum(head_two_grad, axis=0)
    head_two_low = head_two_grad.astype(jnp.bfloat16)
    project_grad = row_contract(act_four, head_two_low)
    act_four_grad = times_transposed(head_two_low, w_project)
    head_one_grad, gain_four_grad, shift_four_grad = normalize_back(
        gelu_back(norm_four, act_four_grad), crop_weight, gain_four, saved_four
    )
    head_one_low = head_one_grad.astype(jnp.bfloat16)
    hidden_grad = row_contract(pooled, head_one_low)
    pooled_grad = times_transposed(head_one_low, w_hidden)
    large_spread = spread_rows(pooled_grad, 2 * image_count, LSIDE * LSIDE)
    small_spread = jnp.concatenate(
        [
            spread_rows(pooled_grad, slot_count, SSIDE * SSIDE),
            jnp.zeros((row_count - slot_rows, depth), jnp.float32),
        ],
        axis=0,
    )
    out_grad = jnp.where(big_crop, large_spread, small_spread)
    joined_grad = gelu_back(joined, out_grad)
    three_grad, gain_three_grad, shift_three_grad = normalize_back(
        joined_grad, row_weight, gain_three, saved_three
    )
    three_low = three_grad.astype(jnp.bfloat16)
    expand_grad = row_contract(act_two, three_low)
    act_two_grad = times_transposed(three_low, w_expand)
    two_grad, gain_two_grad, shift_two_grad = normalize_back(
        gelu_back(norm_two, act_two_grad), row_weight, gain_two, saved_two
    )
    two_low = two_grad.astype(jnp.bfloat16)
    spatial_grad = row_contract(columns, two_low)
    column_grad = times_transposed(two_low, w_spatial)
    act_one_grad = scatter_taps(column_grad, layout, big_crop, width)
    one_grad, gain_one_grad, shift_one_grad = normalize_back(
        gelu_back(norm_one, act_one_grad), row_weight, gain_one, saved_one
    )
    one_low = one_grad.astype(jnp.bfloat16)
    reduce_grad = row_contract(inputs, one_low)
    input_grad = (joined_grad + times_transposed(one_low, w_reduce)) * row_weight
    weight_terms = (
        reduce_grad.reshape(-1),
        spatial_grad.reshape(-1),
        expand_grad.reshape(-1),
        hidden_grad.reshape(-1),
        project_grad.reshape(-1),
    )
    summed = (
        lax.psum_scatter(weight_terms[0], ("res", "dp"), scatter_dimension=0, tiled=True),
        lax.psum_scatter(weight_terms[1], ("res", "dp"), scatter_dimension=0, tiled=True),
        lax.psum_scatter(weight_terms[2], ("res", "dp"), scatter_dimension=0, tiled=True),
        lax.psum_scatter(weight_terms[3], ("res", "dp"), scatter_dimension=0, tiled=True),
        lax.psum_scatter(weight_terms[4], ("res", "dp"), scatter_dimension=0, tiled=True),
    )
    gain_local = jnp.concatenate([gain_one_grad, gain_two_grad, gain_three_grad, gain_four_grad])
    shift_local = jnp.concatenate(
        [shift_one_grad, shift_two_grad, shift_three_grad, shift_four_grad, bias_grad]
    )
    gain_total, shift_total, proto_total = lax.psum(
        (gain_local, shift_local, proto_grad.reshape(-1)), ("res", "dp")
    )
    return (
        loss,
        input_grad[None],
        summed[0],
        summed[1],
        summed[2],
        summed[3],
        summed[4],
        proto_total,
        gain_total,
        shift_total,
    )


MESH = pl.DeviceIdType.MESH
BF = jnp.bfloat16
F32 = jnp.float32
GROUP = 16
ROWS = 784
WIDTH = 512
DEPTH = 2048
HIDDEN = 2048
FEATS = 128
SLOTS = 64
IMAGES = 8
PROTOS = 3000
PADDED = 3072
LANES = 128
EDGE = 16
STRIPE = 112
TANH_IN = 0.7978845608
TANH_CUBE = 0.044715

X_COUNT, X_ONE, X_TWO, X_THREE, X_FOUR = 0, 1, 2, 3, 7
X_FOUR_BACK, X_EXTRA, EXCHANGES = 11, 15, 16
X_THREE_BACK, X_TWO_BACK, X_ONE_BACK = X_THREE, X_TWO, X_ONE
SPATIAL_HALF = 2304
PROTO_HALF = 1536


def mm(left, right):
    return jnp.dot(left, right, preferred_element_type=F32)


def mm_t(left, right):
    return lax.dot_general(left, right, (((1,), (1,)), ((), ())), preferred_element_type=F32)


def t_mm(left, right):
    return lax.dot_general(left, right, (((0,), (0,)), ((), ())), preferred_element_type=F32)


def gelu(v):
    return 0.5 * v * (1.0 + jnp.tanh(TANH_IN * (v + TANH_CUBE * (v * v * v))))


def gelu_slope(v):
    square = v * v
    t = jnp.tanh(TANH_IN * (v + TANH_CUBE * (v * square)))
    return 0.5 * (1.0 + t) + 0.5 * v * (1.0 - t * t) * (
        TANH_IN * (1.0 + (3.0 * TANH_CUBE) * square)
    )


def two_parts(v):
    high = v.astype(BF)
    return high, (v - high.astype(F32)).astype(BF)


def at(start, size):
    return pl.ds(pl.multiple_of(start, size if size % 8 == 0 else 8), size)


def lanes(index, width=LANES):
    if isinstance(index, int):
        return slice(index * width, (index + 1) * width)
    return pl.ds(pl.multiple_of(index * width, width), width)


def tower_kernel(
    feat,
    crop_row,
    count_row,
    w_reduce,
    w_spatial,
    w_expand,
    w_hidden,
    w_project,
    protos,
    gain,
    shift,
    loss_out,
    feature_out,
    reduce_out,
    spatial_out,
    expand_out,
    hidden_out,
    project_out,
    proto_out,
    gain_out,
    shift_out,
    PG,
    RB_S,
    RB_R,
    RB_E,
    RB_P,
    F,
    WR,
    WS,
    WE,
    WHB,
    WHC,
    WP,
    PROWS,
    PR,
    C1,
    C2,
    C3,
    DJ,
    APAD,
    COLS,
    A2,
    A1T,
    PO,
    H1,
    A4,
    DA4,
    DH1,
    DS,
    UL,
    D2F,
    D2A,
    TAB,
    Q,
    RACC,
    RINV,
    UNITS,
    UOWN,
    RW,
    CW,
    GRID,
    PT,
    P,
    PRM1,
    PRM2,
    PRM3,
    PRM4,
    MSG,
    RECV,
    FAR,
    OUT,
    RC_E,
    RC_P,
    OUT_P,
    STG,
    STGP,
    HB,
    HAL,
    PACC,
    PREC,
    PIN,
    load_sem,
    send_sem,
    recv_sem,
    unit_sem,
    out_sem,
    far_sem,
    wh_sem,
    rs_send,
    rs_recv,
    stage_sem,
    gather_send,
    gather_recv,
    core_send,
    core_recv,
    row_sem,
    free_sem,
):
    r = lax.axis_index("res")
    d = lax.axis_index("dp")
    big = r == 0
    area = jnp.where(big, LSIDE * LSIDE, SSIDE * SSIDE)
    area_f = area.astype(F32)
    side_f = jnp.where(big, float(LSIDE), float(SSIDE))
    area_inv = jnp.where(big, 1.0 / (LSIDE * LSIDE), 1.0 / (SSIDE * SSIDE))
    side_inv = jnp.where(big, 1.0 / LSIDE, 1.0 / SSIDE)

    loads = [
        pltpu.make_async_copy(source, target, load_sem.at[index])
        for index, (source, target) in enumerate(
            [
                (feat.at[0], F),
                (w_reduce, WR),
                (w_spatial, WS),
                (w_expand, WE),
                (w_hidden.at[:, pl.ds(pl.multiple_of(d * LANES, LANES), LANES)], WHC),
                (w_project, WP),
                (protos, PROWS),
            ]
        )
    ]
    loads[0].start()
    loads[1].start()

    def hidden_load(k, slot):
        return pltpu.make_async_copy(
            w_hidden.at[:, lanes(k, 256)], WHB.at[slot], wh_sem.at[slot]
        )


    barrier = pltpu.get_barrier_semaphore()

    @pl.loop(1, GROUP)
    def _(k):
        pl.semaphore_signal(
            barrier, inc=1, device_id=(r, lax.rem(d + k, GROUP)), device_id_type=MESH
        )

    pl.semaphore_signal(barrier, inc=1, device_id=(1 - r, d), device_id_type=MESH)

    slot_of = lax.broadcasted_iota(jnp.int32, (ROWS, SLOTS), 1)
    row_of = lax.broadcasted_iota(jnp.int32, (ROWS, SLOTS), 0)
    inside = ((row_of >= slot_of * area) & (row_of < slot_of * area + area)).astype(F32)
    lane_ids = lax.broadcasted_iota(jnp.int32, (1, SLOTS), 1)
    crop_ids = crop_row[...]
    live = jnp.where(big, (lane_ids < 2 * IMAGES).astype(F32), (crop_ids >= 0).astype(F32))
    RW[...] = jnp.broadcast_to(jnp.sum(inside * live, axis=1, keepdims=True), (ROWS, LANES))
    PT[...] = inside.astype(BF)
    slot_row = lax.broadcasted_iota(jnp.int32, (SLOTS, ROWS), 0)
    pixel_lane = lax.broadcasted_iota(jnp.int32, (SLOTS, ROWS), 1)
    P[...] = (
        ((pixel_lane >= slot_row * area) & (pixel_lane < slot_row * area + area))
        .astype(F32)
        .astype(BF)
    )
    square_row = lax.broadcasted_iota(jnp.int32, (SLOTS, SLOTS), 0)
    square_lane = lax.broadcasted_iota(jnp.int32, (SLOTS, SLOTS), 1)
    eye = (square_row == square_lane).astype(F32)
    CW[...] = jnp.broadcast_to(jnp.sum(eye * live, axis=1, keepdims=True), (SLOTS, LANES))
    live_total = jnp.sum(live, axis=1, keepdims=True)
    own_crops = jnp.broadcast_to(live_total, (1, LANES))
    own_rows = own_crops * area_f
    row_f = lax.broadcasted_iota(jnp.int32, (ROWS, LANES), 0).astype(F32)
    pixel = row_f - jnp.floor((row_f + 0.5) * area_inv) * area_f
    line = jnp.floor((pixel + 0.5) * side_inv)
    GRID[...] = line * 8.0 + (pixel - line * side_f)
    APAD[0:EDGE, :] = jnp.zeros((EDGE, WIDTH), F32)
    APAD[EDGE + ROWS :, :] = jnp.zeros((EDGE, WIDTH), F32)
    for prm, base, blocks in ((PRM1, 0, 4), (PRM2, 4, 4), (PRM3, 8, 16), (PRM4, 24, 16)):
        for q in range(blocks):
            prm[q, 2:3, :] = gain[base + q : base + q + 1, :]
            prm[q, 3:4, :] = shift[base + q : base + q + 1, :]
    MSG[X_COUNT] = jnp.broadcast_to(own_rows, (8, LANES))

    place = {1: lax.rem(d, 2), 2: lax.rem(d // 2, 2), 4: lax.rem(d // 4, 2), 8: d // 8}

    def across(mask):
        index = d
        for bit in (1, 2, 4, 8):
            if mask & bit:
                index = index + bit * (1 - 2 * place[bit])
        return index

    far_first = sorted(range(1, GROUP), key=lambda m: -(2 * (m // 8) + m // 4 % 2 + m // 2 % 2 + m % 2))
    peers = [across(mask) for mask in far_first]

    def announce(x):
        for peer in peers:
            pltpu.make_async_remote_copy(
                MSG.at[x],
                RECV.at[x, d],
                send_sem.at[x],
                recv_sem.at[x],
                device_id=(r, peer),
                device_id_type=MESH,
            ).start()

        RECV[x, d] = MSG[x]

    def collect(x):
        others = RECV.at[x, pl.ds(0, GROUP - 1)]
        pltpu.make_async_copy(others, others, recv_sem.at[x]).wait()
        pltpu.make_async_copy(others, others, send_sem.at[x]).wait()

    def partner(bit):
        return (r, across(bit))

    def block_of(order, stage, j, flip):
        index = 0
        for t, bit in enumerate(order):
            if t < stage:
                index = index + bit * place[bit]
            elif t == stage:
                index = index + bit * ((1 - place[bit]) if flip else place[bit])
            else:
                index = index + bit * ((j >> (t - stage - 1)) & 1)
        return index

    class Strip:
        def __init__(self, own, base, stride, depth, landing, staging, order, number):
            self.own, self.base, self.stride, self.depth = own, base, stride, depth
            self.landing, self.staging, self.order, self.number = landing, staging, order, number

        def block(self, index):
            start = pl.multiple_of(self.base + index * self.stride, 8)
            return self.own.at[pl.ds(start, self.depth), :]

        def rows(self, stage):
            first = 16 - (16 >> stage)
            return first * self.depth, (8 >> stage) * self.depth

        def start(self, stage):
            first, _ = self.rows(stage)
            for j in range(8 >> stage):
                pltpu.make_async_remote_copy(
                    self.block(block_of(self.order, stage, j, True)),
                    self.landing.at[pl.ds(first + j * self.depth, self.depth), :],
                    rs_send.at[self.number, stage],
                    rs_recv.at[self.number, stage],
                    device_id=partner(self.order[stage]),
                    device_id_type=MESH,
                ).start()

        def landed(self, stage):
            first, size = self.rows(stage)
            return self.landing.at[pl.ds(first, size), :]

        def fetch(self, stage, slot):
            area = self.landed(stage)
            pltpu.make_async_copy(area, area, rs_recv.at[self.number, stage]).wait()
            _, size = self.rows(stage)
            copy = pltpu.make_async_copy(
                area, self.staging.at[slot, pl.ds(0, size), :], stage_sem.at[slot]
            )
            copy.start()
            return copy

        def fold(self, stage, slot):
            for j in range(8 >> stage):
                target = self.block(block_of(self.order, stage, j, False))
                target[...] += self.staging[slot, j * self.depth : (j + 1) * self.depth, :]

        def close(self):
            for stage in range(4):
                area = self.landed(stage)
                pltpu.make_async_copy(area, area, rs_send.at[self.number, stage]).wait()

    def advance(steps):
        copies = [steps[0][0].fetch(steps[0][1], 0)]
        for k, (strip, stage) in enumerate(steps):
            if k + 1 < len(steps):
                copies.append(steps[k + 1][0].fetch(steps[k + 1][1], (k + 1) % 2))
            copies[k].wait()
            strip.fold(stage, k % 2)
            if stage < 3:
                strip.start(stage + 1)

    def wave(strips, stage):
        return [(strip, stage) for strip in strips]

    orders = ((1, 2, 4, 8), (2, 4, 1, 8), (4, 1, 2, 8))
    spatial_strips = [
        Strip(C3, 48 * p, 144, 48, RB_S.at[p], STG, orders[p], p) for p in range(3)
    ]
    reduce_strips = [
        Strip(C3, SPATIAL_HALF + 24 * p, 64, depth, RB_R.at[p], STG, orders[p], 3 + p)
        for p, depth in enumerate((24, 24, 16))
    ]
    expand_strips = [
        Strip(RC_E, base, 16, depth, RB_E.at[p], STG, orders[p % 3], 6 + p)
        for p, (base, depth) in enumerate(((0, 16), (256, 16), (512, 16), (768, 8), (776, 8)))
    ]
    proto_strips = [
        Strip(RC_P, 32 * p, 96, 32, RB_P.at[p], STGP, orders[p], 11 + p) for p in range(3)
    ]

    def gathered_block(order, stage, j):
        index = 0
        for t, bit in enumerate(order):
            if t < stage:
                index = index + bit * ((j >> t) & 1)
            else:
                index = index + bit * place[bit]
        return index

    def gather_start(ref, base, stride, depth, columns, order, stage, number, which=None):
        for j in which or range(1 << stage):
            start = pl.multiple_of(base + gathered_block(order, stage, j) * stride, 16)
            area = ref.at[pl.ds(start, depth), columns]
            pltpu.make_async_remote_copy(
                area,
                area,
                gather_send.at[number, stage],
                gather_recv.at[number, stage],
                device_id=partner(order[stage]),
                device_id_type=MESH,
            ).start()

    def gather_wait(ref, depth, columns, stage, number, sems):
        area = ref.at[pl.ds(0, depth << stage), columns]
        pltpu.make_async_copy(area, area, sems.at[number, stage]).wait()

    pooled_parts = (
        (slice(0, 640), (8, 4, 1, 2)),
        (slice(640, 1280), (8, 1, 2, 4)),
        (slice(1280, 2048), (8, 2, 4, 1)),
    )

    def by_size(action):
        @pl.when(big)
        def _():
            action(2 * IMAGES)

        @pl.when(jnp.logical_not(big))
        def _():
            action(SLOTS)

    def pooled_gather(stage, parts=(0, 1, 2), which=None):
        def action(depth):
            for number in parts:
                columns, order = pooled_parts[number]
                gather_start(PG, 0, depth, depth, columns, order, stage, number, which)

        by_size(action)

    def pooled_arrived(stage):
        def action(depth):
            for number, (columns, order) in enumerate(pooled_parts):
                gather_wait(PG, depth, columns, stage, number, gather_recv)

        by_size(action)

    def core_copy(source, target, sent, landed):
        return pltpu.make_async_remote_copy(
            source,
            target,
            core_send.at[sent],
            core_recv.at[landed],
            device_id=(1 - r, d),
            device_id_type=MESH,
        )

    def half_tile(index):
        return pl.ds(pl.multiple_of(index * 256, 256), 256)

    def local_moments(values, rows, first_lane, weight, own, x):
        for q in range(4):
            v = values[rows, first_lane + q * LANES : first_lane + (q + 1) * LANES]
            w = weight[...]
            total = jnp.sum(v * w, axis=0, keepdims=True)
            centred = (v - total / own) * w
            MSG[x, q : q + 1, :] = total
            MSG[x, 4 + q : 5 + q, :] = jnp.sum(centred * centred, axis=0, keepdims=True)

    def whole_moments(x, counts, prm, first):
        whole = jnp.sum(counts, axis=0, keepdims=True)
        each = counts[:, None, :]
        sums = RECV[x, :, 0:4, :]
        spreads = RECV[x, :, 4:8, :]
        mean = jnp.sum(sums, axis=0) / whole
        off = sums / each - mean[None]
        var = jnp.sum(spreads + each * off * off, axis=0) / whole
        scale = lax.rsqrt(var + EPS_NORM)
        for q in range(4):
            prm[first + q, 0:1, :] = mean[q : q + 1]
            prm[first + q, 1:2, :] = scale[q : q + 1]

    def whole_back(x, whole, prm, first, place):
        ones = jnp.sum(RECV[x, :, 0:4, :], axis=0)
        twos = jnp.sum(RECV[x, :, 4:8, :], axis=0)
        for q in range(4):
            prm[first + q, 4:5, :] = ones[q : q + 1] / whole
            prm[first + q, 5:6, :] = twos[q : q + 1] / whole
        FAR[0, pl.ds(place, 4), :] = twos
        FAR[0, pl.ds(48 + place, 4), :] = ones

    def norm_terms(v, prm, index):
        centred = (v - prm[index, 0:1, :]) * prm[index, 1:2, :]
        return centred, centred * prm[index, 2:3, :] + prm[index, 3:4, :]

    def back_through(du, centred, weight, prm, index):
        inner = du - weight * (prm[index, 4:5, :] + centred * prm[index, 5:6, :])
        return prm[index, 2:3, :] * prm[index, 1:2, :] * inner

    def spread_taps(sign):
        def for_side(side):
            @pl.loop(0, ROWS // STRIPE)
            def _(s):
                base = pl.multiple_of(s * STRIPE, STRIPE)
                rows = pl.ds(base, STRIPE)
                window = pl.ds(base, STRIPE + 2 * EDGE)
                line_ids = jnp.floor(GRID[rows, :] * 0.125)
                column_ids = GRID[rows, :] - line_ids * 8.0
                for tap in range(9):
                    dy, dx = sign * (tap // 3 - 1), sign * (tap % 3 - 1)
                    y = line_ids + float(dy)
                    x = column_ids + float(dx)
                    keep = (y >= 0.0) & (y < float(side)) & (x >= 0.0) & (x < float(side))
                    start = EDGE + dy * side + dx
                    for q in range(4):
                        moved = APAD[window, lanes(q)][start : start + STRIPE]
                        COLS[rows, tap * WIDTH + q * LANES : tap * WIDTH + (q + 1) * LANES] = (
                            jnp.where(keep, moved, 0.0).astype(BF)
                        )

        @pl.when(big)
        def _():
            for_side(LSIDE)

        @pl.when(jnp.logical_not(big))
        def _():
            for_side(SSIDE)

    loads[0].wait()
    loads[1].wait()
    for load in loads[2:]:
        load.start()
    for k in range(2):
        hidden_load(k, k).start()
    C1[...] = mm(F[...], WR[...])
    every = pl.ds(0, ROWS)
    local_moments(C1, every, 0, RW, own_rows, X_ONE)
    pl.semaphore_wait(barrier, GROUP)
    announce(X_ONE)
    announce(X_COUNT)
    collect(X_COUNT)
    row_counts = RECV[X_COUNT, :, 0, :]
    crop_counts = row_counts * area_inv
    whole_rows = jnp.sum(row_counts, axis=0, keepdims=True)
    whole_crops = jnp.sum(crop_counts, axis=0, keepdims=True)
    collect(X_ONE)
    whole_moments(X_ONE, row_counts, PRM1, 0)
    for q in range(4):
        _, before = norm_terms(C1[:, lanes(q)], PRM1, q)
        act = gelu(before)
        APAD[EDGE : EDGE + ROWS, lanes(q)] = act
        A1T[lanes(q), :] = act.astype(BF).T
    spread_taps(1)
    loads[2].wait()

    @pl.loop(0, 2)
    def _(h):
        C2[:, lanes(h, 256)] = mm(COLS[...], WS[:, lanes(h, 256)])

    local_moments(C2, every, 0, RW, own_rows, X_TWO)
    announce(X_TWO)
    collect(X_TWO)
    whole_moments(X_TWO, row_counts, PRM2, 0)
    for q in range(4):
        _, before = norm_terms(C2[:, lanes(q)], PRM2, q)
        A2[:, lanes(q)] = gelu(before).astype(BF)
    loads[3].wait()

    @pl.loop(0, 4)
    def _(j):
        rows = at(j * ROWS, ROWS)
        C3[rows, :] = mm(A2[...], WE[:, lanes(j, WIDTH)])
        local_moments(C3, rows, 0, RW, own_rows, X_THREE + j)
        announce(X_THREE + j)

    @pl.loop(0, 4)
    def _(j):
        collect(X_THREE + j)
        whole_moments(X_THREE + j, row_counts, PRM3, 4 * j)
        rows = at(j * ROWS, ROWS)
        for q in range(4):
            _, before = norm_terms(C3[rows, lanes(q)], PRM3, 4 * j + q)
            joined = before + F[:, lanes(4 * j + q)].astype(F32)
            high, low = two_parts(gelu(joined))
            pooled = (mm(P[...], high) + mm(P[...], low)) * area_inv
            pooled_low = pooled.astype(BF)
            PO[:, lanes(4 * j + q)] = pooled_low
            DA4[j, :, lanes(q)] = pooled_low.astype(F32) * CW[...]

    def keep_pooled(depth):
        own = PG.at[pl.ds(pl.multiple_of(d * depth, 16), depth), :]
        for j in range(4):
            pltpu.make_async_copy(
                DA4.at[j, pl.ds(0, depth), :], own.at[:, lanes(j, WIDTH)], row_sem.at[0]
            ).start()
        pltpu.make_async_copy(own, own, row_sem.at[0]).wait()

    by_size(keep_pooled)

    @pl.loop(0, 4)
    def _(j):
        for half in range(2):
            k = 2 * j + half
            hidden_load(k, half).wait()
            H1[j, :, half * 256 : half * 256 + 256] = mm(PO[...], WHB[half])
            hidden_load(lax.rem(k + 2, 8), half).start()
        local_moments(H1.at[j], pl.ds(0, SLOTS), 0, CW, own_crops, X_FOUR + j)
        announce(X_FOUR + j)

    pooled_gather(0, (0,))
    loads[5].wait()
    loads[6].wait()
    TAB[0:PROTOS, :] = PROWS[...].astype(F32)
    TAB[PROTOS:, :] = jnp.zeros((PADDED - PROTOS, FEATS), F32)
    PR[...] = TAB[...].astype(BF)

    @pl.loop(0, 4)
    def _(j):
        collect(X_FOUR + j)
        whole_moments(X_FOUR + j, crop_counts, PRM4, 4 * j)
        for q in range(4):
            _, before = norm_terms(H1[j, :, lanes(q)], PRM4, 4 * j + q)
            A4[:, lanes(4 * j + q)] = gelu(before).astype(BF)

    head_two = mm(A4[...], WP[...]) + shift[40:41, :]
    length_inv = lax.rsqrt(jnp.sum(head_two * head_two, axis=1, keepdims=True) + EPS_UNIT)
    unit = head_two * length_inv
    unit_low = unit.astype(BF)
    UOWN[...] = unit_low[0 : 2 * IMAGES].astype(F32)
    UL[...] = unit_low

    def unit_copy(peer):
        return pltpu.make_async_remote_copy(
            UOWN,
            UNITS.at[d],
            unit_sem.at[0],
            unit_sem.at[1],
            device_id=(r, peer),
            device_id_type=MESH,
        )

    forward_units = pltpu.make_async_remote_copy(
        UNITS, UNITS, unit_sem.at[2], unit_sem.at[3], device_id=(1 - r, d), device_id_type=MESH
    )

    @pl.when(big)
    def _():
        for peer in peers:
            unit_copy(peer).start()

        UNITS[d] = UOWN[...]

    pooled_gather(0, (1, 2))

    @pl.when(big)
    def _():
        others = UNITS.at[pl.ds(0, GROUP - 1)]
        pltpu.make_async_copy(others, others, unit_sem.at[1]).wait()
        pltpu.make_async_copy(others, others, unit_sem.at[0]).wait()
        forward_units.start()

    @pl.when(jnp.logical_not(big))
    def _():
        forward_units.wait_recv()

    chunk = 512
    chunks = PADDED // chunk
    images = GROUP * IMAGES
    chunk_lane = lax.broadcasted_iota(jnp.int32, (1, chunk), 1)

    @pl.loop(0, 2)
    def _(v):
        view = UNITS[:, pl.ds(pl.multiple_of(v * IMAGES, IMAGES), IMAGES), :]
        view = view.reshape(images, FEATS).astype(BF)

        def sweep(first):
            RACC[...] = jnp.zeros_like(RACC)

            @pl.loop(0, chunks)
            def _(c):
                valid = (chunk_lane + c * chunk) < PROTOS
                if first:
                    raised = jnp.exp(mm_t(view, PR[at(c * chunk, chunk), :]) / SHARPNESS)
                for q in range(chunk // LANES):
                    tile = pl.ds(pl.multiple_of(c * chunk + q * LANES, LANES), images)
                    if first:
                        table = raised[:, lanes(q)]
                    else:
                        table = TAB[tile, :] * RINV[...]
                    total = jnp.sum(table, axis=0, keepdims=True)
                    table = table * jnp.where(valid[:, lanes(q)], 1.0 / total, 0.0)
                    TAB[tile, :] = table
                    RACC[...] += table

            RINV[...] = jnp.broadcast_to(
                1.0 / jnp.sum(RACC[...], axis=1, keepdims=True), (images, LANES)
            )

        for number in range(SINK):
            sweep(number == 0)
        row_inv = RINV[pl.ds(pl.multiple_of(d * IMAGES, IMAGES), IMAGES), :]
        for c in range(PADDED // LANES):
            own = pl.ds(pl.multiple_of(c * LANES + d * IMAGES, IMAGES), IMAGES)
            Q[pl.ds(pl.multiple_of(v * IMAGES, IMAGES), IMAGES), lanes(c)] = TAB[own, :] * row_inv

    ident_f = jnp.sum(eye * crop_ids.astype(F32), axis=1, keepdims=True)
    pick_lane = lax.broadcasted_iota(jnp.int32, (SLOTS, 2 * IMAGES), 1)
    pick_row = lax.broadcasted_iota(jnp.int32, (SLOTS, 2 * IMAGES), 0)
    image_lane = jnp.where(pick_lane < IMAGES, pick_lane, pick_lane - IMAGES)
    first_image = (d * IMAGES).astype(F32)
    crossed = (pick_row < 2 * IMAGES) & (jnp.abs(pick_row - pick_lane) == IMAGES)
    matched = ident_f == image_lane.astype(F32) + first_image
    picked = jnp.where(big, crossed.astype(F32), matched.astype(F32))
    image_weight = 1.0 / (2.0 * (1.0 + count_row[...].astype(F32)))
    picked = picked * jnp.concatenate([image_weight, image_weight], axis=1)
    valid_all = lax.broadcasted_iota(jnp.int32, (1, PADDED), 1) < PROTOS
    loss_rows = []
    for s in range(4):
        rows = slice(16 * s, 16 * s + 16)
        target = jnp.dot(picked[rows], Q[...], precision=HIGH, preferred_element_type=F32)
        logit = jnp.where(valid_all, mm_t(UL[rows, :], PR[...]) / SOFTMAX_HEAT, -1e30)
        shifted = logit - jnp.max(logit, axis=1, keepdims=True)
        raised = jnp.exp(shifted)
        total = jnp.sum(raised, axis=1, keepdims=True)
        loss_rows.append(jnp.sum(target * (shifted - jnp.log(total)), axis=1, keepdims=True))
        mass = jnp.sum(target, axis=1, keepdims=True)
        DS[rows, :] = ((raised * (mass / total) - target) / SOFTMAX_HEAT).astype(BF)
    loss_local = -jnp.sum(
        loss_rows[0] + loss_rows[1] + loss_rows[2] + loss_rows[3], axis=0, keepdims=True
    )

    def proto_half(which):
        return t_mm(DS[:, pl.ds(pl.multiple_of(which * PROTO_HALF, LANES), PROTO_HALF)], UL[...])

    unit_grad = mm(DS[...], PR[...])
    along = jnp.sum(unit * unit_grad, axis=1, keepdims=True)
    head_two_grad = (unit_grad - unit * along) * length_inv
    bias_grad = jnp.sum(head_two_grad, axis=0, keepdims=True)
    head_two_low = head_two_grad.astype(BF)

    @pl.loop(0, 4)
    def _(j):
        DA4[j] = mm_t(head_two_low, WP[at(j * WIDTH, WIDTH), :])
        for q in range(4):
            centred, before = norm_terms(H1[j, :, lanes(q)], PRM4, 4 * j + q)
            du = DA4[j, :, lanes(q)] * gelu_slope(before) * CW[...]
            DA4[j, :, lanes(q)] = du
            MSG[X_FOUR_BACK + j, q : q + 1, :] = jnp.sum(du, axis=0, keepdims=True)
            MSG[X_FOUR_BACK + j, 4 + q : 5 + q, :] = jnp.sum(du * centred, axis=0, keepdims=True)
        announce(X_FOUR_BACK + j)

    D2F[...] = head_two_low.astype(F32)

    def share_rows(depth):
        own = pl.ds(pl.multiple_of(d * depth, 16), depth)

        @pl.loop(1, GROUP)
        def _(k):
            pltpu.make_async_remote_copy(
                D2F.at[pl.ds(0, depth), :],
                D2A.at[own, :],
                row_sem.at[1],
                row_sem.at[2],
                device_id=(r, lax.rem(d + k, GROUP)),
                device_id_type=MESH,
            ).start()

        D2A[own, :] = D2F[0:depth, :]

    by_size(share_rows)
    MSG[X_EXTRA] = jnp.concatenate(
        [bias_grad, jnp.broadcast_to(loss_local, (1, LANES)), jnp.zeros((6, LANES), F32)], axis=0
    )
    announce(X_EXTRA)
    OUT_P[...] = proto_half(1 - r)
    proto_swap = core_copy(OUT_P, RC_P, 4, 17)
    proto_swap.start()
    pooled_arrived(0)
    pooled_gather(1)

    @pl.loop(0, 4)
    def _(j):
        collect(X_FOUR_BACK + j)
        whole_back(X_FOUR_BACK + j, whole_crops, PRM4, 4 * j, 24 + 4 * j)
        for q in range(4):
            centred, _ = norm_terms(H1[j, :, lanes(q)], PRM4, 4 * j + q)
            DH1[:, lanes(4 * j + q)] = back_through(
                DA4[j, :, lanes(q)], centred, CW[...], PRM4, 4 * j + q
            ).astype(BF)

    pooled_arrived(1)
    pooled_gather(2)
    DP = H1
    for j in range(4):
        DP[j] = jnp.zeros((SLOTS, WIDTH), F32)

    @pl.loop(0, 4)
    def _(i):
        for half in range(2):
            k = 2 * i + half
            hidden_load(k, half).wait()
            back = mm_t(DH1[:, lanes(k, 256)], WHB[half])
            for j in range(4):
                DP[j] += back[:, lanes(j, WIDTH)]

            @pl.when(k + 2 < 8)
            def _():
                hidden_load(k + 2, half).start()

    @pl.loop(0, 4)
    def _(j):
        rows = at(j * ROWS, ROWS)
        for q in range(4):
            high, low = two_parts(DP[j, :, lanes(q)] * area_inv)
            out_grad = mm(PT[...], high) + mm(PT[...], low)
            centred, before = norm_terms(C3[rows, lanes(q)], PRM3, 4 * j + q)
            joined = before + F[:, lanes(4 * j + q)].astype(F32)
            du = out_grad * gelu_slope(joined)
            DJ[rows, lanes(q)] = du
            MSG[X_THREE_BACK + j, q : q + 1, :] = jnp.sum(du, axis=0, keepdims=True)
            MSG[X_THREE_BACK + j, 4 + q : 5 + q, :] = jnp.sum(du * centred, axis=0, keepdims=True)
        announce(X_THREE_BACK + j)

    pooled_arrived(2)
    pooled_gather(3, which=range(4))
    proto_own = proto_half(r)
    proto_swap.wait_recv()
    RC_P[...] += proto_own
    for strip in proto_strips:
        strip.start(0)

    @pl.loop(0, 4)
    def _(j):
        collect(X_THREE_BACK + j)
        whole_back(X_THREE_BACK + j, whole_rows, PRM3, 4 * j, 8 + 4 * j)
        rows = at(j * ROWS, ROWS)
        for q in range(4):
            centred, _ = norm_terms(C3[rows, lanes(q)], PRM3, 4 * j + q)
            COLS[:, lanes(4 * j + q)] = back_through(
                DJ[rows, lanes(q)], centred, RW[...], PRM3, 4 * j + q
            ).astype(BF)

    pl.semaphore_signal(free_sem, inc=1, device_id=(1 - r, d), device_id_type=MESH)
    centre = pl.ds(EDGE, ROWS)

    @pl.loop(0, 2)
    def _(h):
        APAD[centre, lanes(h, 256)] = mm_t(COLS[:, 0:DEPTH], WE[at(h * 256, 256), :])

    def through_gelu(values, prm, x):
        for q in range(4):
            centred, before = norm_terms(values[:, lanes(q)], prm, q)
            du = APAD[centre, lanes(q)] * gelu_slope(before) * RW[...]
            APAD[centre, lanes(q)] = du
            MSG[x, q : q + 1, :] = jnp.sum(du, axis=0, keepdims=True)
            MSG[x, 4 + q : 5 + q, :] = jnp.sum(du * centred, axis=0, keepdims=True)
        announce(x)

    through_gelu(C2, PRM2, X_TWO_BACK)

    @pl.loop(0, 4)
    def _(j):
        OUT[half_tile(j), :] = t_mm(A2[:, half_tile(1 - r)], COLS[:, lanes(j, WIDTH)])
        core_copy(OUT.at[half_tile(j), :], RC_E.at[half_tile(j), :], j, j).start()

    @pl.loop(0, 4)
    def _(j):
        own = t_mm(A2[:, half_tile(r)], COLS[:, lanes(j, WIDTH)])
        tile = RC_E.at[half_tile(j), :]
        core_copy(tile, tile, j, j).wait_recv()
        tile[...] += own

    for strip in expand_strips:
        strip.start(0)
    advance(wave(proto_strips, 0))
    collect(X_TWO_BACK)
    whole_back(X_TWO_BACK, whole_rows, PRM2, 0, 4)
    for q in range(4):
        centred, _ = norm_terms(C2[:, lanes(q)], PRM2, q)
        APAD[centre, lanes(q)] = back_through(APAD[centre, lanes(q)], centred, RW[...], PRM2, q)
    spread_taps(-1)

    @pl.loop(0, 2)
    def _(h):
        total = mm_t(COLS[:, 0:WIDTH], WS[at(h * 256, 256), :])
        for tap in range(1, 9):
            total += mm_t(
                COLS[:, tap * WIDTH : (tap + 1) * WIDTH], WS[at(tap * WIDTH + h * 256, 256), :]
            )
        APAD[centre, lanes(h, 256)] = total

    through_gelu(C1, PRM1, X_ONE_BACK)

    pooled_gather(3, which=range(4, 8))
    advance(wave(expand_strips, 0))
    advance(wave(proto_strips, 1))

    def half_tap(which, m):
        g = 9 * which + m
        return mm(A1T[half_tile(lax.rem(g, 2)), :], COLS[:, lanes(g // 2, WIDTH)])

    pl.semaphore_wait(free_sem, 1)

    def ring(slot):
        tile = OUT.at[half_tile(slot), :]
        return tile, core_copy(tile, tile, slot, 0)

    def add_half_tap(m):
        own = half_tap(r, m)
        tile = C3.at[half_tile(m), :]
        core_copy(tile, tile, 0, 4 + m).wait_recv()
        tile[...] += own

    @pl.loop(0, 9)
    def _(m):
        slot = lax.rem(m, 4)
        tile, last = ring(slot)
        last.wait_send()
        tile[...] = half_tap(1 - r, m)
        core_copy(tile, C3.at[half_tile(m), :], slot, 4 + m).start()

        @pl.when(m >= 2)
        def _():
            add_half_tap(m - 2)

    add_half_tap(7)
    add_half_tap(8)
    for strip in spatial_strips:
        strip.start(0)

    collect(X_ONE_BACK)
    whole_back(X_ONE_BACK, whole_rows, PRM1, 0, 0)
    for q in range(4):
        centred, _ = norm_terms(C1[:, lanes(q)], PRM1, q)
        A2[:, lanes(q)] = back_through(APAD[centre, lanes(q)], centred, RW[...], PRM1, q).astype(BF)

    def reduce_tile(which, j):
        columns = pl.ds(pl.multiple_of(which * 1024 + j * 256, 256), 256)
        return t_mm(F[:, columns], A2[...])

    def reduce_rows(j):
        return C3.at[pl.ds(pl.multiple_of(SPATIAL_HALF + j * 256, 256), 256), :]

    @pl.loop(0, 4)
    def _(j):
        slot = lax.rem(j + 1, 4)
        tile, last = ring(slot)
        last.wait_send()
        tile[...] = reduce_tile(1 - r, j)
        core_copy(tile, reduce_rows(j), slot, 13 + j).start()

    @pl.loop(0, 4)
    def _(j):
        own = reduce_tile(r, j)
        tile = reduce_rows(j)
        core_copy(tile, tile, 0, 13 + j).wait_recv()
        tile[...] += own

    for strip in reduce_strips:
        strip.start(0)
    collect(X_EXTRA)
    extra = jnp.sum(RECV[X_EXTRA], axis=0)
    FAR[0, 88:96, :] = extra
    far = pltpu.make_async_remote_copy(
        FAR.at[0],
        FAR.at[1],
        far_sem.at[0],
        far_sem.at[1],
        device_id=(1 - r, d),
        device_id_type=MESH,
    )
    far.start()

    @pl.loop(0, 4)
    def _(j):
        rows = at(j * ROWS, ROWS)
        grad = mm_t(A2[...], WR[at(j * WIDTH, WIDTH), :])
        for q in range(4):
            DJ[rows, lanes(q)] = (DJ[rows, lanes(q)] + grad[:, lanes(q)]) * RW[...]
        pltpu.make_async_copy(
            DJ.at[rows, :], feature_out.at[0, :, lanes(j, WIDTH)], out_sem.at[0]
        ).start()

    advance(wave(proto_strips, 2))
    advance(wave(expand_strips, 1))
    HACC = HB.at[pl.ds(0, DEPTH), :]
    HREC = HB.at[pl.ds(DEPTH, 1024), :]

    unit_rows = pl.ds(pl.multiple_of(d * LANES, LANES), LANES)

    def hidden_gradient(depth):
        pooled_arrived(3)
        others = D2A.at[pl.ds(0, (GROUP - 1) * depth), :]
        pltpu.make_async_copy(others, others, row_sem.at[2]).wait()
        pltpu.make_async_copy(others, others, row_sem.at[1]).wait()
        total = GROUP * depth
        pieces = [(c, j) for c in range(total // 256) for j in range(4)]

        def load(k):
            c, j = pieces[k]
            return pltpu.make_async_copy(
                PG.at[pl.ds(256 * c, 256), lanes(j, WIDTH)],
                STG.at[k % 2, pl.ds(0, 256), :],
                stage_sem.at[k % 2],
            )

        load(0).start()
        for k, (c, j) in enumerate(pieces):
            if k + 1 < len(pieces):
                load(k + 1).start()
            load(k).wait()
            COLS[
                256 * (c % 2) : 256 * (c % 2) + 256,
                DEPTH * (c // 2) + WIDTH * j : DEPTH * (c // 2) + WIDTH * j + WIDTH,
            ] = STG[k % 2, 0:256, :].astype(BF)
        for part in range((total + 511) // 512):
            count = min(512, total)
            pooled_all = COLS[0:count, DEPTH * part : DEPTH * part + DEPTH]
            head = mm(pooled_all, WHC[...])
            centred, earlier = norm_terms(head, PRM4, d)
            low_rows = D2A[512 * part : 512 * part + count, :].astype(BF)
            du = mm_t(low_rows, WP[unit_rows, :]) * gelu_slope(earlier)
            dh = back_through(du, centred, 1.0, PRM4, d).astype(BF)
            act = gelu(earlier).astype(BF)
            if part == 0:
                PACC[...] = t_mm(act, low_rows)
            else:
                PACC[...] += t_mm(act, low_rows)
            for j in range(4):
                columns = slice(DEPTH * part + WIDTH * j, DEPTH * part + WIDTH * j + WIDTH)
                rows = slice(WIDTH * j, WIDTH * j + WIDTH)
                if part == 0:
                    HACC[rows, :] = t_mm(COLS[0:count, columns], dh)
                else:
                    HACC[rows, :] += t_mm(COLS[0:count, columns], dh)

    loads[4].wait()
    by_size(hidden_gradient)

    def hidden_half(which):
        return HB.at[pl.ds(pl.multiple_of(which * 1024, 1024), 1024), :]

    hidden_swap = core_copy(hidden_half(1 - r), HREC, 5, 18)
    hidden_swap.start()
    project_swap = core_copy(PACC, PREC, 6, 19)
    project_swap.start()
    advance(wave(spatial_strips, 0))
    advance(wave(expand_strips, 2))
    hidden_swap.wait_recv()
    hidden_half(r)[...] += HREC[...]

    @pl.loop(1, GROUP)
    def _(k):
        to = lax.rem(d + k, GROUP)
        pltpu.make_async_remote_copy(
            HB.at[pl.ds(pl.multiple_of(r * 1024 + to * 64, 64), 64), :],
            HAL.at[d],
            row_sem.at[3],
            row_sem.at[4],
            device_id=(r, to),
            device_id_type=MESH,
        ).start()

    HAL[d] = HB[pl.ds(pl.multiple_of(r * 1024 + d * 64, 64), 64), :]

    project_swap.wait()
    PACC[...] = jnp.where(big, PACC[...], PREC[...]) + jnp.where(big, PREC[...], PACC[...])
    serves = (d // 8) == r
    first_owner = lax.rem(2 * d, GROUP)
    for half in range(2):
        owner = first_owner + half
        part = PACC.at[pl.ds(64 * half, 64), :]
        local = owner == d

        @pl.when(serves & jnp.logical_not(local))
        def _():
            pltpu.make_async_remote_copy(
                part, PIN, core_send.at[7 + half], row_sem.at[5],
                device_id=(r, owner), device_id_type=MESH,
            ).start()

        @pl.when(serves & local)
        def _():
            PIN[...] = part[...]

    chip_of_own = (r * GROUP + d) // 2
    from_self = chip_of_own == d

    advance(wave(reduce_strips, 0))
    advance(wave(proto_strips, 3))
    proto_own_rows = pl.ds(pl.multiple_of(r * PROTO_HALF + d * 96, 16), 96)
    TAB[proto_own_rows, :] = RC_P[pl.ds(pl.multiple_of(d * 96, 16), 96), :]
    proto_orders = ((8, 4, 1, 2), (8, 1, 2, 4), (8, 2, 4, 1))
    every_lane = slice(0, LANES)

    def proto_gather(stage):
        for p, order in enumerate(proto_orders):
            gather_start(
                TAB, r * PROTO_HALF + 32 * p, 96, 32, every_lane, order, stage, 3 + p
            )

    def proto_wait(stage, sems):
        for p in range(3):
            gather_wait(TAB, 32, every_lane, stage, 3 + p, sems)

    def proto_arrived(stage):
        proto_wait(stage, gather_recv)

    proto_gather(0)
    advance(wave(spatial_strips, 1))
    proto_arrived(0)
    proto_gather(1)
    advance(wave(reduce_strips, 1))
    advance(wave(expand_strips, 3))
    proto_arrived(1)
    proto_gather(2)
    advance(wave(spatial_strips, 2))
    proto_arrived(2)
    proto_gather(3)
    advance(wave(reduce_strips, 2))
    for j in range(4):
        for q in range(4):
            expand_out[pl.ds(4 * j + q, 16, stride=16), :] = RC_E[
                pl.ds(pl.multiple_of(256 * j + d * 16, 16), 16), lanes(q)
            ]
    proto_arrived(3)
    proto_part = TAB.at[pl.ds(pl.multiple_of(r * PROTO_HALF, LANES), PROTO_HALF), :]
    proto_far = core_copy(proto_part, proto_part, 9, 20)
    proto_far.start()
    far.wait()
    both = jnp.where(big, FAR[0], FAR[1]) + jnp.where(big, FAR[1], FAR[0])
    gain_out[...] = both[0:40]
    shift_out[0:40, :] = both[48:88]
    shift_out[40:41, :] = both[88:89]
    loss_out[...] = both[89:90, 0:1] / float(GROUP * IMAGES)
    arrived = HAL.at[pl.ds(0, GROUP - 1)]
    pltpu.make_async_copy(arrived, arrived, row_sem.at[4]).wait()
    pltpu.make_async_copy(arrived, arrived, row_sem.at[3]).wait()
    for source in range(GROUP):
        hidden_out[pl.ds(source, 64, stride=16), :] = HAL[source]

    @pl.when(jnp.logical_not(from_self))
    def _():
        pltpu.make_async_copy(PIN, PIN, row_sem.at[5]).wait()

    project_out[...] = PIN[...]
    for half in range(2):

        @pl.when(serves & jnp.logical_not(first_owner + half == d))
        def _():
            pltpu.make_async_copy(PIN, PIN, core_send.at[7 + half]).wait()

    proto_far.wait()
    hidden_swap.wait_send()
    for stage in range(4):
        proto_wait(stage, gather_send)
    for c in range(PADDED // LANES):
        TAB[c * LANES : c * LANES + LANES, :] = TAB[c * LANES : c * LANES + LANES, :].T
    lane_row = lax.broadcasted_iota(jnp.int32, (8, LANES), 1)
    carry = jnp.zeros((8, LANES), F32)
    for b in range(16):
        offset = (PROTOS * b) % LANES
        first = (PROTOS * b) // LANES
        whole = (offset + PROTOS) // LANES
        for t in range(whole + 1):
            if t < PADDED // LANES:
                tile = TAB[pl.ds(LANES * t + b, 8, stride=16), :]
                turned = pltpu.roll(tile, offset, 1) if offset else tile
            else:
                turned = jnp.zeros((8, LANES), F32)
            line = jnp.where(lane_row < offset, carry, turned) if offset else turned
            if t < whole:
                HB[pl.ds(first + t, 8, stride=375), :] = line
                carry = turned
            else:
                carry = line
    flat_copy = pltpu.make_async_copy(HB.at[pl.ds(0, PROTOS), :], proto_out, out_sem.at[2])
    flat_copy.start()
    advance(wave(spatial_strips, 3))
    for q in range(4):
        spatial_out[pl.ds(q, 144, stride=4), :] = C3[
            pl.ds(pl.multiple_of(d * 144, 16), 144), lanes(q)
        ]
    advance(wave(reduce_strips, 3))
    for q in range(4):
        reduce_out[pl.ds(q, 64, stride=4), :] = C3[
            pl.ds(pl.multiple_of(SPATIAL_HALF + d * 64, 16), 64), lanes(q)
        ]


    @pl.when(big)
    def _():
        forward_units.wait_send()

    proto_swap.wait_send()
    for stage in range(4):

        def pooled_sent(depth):
            for number, (columns, _) in enumerate(pooled_parts):
                gather_wait(PG, depth, columns, stage, number, gather_send)

        by_size(pooled_sent)
    for strip in spatial_strips + reduce_strips + expand_strips + proto_strips:
        strip.close()
    flat_copy.wait()
    for slot in range(4):
        ring(slot)[1].wait_send()
    pltpu.make_async_copy(feature_out.at[0], feature_out.at[0], out_sem.at[0]).wait()


def tower(
    features,
    crop_counts,
    crop_image,
    w_reduce,
    w_spatial,
    w_expand,
    w_hidden,
    w_project,
    prototypes,
    norm_gain,
    norm_shift,
):
    anywhere = pl.BlockSpec(memory_space=pl.ANY)
    inside = pl.BlockSpec(memory_space=pltpu.VMEM)
    in_hbm = pl.BlockSpec(memory_space=pltpu.HBM)

    def vm(*shape, dtype=F32):
        return pltpu.VMEM(shape, dtype)

    dma = pltpu.SemaphoreType.DMA

    def shaped(*shape):
        return jax.ShapeDtypeStruct(shape, F32)

    return pl.pallas_call(
        tower_kernel,
        out_shape=(
            shaped(1, 1),
            shaped(1, ROWS, DEPTH),
            shaped(256, LANES),
            shaped(576, LANES),
            shaped(256, LANES),
            shaped(1024, LANES),
            shaped(64, LANES),
            shaped(PROTOS, FEATS),
            shaped(40, LANES),
            shaped(41, LANES),
            shaped(GROUP * SLOTS, DEPTH),
            shaped(3, 15 * 48, WIDTH),
            shaped(3, 15 * 24, WIDTH),
            shaped(5, 15 * 16, WIDTH),
            shaped(3, 15 * 32, LANES),
        ),
        in_specs=[anywhere, inside, inside] + [anywhere] * 6 + [inside, inside],
        out_specs=(
            (inside, anywhere) + (inside,) * 5 + (anywhere, inside, inside) + (in_hbm,) * 5
        ),
        scratch_shapes=[
            vm(ROWS, DEPTH, dtype=BF),
            vm(DEPTH, WIDTH, dtype=BF),
            vm(9 * WIDTH, WIDTH, dtype=BF),
            vm(WIDTH, DEPTH, dtype=BF),
            vm(2, DEPTH, 256, dtype=BF),
            vm(DEPTH, LANES, dtype=BF),
            vm(HIDDEN, FEATS, dtype=BF),
            vm(PROTOS, FEATS, dtype=BF),
            vm(PADDED, FEATS, dtype=BF),
            vm(ROWS, WIDTH),
            vm(ROWS, WIDTH),
            vm(SPATIAL_HALF + 1024, WIDTH),
            vm(4 * ROWS, WIDTH),
            vm(ROWS + 2 * EDGE, WIDTH),
            vm(ROWS, 9 * WIDTH, dtype=BF),
            vm(ROWS, WIDTH, dtype=BF),
            vm(WIDTH, ROWS, dtype=BF),
            vm(SLOTS, DEPTH, dtype=BF),
            vm(4, SLOTS, WIDTH),
            vm(SLOTS, HIDDEN, dtype=BF),
            vm(4, SLOTS, WIDTH),
            vm(SLOTS, HIDDEN, dtype=BF),
            vm(SLOTS, PADDED, dtype=BF),
            vm(SLOTS, FEATS, dtype=BF),
            vm(SLOTS, FEATS),
            vm(GROUP * SLOTS, FEATS),
            vm(PADDED, GROUP * IMAGES),
            vm(2 * IMAGES, PADDED),
            vm(GROUP * IMAGES, LANES),
            vm(GROUP * IMAGES, LANES),
            vm(GROUP, 2 * IMAGES, FEATS),
            vm(2 * IMAGES, FEATS),
            vm(ROWS, LANES),
            vm(SLOTS, LANES),
            vm(ROWS, LANES),
            vm(ROWS, SLOTS, dtype=BF),
            vm(SLOTS, ROWS, dtype=BF),
            vm(4, 8, LANES),
            vm(4, 8, LANES),
            vm(16, 8, LANES),
            vm(16, 8, LANES),
            vm(EXCHANGES, 8, LANES),
            vm(EXCHANGES, GROUP, 8, LANES),
            vm(2, 96, LANES),
            vm(1024, WIDTH),
            vm(1024, WIDTH),
            vm(PROTO_HALF, LANES),
            vm(PROTO_HALF, LANES),
            vm(2, 8 * 48, WIDTH),
            vm(2, 8 * 32, LANES),
            vm(DEPTH + 1024, LANES),
            vm(GROUP, 64, LANES),
            vm(LANES, LANES),
            vm(LANES, LANES),
            vm(64, LANES),
            dma((7,)),
            dma((EXCHANGES,)),
            dma((EXCHANGES,)),
            dma((4,)),
            dma((4,)),
            dma((2,)),
            dma((2,)),
            dma((14, 4)),
            dma((14, 4)),
            dma((2,)),
            dma((6, 4)),
            dma((6, 4)),
            dma((10,)),
            dma((21,)),
            dma((6,)),
            pltpu.SemaphoreType.REGULAR,
        ],
        compiler_params=pltpu.CompilerParams(
            collective_id=0, has_side_effects=True, vmem_limit_bytes=63 << 20
        ),
    )(
        features,
        crop_image.reshape(1, SLOTS),
        crop_counts.reshape(1, IMAGES),
        w_reduce,
        w_spatial,
        w_expand,
        w_hidden,
        w_project,
        prototypes.T,
        norm_gain.reshape(40, LANES),
        norm_shift.reshape(41, LANES),
    )


def copy_kernel(*refs):
    count = len(refs) // 2
    refs[count][...] = refs[0][...]

    @pl.when(pl.program_id(0) == 0)
    def _():
        for source, target in zip(refs[1:count], refs[count + 1 :]):
            target[...] = source[...]


def handed_on(arrays):
    parts = 7
    blocks = [pl.BlockSpec((1, ROWS // parts, DEPTH), lambda k: (0, k, 0))]
    blocks += [pl.BlockSpec(a.shape, lambda k: (0, 0)) for a in arrays[1:]]
    return pl.pallas_call(
        copy_kernel,
        grid=(parts,),
        out_shape=tuple(jax.ShapeDtypeStruct(a.shape, a.dtype) for a in arrays),
        in_specs=blocks,
        out_specs=tuple(blocks),
        compiler_params=pltpu.CompilerParams(vmem_limit_bytes=62 << 20),
    )(*arrays)


def fused_body(*arrays):
    loss, *results = tower(*arrays)[:10]
    feature, *flats, loss = handed_on(results + [loss])
    return (loss.reshape(()), feature) + tuple(a.reshape(-1) for a in flats)


def solution(mesh):
    return jax.shard_map(
        fused_body if mesh.shape["dp"] == GROUP else body,
        mesh=mesh,
        in_specs=(P("res", "dp", None), P("dp"), P("dp"), P(), P(), P(), P(), P(), P(), P(), P()),
        out_specs=(
            P(),
            P("res", "dp", None),
            P(("res", "dp")),
            P(("res", "dp")),
            P(("res", "dp")),
            P(("res", "dp")),
            P(("res", "dp")),
            P(),
            P(),
            P(),
        ),
        check_vma=False,
    )
```

```python
import functools

import jax
import jax.numpy as jnp
from jax import lax
from jax.experimental import pallas as pl
from jax.experimental.pallas import tpu as pltpu
from jax.sharding import PartitionSpec as P

LSIDE = 7
SSIDE = 3
SINK = 3


HIGH = lax.Precision.HIGHEST
SOFTMAX_HEAT = 0.1
SHARPNESS = 0.05
EPS_NORM = 1e-05
EPS_UNIT = 1e-06


def combined_all(part, axis, combine):
    gathered = jax.tree.map(lambda a: lax.all_gather(a, axis), part)

    def take(source):
        return jax.tree.map(lambda a: lax.dynamic_index_in_dim(a, source, 0, False), gathered)

    return lax.fori_loop(
        1, lax.axis_size(axis), lambda source, state: combine(state, take(source)), take(0)
    )


def from_behind(value, axis, steps):
    count = lax.axis_size(axis)
    leading, last = (max(0, -steps), min(count, count - steps))
    return lax.ppermute(value, axis, [(source, source + steps) for source in range(leading, last)])


def row_contract(left, right):
    return lax.dot_general(
        left, right, (((0,), (0,)), ((), ())), preferred_element_type=jnp.float32
    )


def times_transposed(left, right):
    return lax.dot_general(
        left, right, (((1,), (1,)), ((), ())), preferred_element_type=jnp.float32
    )


def split_norms(vector, width, depth):
    return (
        vector[:width],
        vector[width : 2 * width],
        vector[2 * width : 2 * width + depth],
        vector[2 * width + depth :],
    )


def displaced(values, offset):
    if offset == 0:
        return values
    filler = jnp.zeros((abs(offset),) + values.shape[1:], values.dtype)
    if offset > 0:
        return jnp.concatenate([values[offset:], filler], axis=0)
    return jnp.concatenate([filler, values[:offset]], axis=0)


def tap_layout(row_count, big_crop):
    row_ids = jnp.arange(row_count)
    side_len = jnp.where(big_crop, LSIDE, SSIDE)
    pixel = row_ids % (side_len * side_len)
    line_ids = pixel // side_len
    column_ids = pixel % side_len
    layout = []
    for tap_y in (-1, 0, 1):
        for tap_x in (-1, 0, 1):
            inside = (
                (line_ids + tap_y >= 0)
                & (line_ids + tap_y < side_len)
                & (column_ids + tap_x >= 0)
                & (column_ids + tap_x < side_len)
            )
            layout.append((inside[:, None], tap_y * LSIDE + tap_x, tap_y * SSIDE + tap_x))
    return layout


def gather_taps(acts, layout, big_crop):
    pieces = []
    for inside, step_large, step_small in layout:
        moved_rows = jnp.where(big_crop, displaced(acts, step_large), displaced(acts, step_small))
        pieces.append(jnp.where(inside, moved_rows, jnp.zeros_like(moved_rows)))
    return jnp.concatenate(pieces, axis=1)


def scatter_taps(column_grad, layout, big_crop, channels):
    result = jnp.zeros((column_grad.shape[0], channels), jnp.float32)
    for tap_index, (inside, step_large, step_small) in enumerate(layout):
        piece = column_grad[:, tap_index * channels : (tap_index + 1) * channels]
        piece = jnp.where(inside, piece, jnp.zeros_like(piece))
        result = result + jnp.where(
            big_crop, displaced(piece, -step_large), displaced(piece, -step_small)
        )
    return result


def merge_moments(first_part, second_part):
    merged_count = first_part[0] + second_part[0]
    delta = second_part[1] - first_part[1]
    merged_mean = first_part[1] + delta * (second_part[0] / merged_count)
    merged_spread = (
        first_part[2]
        + second_part[2]
        + delta * delta * (first_part[0] * second_part[0] / merged_count)
    )
    return (merged_count, merged_mean, merged_spread)


def moments(values, weight):
    row_total = jnp.sum(weight)
    local_mean = jnp.sum(values * weight, axis=0) / row_total
    centred = values - local_mean
    local_spread = jnp.sum(weight * centred * centred, axis=0)
    whole_count, mean_vec, whole_spread = combined_all(
        (row_total, local_mean, local_spread), "dp", merge_moments
    )
    return (mean_vec, whole_spread / whole_count, whole_count)


def normalize(values, weight, gain_vec, shift_vec):
    mean_vec, var_vec, whole_count = moments(values, weight)
    scale_vec = lax.rsqrt(var_vec + EPS_NORM)
    centred = (values - mean_vec) * scale_vec
    return (centred * gain_vec + shift_vec, (centred, scale_vec, whole_count))


def normalize_back(upstream, weight, gain_vec, saved_stats):
    centred, scale_vec, whole_count = saved_stats
    upstream = upstream * weight
    local_first = jnp.sum(upstream, axis=0)
    local_second = jnp.sum(upstream * centred, axis=0)
    whole_first, whole_second = lax.psum((local_first, local_second), "dp")
    result = (
        gain_vec
        * scale_vec
        * (upstream - weight * (whole_first + centred * whole_second) / whole_count)
    )
    return (result, local_second, local_first)


def gelu_back(before, upstream):
    return jax.vjp(jax.nn.gelu, before)[1](upstream)[0]


def spread_rows(crop_grad, crop_total, area):
    depth = crop_grad.shape[1]
    widened = jnp.broadcast_to(crop_grad[:crop_total, None, :], (crop_total, area, depth))
    return widened.reshape(crop_total * area, depth) / area


def body(
    features,
    crop_counts,
    crop_image,
    w_reduce,
    w_spatial,
    w_expand,
    w_hidden,
    w_project,
    prototypes,
    norm_gain,
    norm_shift,
):
    inputs = features[0]
    row_count = inputs.shape[0]
    depth = w_reduce.shape[0]
    width = w_reduce.shape[1]
    hidden = w_hidden.shape[1]
    slot_count = crop_image.shape[0]
    image_count = crop_counts.shape[0]
    image_total = image_count * lax.axis_size("dp")
    big_crop = lax.axis_index("res") == 0
    first_image = lax.axis_index("dp") * image_count
    live_slot = (crop_image >= 0).astype(jnp.float32)
    slot_rows = SSIDE * SSIDE * slot_count
    live_rows = jnp.concatenate(
        [jnp.repeat(live_slot, SSIDE * SSIDE), jnp.zeros((row_count - slot_rows,), jnp.float32)]
    )
    row_weight = jnp.where(big_crop, jnp.ones_like(live_rows), live_rows)[:, None]
    large_crops = (jnp.arange(slot_count) < 2 * image_count).astype(jnp.float32)
    crop_weight = jnp.where(big_crop, large_crops, live_slot)[:, None]
    gain_one, gain_two, gain_three, gain_four = split_norms(norm_gain, width, depth)
    shift_one, shift_two, shift_three, shift_rest = split_norms(norm_shift, width, depth)
    shift_four = shift_rest[:hidden]
    head_bias = shift_rest[hidden:]
    layout = tap_layout(row_count, big_crop)
    conv_one = jnp.dot(inputs, w_reduce, preferred_element_type=jnp.float32)
    norm_one, saved_one = normalize(conv_one, row_weight, gain_one, shift_one)
    act_one = jax.nn.gelu(norm_one).astype(jnp.bfloat16)
    columns = gather_taps(act_one, layout, big_crop)
    conv_two = jnp.dot(columns, w_spatial, preferred_element_type=jnp.float32)
    norm_two, saved_two = normalize(conv_two, row_weight, gain_two, shift_two)
    act_two = jax.nn.gelu(norm_two).astype(jnp.bfloat16)
    conv_three = jnp.dot(act_two, w_expand, preferred_element_type=jnp.float32)
    norm_three, saved_three = normalize(conv_three, row_weight, gain_three, shift_three)
    joined = norm_three + inputs.astype(jnp.float32)
    block_out = jax.nn.gelu(joined)
    large_pool = jnp.mean(block_out.reshape(2 * image_count, LSIDE * LSIDE, depth), axis=1)
    large_pool = jnp.concatenate(
        [large_pool, jnp.zeros((slot_count - 2 * image_count, depth), jnp.float32)], axis=0
    )
    small_pool = jnp.mean(block_out[:slot_rows].reshape(slot_count, SSIDE * SSIDE, depth), axis=1)
    pooled = jnp.where(big_crop, large_pool, small_pool).astype(jnp.bfloat16)
    head_one = jnp.dot(pooled, w_hidden, preferred_element_type=jnp.float32)
    norm_four, saved_four = normalize(head_one, crop_weight, gain_four, shift_four)
    act_four = jax.nn.gelu(norm_four).astype(jnp.bfloat16)
    head_two = jnp.dot(act_four, w_project, preferred_element_type=jnp.float32) + head_bias
    unit, unit_back = jax.vjp(
        lambda vec: vec * lax.rsqrt(jnp.sum(vec * vec, axis=1, keepdims=True) + EPS_UNIT), head_two
    )
    unit_low = unit.astype(jnp.bfloat16)
    scores = jnp.dot(unit_low, prototypes, preferred_element_type=jnp.float32)
    table = jnp.exp(scores[: 2 * image_count].reshape(2, image_count, -1) / SHARPNESS)
    for sweep in range(SINK):
        column_total = lax.psum(jnp.sum(table, axis=1), "dp")
        table = table / column_total[:, None, :]
        table = table / jnp.sum(table, axis=2, keepdims=True)
    own_codes = table
    far_codes = from_behind(own_codes, "res", 1)
    weight_image = 1.0 / (2.0 * (1.0 + crop_counts.astype(jnp.float32)))
    onehot = ((crop_image - first_image)[:, None] == jnp.arange(image_count)[None, :]).astype(
        jnp.float32
    )
    slot_scale = jnp.dot(onehot, weight_image, precision=HIGH) * live_slot
    small_targets = jnp.dot(onehot, far_codes[0] + far_codes[1], precision=HIGH)

    def partial_loss(scores_by_row):
        log_probability = jax.nn.log_softmax(scores_by_row / SOFTMAX_HEAT, axis=-1)
        view_zero = log_probability[:image_count]
        view_one = log_probability[image_count : 2 * image_count]
        large_share = -jnp.sum(
            weight_image
            * (
                jnp.sum(own_codes[0] * view_one, axis=-1)
                + jnp.sum(own_codes[1] * view_zero, axis=-1)
            )
        )
        small_share = -jnp.sum(slot_scale * jnp.sum(small_targets * log_probability, axis=-1))
        return jnp.where(big_crop, large_share, small_share)

    local_total, total_back = jax.vjp(partial_loss, scores)
    whole_total = lax.psum(local_total, ("res", "dp"))
    loss = whole_total / image_total
    score_grad = total_back(jnp.ones_like(local_total))[0].astype(jnp.bfloat16)
    proto_grad = row_contract(unit_low, score_grad)
    unit_grad = times_transposed(score_grad, prototypes)
    head_two_grad = unit_back(unit_grad)[0]
    bias_grad = jnp.sum(head_two_grad, axis=0)
    head_two_low = head_two_grad.astype(jnp.bfloat16)
    project_grad = row_contract(act_four, head_two_low)
    act_four_grad = times_transposed(head_two_low, w_project)
    head_one_grad, gain_four_grad, shift_four_grad = normalize_back(
        gelu_back(norm_four, act_four_grad), crop_weight, gain_four, saved_four
    )
    head_one_low = head_one_grad.astype(jnp.bfloat16)
    hidden_grad = row_contract(pooled, head_one_low)
    pooled_grad = times_transposed(head_one_low, w_hidden)
    large_spread = spread_rows(pooled_grad, 2 * image_count, LSIDE * LSIDE)
    small_spread = jnp.concatenate(
        [
            spread_rows(pooled_grad, slot_count, SSIDE * SSIDE),
            jnp.zeros((row_count - slot_rows, depth), jnp.float32),
        ],
        axis=0,
    )
    out_grad = jnp.where(big_crop, large_spread, small_spread)
    joined_grad = gelu_back(joined, out_grad)
    three_grad, gain_three_grad, shift_three_grad = normalize_back(
        joined_grad, row_weight, gain_three, saved_three
    )
    three_low = three_grad.astype(jnp.bfloat16)
    expand_grad = row_contract(act_two, three_low)
    act_two_grad = times_transposed(three_low, w_expand)
    two_grad, gain_two_grad, shift_two_grad = normalize_back(
        gelu_back(norm_two, act_two_grad), row_weight, gain_two, saved_two
    )
    two_low = two_grad.astype(jnp.bfloat16)
    spatial_grad = row_contract(columns, two_low)
    column_grad = times_transposed(two_low, w_spatial)
    act_one_grad = scatter_taps(column_grad, layout, big_crop, width)
    one_grad, gain_one_grad, shift_one_grad = normalize_back(
        gelu_back(norm_one, act_one_grad), row_weight, gain_one, saved_one
    )
    one_low = one_grad.astype(jnp.bfloat16)
    reduce_grad = row_contract(inputs, one_low)
    input_grad = (joined_grad + times_transposed(one_low, w_reduce)) * row_weight
    weight_terms = (
        reduce_grad.reshape(-1),
        spatial_grad.reshape(-1),
        expand_grad.reshape(-1),
        hidden_grad.reshape(-1),
        project_grad.reshape(-1),
    )
    summed = (
        lax.psum_scatter(weight_terms[0], ("res", "dp"), scatter_dimension=0, tiled=True),
        lax.psum_scatter(weight_terms[1], ("res", "dp"), scatter_dimension=0, tiled=True),
        lax.psum_scatter(weight_terms[2], ("res", "dp"), scatter_dimension=0, tiled=True),
        lax.psum_scatter(weight_terms[3], ("res", "dp"), scatter_dimension=0, tiled=True),
        lax.psum_scatter(weight_terms[4], ("res", "dp"), scatter_dimension=0, tiled=True),
    )
    gain_local = jnp.concatenate([gain_one_grad, gain_two_grad, gain_three_grad, gain_four_grad])
    shift_local = jnp.concatenate(
        [shift_one_grad, shift_two_grad, shift_three_grad, shift_four_grad, bias_grad]
    )
    gain_total, shift_total, proto_total = lax.psum(
        (gain_local, shift_local, proto_grad.reshape(-1)), ("res", "dp")
    )
    return (
        loss,
        input_grad[None],
        summed[0],
        summed[1],
        summed[2],
        summed[3],
        summed[4],
        proto_total,
        gain_total,
        shift_total,
    )


MESH = pl.DeviceIdType.MESH
BF = jnp.bfloat16
F32 = jnp.float32
GROUP = 16
ROWS = 784
WIDTH = 512
DEPTH = 2048
HIDDEN = 2048
FEATS = 128
SLOTS = 64
IMAGES = 8
PROTOS = 3000
PADDED = 3072
LANES = 128
EDGE = 16
STRIPE = 112
TANH_IN = 0.7978845608
TANH_CUBE = 0.044715

X_COUNT, X_ONE, X_TWO, X_THREE, X_FOUR = 0, 1, 2, 3, 7
X_FOUR_BACK, X_EXTRA, EXCHANGES = 11, 15, 16
X_THREE_BACK, X_TWO_BACK, X_ONE_BACK = X_THREE, X_TWO, X_ONE
SPATIAL_HALF = 2304
PROTO_HALF = 1536


def mm(left, right):
    return jnp.dot(left, right, preferred_element_type=F32)


def mm_t(left, right):
    return lax.dot_general(left, right, (((1,), (1,)), ((), ())), preferred_element_type=F32)


def t_mm(left, right):
    return lax.dot_general(left, right, (((0,), (0,)), ((), ())), preferred_element_type=F32)


def gelu(v):
    return 0.5 * v * (1.0 + jnp.tanh(TANH_IN * (v + TANH_CUBE * (v * v * v))))


def gelu_slope(v):
    square = v * v
    t = jnp.tanh(TANH_IN * (v + TANH_CUBE * (v * square)))
    return 0.5 * (1.0 + t) + 0.5 * v * (1.0 - t * t) * (
        TANH_IN * (1.0 + (3.0 * TANH_CUBE) * square)
    )


def two_parts(v):
    high = v.astype(BF)
    return high, (v - high.astype(F32)).astype(BF)


def at(start, size):
    return pl.ds(pl.multiple_of(start, size if size % 8 == 0 else 8), size)


def lanes(index, width=LANES):
    if isinstance(index, int):
        return slice(index * width, (index + 1) * width)
    return pl.ds(pl.multiple_of(index * width, width), width)


def tower_kernel(
    feat,
    crop_row,
    count_row,
    w_reduce,
    w_spatial,
    w_expand,
    w_hidden,
    w_project,
    protos,
    gain,
    shift,
    loss_out,
    feature_out,
    reduce_out,
    spatial_out,
    expand_out,
    hidden_out,
    project_out,
    proto_out,
    gain_out,
    shift_out,
    PG,
    RB_S,
    RB_R,
    RB_E,
    RB_P,
    F,
    WR,
    WS,
    WE,
    WHB,
    WHC,
    WP,
    PROWS,
    PR,
    C1,
    C2,
    C3,
    DJ,
    APAD,
    COLS,
    A2,
    A1T,
    PO,
    H1,
    A4,
    DA4,
    DH1,
    DS,
    UL,
    D2F,
    D2A,
    TAB,
    Q,
    RACC,
    RINV,
    UNITS,
    UOWN,
    RW,
    CW,
    GRID,
    PT,
    P,
    PRM1,
    PRM2,
    PRM3,
    PRM4,
    MSG,
    RECV,
    FAR,
    OUT,
    RC_E,
    RC_P,
    OUT_P,
    STG,
    STGP,
    HB,
    HAL,
    PACC,
    PREC,
    PIN,
    load_sem,
    send_sem,
    recv_sem,
    unit_sem,
    out_sem,
    far_sem,
    wh_sem,
    rs_send,
    rs_recv,
    stage_sem,
    gather_send,
    gather_recv,
    core_send,
    core_recv,
    row_sem,
    free_sem,
):
    r = lax.axis_index("res")
    d = lax.axis_index("dp")
    big = r == 0
    area = jnp.where(big, LSIDE * LSIDE, SSIDE * SSIDE)
    area_f = area.astype(F32)
    side_f = jnp.where(big, float(LSIDE), float(SSIDE))
    area_inv = jnp.where(big, 1.0 / (LSIDE * LSIDE), 1.0 / (SSIDE * SSIDE))
    side_inv = jnp.where(big, 1.0 / LSIDE, 1.0 / SSIDE)

    loads = [
        pltpu.make_async_copy(source, target, load_sem.at[index])
        for index, (source, target) in enumerate(
            [
                (feat.at[0], F),
                (w_reduce, WR),
                (w_spatial, WS),
                (w_expand, WE),
                (w_hidden.at[:, pl.ds(pl.multiple_of(d * LANES, LANES), LANES)], WHC),
                (w_project, WP),
                (protos, PROWS),
            ]
        )
    ]
    loads[0].start()
    loads[1].start()

    def hidden_load(k, slot):
        return pltpu.make_async_copy(
            w_hidden.at[:, lanes(k, 256)], WHB.at[slot], wh_sem.at[slot]
        )


    barrier = pltpu.get_barrier_semaphore()

    @pl.loop(1, GROUP)
    def _(k):
        pl.semaphore_signal(
            barrier, inc=1, device_id=(r, lax.rem(d + k, GROUP)), device_id_type=MESH
        )

    pl.semaphore_signal(barrier, inc=1, device_id=(1 - r, d), device_id_type=MESH)

    slot_of = lax.broadcasted_iota(jnp.int32, (ROWS, SLOTS), 1)
    row_of = lax.broadcasted_iota(jnp.int32, (ROWS, SLOTS), 0)
    inside = ((row_of >= slot_of * area) & (row_of < slot_of * area + area)).astype(F32)
    lane_ids = lax.broadcasted_iota(jnp.int32, (1, SLOTS), 1)
    crop_ids = crop_row[...]
    live = jnp.where(big, (lane_ids < 2 * IMAGES).astype(F32), (crop_ids >= 0).astype(F32))
    RW[...] = jnp.broadcast_to(jnp.sum(inside * live, axis=1, keepdims=True), (ROWS, LANES))
    PT[...] = inside.astype(BF)
    slot_row = lax.broadcasted_iota(jnp.int32, (SLOTS, ROWS), 0)
    pixel_lane = lax.broadcasted_iota(jnp.int32, (SLOTS, ROWS), 1)
    P[...] = (
        ((pixel_lane >= slot_row * area) & (pixel_lane < slot_row * area + area))
        .astype(F32)
        .astype(BF)
    )
    square_row = lax.broadcasted_iota(jnp.int32, (SLOTS, SLOTS), 0)
    square_lane = lax.broadcasted_iota(jnp.int32, (SLOTS, SLOTS), 1)
    eye = (square_row == square_lane).astype(F32)
    CW[...] = jnp.broadcast_to(jnp.sum(eye * live, axis=1, keepdims=True), (SLOTS, LANES))
    live_total = jnp.sum(live, axis=1, keepdims=True)
    own_crops = jnp.broadcast_to(live_total, (1, LANES))
    own_rows = own_crops * area_f
    row_f = lax.broadcasted_iota(jnp.int32, (ROWS, LANES), 0).astype(F32)
    pixel = row_f - jnp.floor((row_f + 0.5) * area_inv) * area_f
    line = jnp.floor((pixel + 0.5) * side_inv)
    GRID[...] = line * 8.0 + (pixel - line * side_f)
    APAD[0:EDGE, :] = jnp.zeros((EDGE, WIDTH), F32)
    APAD[EDGE + ROWS :, :] = jnp.zeros((EDGE, WIDTH), F32)
    for prm, base, blocks in ((PRM1, 0, 4), (PRM2, 4, 4), (PRM3, 8, 16), (PRM4, 24, 16)):
        for q in range(blocks):
            prm[q, 2:3, :] = gain[base + q : base + q + 1, :]
            prm[q, 3:4, :] = shift[base + q : base + q + 1, :]
    MSG[X_COUNT] = jnp.broadcast_to(own_rows, (8, LANES))

    place = {1: lax.rem(d, 2), 2: lax.rem(d // 2, 2), 4: lax.rem(d // 4, 2), 8: d // 8}

    def across(mask):
        index = d
        for bit in (1, 2, 4, 8):
            if mask & bit:
                index = index + bit * (1 - 2 * place[bit])
        return index

    far_first = sorted(range(1, GROUP), key=lambda m: -(2 * (m // 8) + m // 4 % 2 + m // 2 % 2 + m % 2))
    peers = [across(mask) for mask in far_first]

    def announce(x):
        for peer in peers:
            pltpu.make_async_remote_copy(
                MSG.at[x],
                RECV.at[x, d],
                send_sem.at[x],
                recv_sem.at[x],
                device_id=(r, peer),
                device_id_type=MESH,
            ).start()

        RECV[x, d] = MSG[x]

    def collect(x):
        others = RECV.at[x, pl.ds(0, GROUP - 1)]
        pltpu.make_async_copy(others, others, recv_sem.at[x]).wait()
        pltpu.make_async_copy(others, others, send_sem.at[x]).wait()

    def partner(bit):
        return (r, across(bit))

    def block_of(order, stage, j, flip):
        index = 0
        for t, bit in enumerate(order):
            if t < stage:
                index = index + bit * place[bit]
            elif t == stage:
                index = index + bit * ((1 - place[bit]) if flip else place[bit])
            else:
                index = index + bit * ((j >> (t - stage - 1)) & 1)
        return index

    class Strip:
        def __init__(self, own, pieces, stride, landing, staging, order, number):
            self.own, self.pieces, self.stride = own, pieces, stride
            self.depth = sum(depth for _, depth in pieces)
            self.landing, self.staging, self.order, self.number = landing, staging, order, number

        def blocks(self, index):
            offset = 0
            for base, depth in self.pieces:
                start = pl.multiple_of(base + index * self.stride, 8)
                yield offset, depth, self.own.at[pl.ds(start, depth), :]
                offset += depth

        def rows(self, stage):
            first = 16 - (16 >> stage)
            return first * self.depth, (8 >> stage) * self.depth

        def start(self, stage):
            first, _ = self.rows(stage)
            for j in range(8 >> stage):
                index = block_of(self.order, stage, j, True)
                for offset, depth, block in self.blocks(index):
                    pltpu.make_async_remote_copy(
                        block,
                        self.landing.at[pl.ds(first + j * self.depth + offset, depth), :],
                        rs_send.at[self.number, stage],
                        rs_recv.at[self.number, stage],
                        device_id=partner(self.order[stage]),
                        device_id_type=MESH,
                    ).start()

        def landed(self, stage):
            first, size = self.rows(stage)
            return self.landing.at[pl.ds(first, size), :]

        def fetch(self, stage, slot):
            area = self.landed(stage)
            pltpu.make_async_copy(area, area, rs_recv.at[self.number, stage]).wait()
            _, size = self.rows(stage)
            copy = pltpu.make_async_copy(
                area, self.staging.at[slot, pl.ds(0, size), :], stage_sem.at[slot]
            )
            copy.start()
            return copy

        def fold(self, stage, slot):
            for j in range(8 >> stage):
                index = block_of(self.order, stage, j, False)
                for offset, depth, block in self.blocks(index):
                    start = j * self.depth + offset
                    block[...] += self.staging[slot, start : start + depth, :]

        def close(self):
            for stage in range(4):
                area = self.landed(stage)
                pltpu.make_async_copy(area, area, rs_send.at[self.number, stage]).wait()

    def advance(steps):
        copies = [steps[0][0].fetch(steps[0][1], 0)]
        for k, (strip, stage) in enumerate(steps):
            if k + 1 < len(steps):
                copies.append(steps[k + 1][0].fetch(steps[k + 1][1], (k + 1) % 2))
            copies[k].wait()
            strip.fold(stage, k % 2)
            if stage < 3:
                strip.start(stage + 1)

    def wave(strips, stage):
        return [(strip, stage) for strip in strips]

    orders = ((1, 2, 4, 8), (2, 4, 1, 8), (4, 1, 2, 8))
    spatial_strips = [
        Strip(C3, ((48 * p, 48),), 144, RB_S.at[p], STG, orders[p], p) for p in range(3)
    ]
    reduce_strips = [
        Strip(C3, ((SPATIAL_HALF + 24 * p, depth),), 64, RB_R.at[p], STG, orders[p], 3 + p)
        for p, depth in enumerate((24, 24, 16))
    ]
    expand_strips = [
        Strip(RC_E, pieces, 16, RB_E.at[p], STG, orders[p], 6 + p)
        for p, pieces in enumerate(
            (((0, 16), (768, 8)), ((256, 16), (776, 8)), ((512, 16),))
        )
    ]
    proto_strips = [
        Strip(RC_P, ((32 * p, 32),), 96, RB_P.at[p], STGP, orders[p], 9 + p) for p in range(3)
    ]

    def gathered_block(order, stage, j):
        index = 0
        for t, bit in enumerate(order):
            if t < stage:
                index = index + bit * ((j >> t) & 1)
            else:
                index = index + bit * place[bit]
        return index

    def gather_start(ref, base, stride, depth, columns, order, stage, number, which=None):
        for j in which or range(1 << stage):
            start = pl.multiple_of(base + gathered_block(order, stage, j) * stride, 16)
            area = ref.at[pl.ds(start, depth), columns]
            pltpu.make_async_remote_copy(
                area,
                area,
                gather_send.at[number, stage],
                gather_recv.at[number, stage],
                device_id=partner(order[stage]),
                device_id_type=MESH,
            ).start()

    def gather_wait(ref, depth, columns, stage, number, sems):
        area = ref.at[pl.ds(0, depth << stage), columns]
        pltpu.make_async_copy(area, area, sems.at[number, stage]).wait()

    row_order = (8, 4, 1, 2)

    def rows_gather(stage):
        by_size(
            lambda depth: gather_start(
                D2A, 0, depth, depth, slice(0, FEATS), row_order, stage, 6
            )
        )

    def rows_arrived(stage, sems):
        by_size(lambda depth: gather_wait(D2A, depth, slice(0, FEATS), stage, 6, sems))

    pooled_parts = (
        (slice(0, 896), (8, 4, 1, 2)),
        (slice(896, 1280), (8, 1, 2, 4)),
        (slice(1280, 2048), (8, 2, 4, 1)),
    )

    def by_size(action):
        @pl.when(big)
        def _():
            action(2 * IMAGES)

        @pl.when(jnp.logical_not(big))
        def _():
            action(SLOTS)

    def pooled_gather(stage, parts=(0, 1, 2), which=None):
        def action(depth):
            for number in parts:
                columns, order = pooled_parts[number]
                gather_start(PG, 0, depth, depth, columns, order, stage, number, which)

        by_size(action)

    def pooled_arrived(stage):
        def action(depth):
            for number, (columns, order) in enumerate(pooled_parts):
                gather_wait(PG, depth, columns, stage, number, gather_recv)

        by_size(action)

    def core_copy(source, target, sent, landed):
        return pltpu.make_async_remote_copy(
            source,
            target,
            core_send.at[sent],
            core_recv.at[landed],
            device_id=(1 - r, d),
            device_id_type=MESH,
        )

    def half_tile(index):
        return pl.ds(pl.multiple_of(index * 256, 256), 256)

    def local_moments(values, rows, first_lane, weight, own, x):
        for q in range(4):
            v = values[rows, first_lane + q * LANES : first_lane + (q + 1) * LANES]
            w = weight[...]
            total = jnp.sum(v * w, axis=0, keepdims=True)
            centred = (v - total / own) * w
            MSG[x, q : q + 1, :] = total
            MSG[x, 4 + q : 5 + q, :] = jnp.sum(centred * centred, axis=0, keepdims=True)

    def whole_moments(x, counts, prm, first):
        whole = jnp.sum(counts, axis=0, keepdims=True)
        each = counts[:, None, :]
        sums = RECV[x, :, 0:4, :]
        spreads = RECV[x, :, 4:8, :]
        mean = jnp.sum(sums, axis=0) / whole
        off = sums / each - mean[None]
        var = jnp.sum(spreads + each * off * off, axis=0) / whole
        scale = lax.rsqrt(var + EPS_NORM)
        for q in range(4):
            prm[first + q, 0:1, :] = mean[q : q + 1]
            prm[first + q, 1:2, :] = scale[q : q + 1]

    def whole_back(x, whole, prm, first, place):
        ones = jnp.sum(RECV[x, :, 0:4, :], axis=0)
        twos = jnp.sum(RECV[x, :, 4:8, :], axis=0)
        for q in range(4):
            prm[first + q, 4:5, :] = ones[q : q + 1] / whole
            prm[first + q, 5:6, :] = twos[q : q + 1] / whole
        FAR[0, pl.ds(place, 4), :] = twos
        FAR[0, pl.ds(48 + place, 4), :] = ones

    def norm_terms(v, prm, index):
        centred = (v - prm[index, 0:1, :]) * prm[index, 1:2, :]
        return centred, centred * prm[index, 2:3, :] + prm[index, 3:4, :]

    def back_through(du, centred, weight, prm, index):
        inner = du - weight * (prm[index, 4:5, :] + centred * prm[index, 5:6, :])
        return prm[index, 2:3, :] * prm[index, 1:2, :] * inner

    def spread_taps(sign):
        def for_side(side):
            @pl.loop(0, ROWS // STRIPE)
            def _(s):
                base = pl.multiple_of(s * STRIPE, STRIPE)
                rows = pl.ds(base, STRIPE)
                window = pl.ds(base, STRIPE + 2 * EDGE)
                line_ids = jnp.floor(GRID[rows, :] * 0.125)
                column_ids = GRID[rows, :] - line_ids * 8.0
                for tap in range(9):
                    dy, dx = sign * (tap // 3 - 1), sign * (tap % 3 - 1)
                    y = line_ids + float(dy)
                    x = column_ids + float(dx)
                    keep = (y >= 0.0) & (y < float(side)) & (x >= 0.0) & (x < float(side))
                    start = EDGE + dy * side + dx
                    for q in range(4):
                        moved = APAD[window, lanes(q)][start : start + STRIPE]
                        COLS[rows, tap * WIDTH + q * LANES : tap * WIDTH + (q + 1) * LANES] = (
                            jnp.where(keep, moved, 0.0).astype(BF)
                        )

        @pl.when(big)
        def _():
            for_side(LSIDE)

        @pl.when(jnp.logical_not(big))
        def _():
            for_side(SSIDE)

    loads[0].wait()
    loads[1].wait()
    for load in loads[2:]:
        load.start()
    for k in range(2):
        hidden_load(k, k).start()
    C1[...] = mm(F[...], WR[...])
    every = pl.ds(0, ROWS)
    local_moments(C1, every, 0, RW, own_rows, X_ONE)
    pl.semaphore_wait(barrier, GROUP)
    announce(X_ONE)
    announce(X_COUNT)
    collect(X_COUNT)
    row_counts = RECV[X_COUNT, :, 0, :]
    crop_counts = row_counts * area_inv
    whole_rows = jnp.sum(row_counts, axis=0, keepdims=True)
    whole_crops = jnp.sum(crop_counts, axis=0, keepdims=True)
    collect(X_ONE)
    whole_moments(X_ONE, row_counts, PRM1, 0)
    for q in range(4):
        _, before = norm_terms(C1[:, lanes(q)], PRM1, q)
        act = gelu(before)
        APAD[EDGE : EDGE + ROWS, lanes(q)] = act
        A1T[lanes(q), :] = act.astype(BF).T
    spread_taps(1)
    loads[2].wait()

    @pl.loop(0, 2)
    def _(h):
        C2[:, lanes(h, 256)] = mm(COLS[...], WS[:, lanes(h, 256)])

    local_moments(C2, every, 0, RW, own_rows, X_TWO)
    announce(X_TWO)
    collect(X_TWO)
    whole_moments(X_TWO, row_counts, PRM2, 0)
    for q in range(4):
        _, before = norm_terms(C2[:, lanes(q)], PRM2, q)
        A2[:, lanes(q)] = gelu(before).astype(BF)
    loads[3].wait()

    @pl.loop(0, 4)
    def _(j):
        rows = at(j * ROWS, ROWS)
        C3[rows, :] = mm(A2[...], WE[:, lanes(j, WIDTH)])
        local_moments(C3, rows, 0, RW, own_rows, X_THREE + j)
        announce(X_THREE + j)

    @pl.loop(0, 4)
    def _(j):
        collect(X_THREE + j)
        whole_moments(X_THREE + j, row_counts, PRM3, 4 * j)
        rows = at(j * ROWS, ROWS)
        for q in range(4):
            _, before = norm_terms(C3[rows, lanes(q)], PRM3, 4 * j + q)
            joined = before + F[:, lanes(4 * j + q)].astype(F32)
            high, low = two_parts(gelu(joined))
            pooled = (mm(P[...], high) + mm(P[...], low)) * area_inv
            pooled_low = pooled.astype(BF)
            PO[:, lanes(4 * j + q)] = pooled_low
            DA4[j, :, lanes(q)] = pooled_low.astype(F32) * CW[...]

    def keep_pooled(depth):
        own = PG.at[pl.ds(pl.multiple_of(d * depth, 16), depth), :]
        for j in range(4):
            pltpu.make_async_copy(
                DA4.at[j, pl.ds(0, depth), :], own.at[:, lanes(j, WIDTH)], row_sem.at[0]
            ).start()
        pltpu.make_async_copy(own, own, row_sem.at[0]).wait()

    by_size(keep_pooled)

    @pl.loop(0, 4)
    def _(j):
        for half in range(2):
            k = 2 * j + half
            hidden_load(k, half).wait()
            H1[j, :, half * 256 : half * 256 + 256] = mm(PO[...], WHB[half])
            hidden_load(lax.rem(k + 2, 8), half).start()
        local_moments(H1.at[j], pl.ds(0, SLOTS), 0, CW, own_crops, X_FOUR + j)
        announce(X_FOUR + j)

    pooled_gather(0, (0,))
    loads[5].wait()
    loads[6].wait()
    TAB[0:PROTOS, :] = PROWS[...].astype(F32)
    TAB[PROTOS:, :] = jnp.zeros((PADDED - PROTOS, FEATS), F32)
    PR[...] = TAB[...].astype(BF)

    @pl.loop(0, 4)
    def _(j):
        collect(X_FOUR + j)
        whole_moments(X_FOUR + j, crop_counts, PRM4, 4 * j)
        for q in range(4):
            _, before = norm_terms(H1[j, :, lanes(q)], PRM4, 4 * j + q)
            A4[:, lanes(4 * j + q)] = gelu(before).astype(BF)

    head_two = mm(A4[...], WP[...]) + shift[40:41, :]
    length_inv = lax.rsqrt(jnp.sum(head_two * head_two, axis=1, keepdims=True) + EPS_UNIT)
    unit = head_two * length_inv
    unit_low = unit.astype(BF)
    UOWN[...] = unit_low[0 : 2 * IMAGES].astype(F32)
    UL[...] = unit_low

    def unit_copy(peer):
        return pltpu.make_async_remote_copy(
            UOWN,
            UNITS.at[d],
            unit_sem.at[0],
            unit_sem.at[1],
            device_id=(r, peer),
            device_id_type=MESH,
        )

    forward_units = pltpu.make_async_remote_copy(
        UNITS, UNITS, unit_sem.at[2], unit_sem.at[3], device_id=(1 - r, d), device_id_type=MESH
    )

    @pl.when(big)
    def _():
        for peer in peers:
            unit_copy(peer).start()

        UNITS[d] = UOWN[...]

    pooled_gather(0, (1, 2))

    @pl.when(big)
    def _():
        others = UNITS.at[pl.ds(0, GROUP - 1)]
        pltpu.make_async_copy(others, others, unit_sem.at[1]).wait()
        pltpu.make_async_copy(others, others, unit_sem.at[0]).wait()
        forward_units.start()

    @pl.when(jnp.logical_not(big))
    def _():
        forward_units.wait_recv()

    chunk = 512
    chunks = PADDED // chunk
    images = GROUP * IMAGES
    chunk_lane = lax.broadcasted_iota(jnp.int32, (1, chunk), 1)

    @pl.loop(0, 2)
    def _(v):
        view = UNITS[:, pl.ds(pl.multiple_of(v * IMAGES, IMAGES), IMAGES), :]
        view = view.reshape(images, FEATS).astype(BF)

        def sweep(first):
            RACC[...] = jnp.zeros_like(RACC)

            @pl.loop(0, chunks)
            def _(c):
                valid = (chunk_lane + c * chunk) < PROTOS
                if first:
                    raised = jnp.exp(mm_t(view, PR[at(c * chunk, chunk), :]) / SHARPNESS)
                for q in range(chunk // LANES):
                    tile = pl.ds(pl.multiple_of(c * chunk + q * LANES, LANES), images)
                    if first:
                        table = raised[:, lanes(q)]
                    else:
                        table = TAB[tile, :] * RINV[...]
                    total = jnp.sum(table, axis=0, keepdims=True)
                    table = table * jnp.where(valid[:, lanes(q)], 1.0 / total, 0.0)
                    TAB[tile, :] = table
                    RACC[...] += table

            RINV[...] = jnp.broadcast_to(
                1.0 / jnp.sum(RACC[...], axis=1, keepdims=True), (images, LANES)
            )

        for number in range(SINK):
            sweep(number == 0)
        row_inv = RINV[pl.ds(pl.multiple_of(d * IMAGES, IMAGES), IMAGES), :]
        for c in range(PADDED // LANES):
            own = pl.ds(pl.multiple_of(c * LANES + d * IMAGES, IMAGES), IMAGES)
            Q[pl.ds(pl.multiple_of(v * IMAGES, IMAGES), IMAGES), lanes(c)] = TAB[own, :] * row_inv

    ident_f = jnp.sum(eye * crop_ids.astype(F32), axis=1, keepdims=True)
    pick_lane = lax.broadcasted_iota(jnp.int32, (SLOTS, 2 * IMAGES), 1)
    pick_row = lax.broadcasted_iota(jnp.int32, (SLOTS, 2 * IMAGES), 0)
    image_lane = jnp.where(pick_lane < IMAGES, pick_lane, pick_lane - IMAGES)
    first_image = (d * IMAGES).astype(F32)
    crossed = (pick_row < 2 * IMAGES) & (jnp.abs(pick_row - pick_lane) == IMAGES)
    matched = ident_f == image_lane.astype(F32) + first_image
    picked = jnp.where(big, crossed.astype(F32), matched.astype(F32))
    image_weight = 1.0 / (2.0 * (1.0 + count_row[...].astype(F32)))
    picked = picked * jnp.concatenate([image_weight, image_weight], axis=1)
    valid_all = lax.broadcasted_iota(jnp.int32, (1, PADDED), 1) < PROTOS
    loss_rows = []
    for s in range(4):
        rows = slice(16 * s, 16 * s + 16)
        target = jnp.dot(picked[rows], Q[...], precision=HIGH, preferred_element_type=F32)
        logit = jnp.where(valid_all, mm_t(UL[rows, :], PR[...]) / SOFTMAX_HEAT, -1e30)
        shifted = logit - jnp.max(logit, axis=1, keepdims=True)
        raised = jnp.exp(shifted)
        total = jnp.sum(raised, axis=1, keepdims=True)
        loss_rows.append(jnp.sum(target * (shifted - jnp.log(total)), axis=1, keepdims=True))
        mass = jnp.sum(target, axis=1, keepdims=True)
        DS[rows, :] = ((raised * (mass / total) - target) / SOFTMAX_HEAT).astype(BF)
    loss_local = -jnp.sum(
        loss_rows[0] + loss_rows[1] + loss_rows[2] + loss_rows[3], axis=0, keepdims=True
    )

    def proto_half(which):
        return t_mm(DS[:, pl.ds(pl.multiple_of(which * PROTO_HALF, LANES), PROTO_HALF)], UL[...])

    unit_grad = mm(DS[...], PR[...])
    along = jnp.sum(unit * unit_grad, axis=1, keepdims=True)
    head_two_grad = (unit_grad - unit * along) * length_inv
    bias_grad = jnp.sum(head_two_grad, axis=0, keepdims=True)
    head_two_low = head_two_grad.astype(BF)

    @pl.loop(0, 4)
    def _(j):
        DA4[j] = mm_t(head_two_low, WP[at(j * WIDTH, WIDTH), :])
        for q in range(4):
            centred, before = norm_terms(H1[j, :, lanes(q)], PRM4, 4 * j + q)
            du = DA4[j, :, lanes(q)] * gelu_slope(before) * CW[...]
            DA4[j, :, lanes(q)] = du
            MSG[X_FOUR_BACK + j, q : q + 1, :] = jnp.sum(du, axis=0, keepdims=True)
            MSG[X_FOUR_BACK + j, 4 + q : 5 + q, :] = jnp.sum(du * centred, axis=0, keepdims=True)
        announce(X_FOUR_BACK + j)

    D2F[...] = head_two_low.astype(F32)

    def keep_rows(depth):
        D2A[pl.ds(pl.multiple_of(d * depth, 16), depth), :] = D2F[0:depth, :]

    by_size(keep_rows)
    MSG[X_EXTRA] = jnp.concatenate(
        [bias_grad, jnp.broadcast_to(loss_local, (1, LANES)), jnp.zeros((6, LANES), F32)], axis=0
    )
    announce(X_EXTRA)
    OUT_P[...] = proto_half(1 - r)
    proto_swap = core_copy(OUT_P, RC_P, 4, 17)
    proto_swap.start()
    rows_gather(0)
    pooled_arrived(0)
    pooled_gather(1)

    @pl.loop(0, 4)
    def _(j):
        collect(X_FOUR_BACK + j)
        whole_back(X_FOUR_BACK + j, whole_crops, PRM4, 4 * j, 24 + 4 * j)
        for q in range(4):
            centred, _ = norm_terms(H1[j, :, lanes(q)], PRM4, 4 * j + q)
            DH1[:, lanes(4 * j + q)] = back_through(
                DA4[j, :, lanes(q)], centred, CW[...], PRM4, 4 * j + q
            ).astype(BF)

    pooled_arrived(1)
    pooled_gather(2)
    rows_arrived(0, gather_recv)
    rows_gather(1)
    DP = H1
    for j in range(4):
        DP[j] = jnp.zeros((SLOTS, WIDTH), F32)

    @pl.loop(0, 4)
    def _(i):
        for half in range(2):
            k = 2 * i + half
            hidden_load(k, half).wait()
            back = mm_t(DH1[:, lanes(k, 256)], WHB[half])
            for j in range(4):
                DP[j] += back[:, lanes(j, WIDTH)]

            @pl.when(k + 2 < 8)
            def _():
                hidden_load(k + 2, half).start()

    @pl.loop(0, 4)
    def _(j):
        rows = at(j * ROWS, ROWS)
        for q in range(4):
            high, low = two_parts(DP[j, :, lanes(q)] * area_inv)
            out_grad = mm(PT[...], high) + mm(PT[...], low)
            centred, before = norm_terms(C3[rows, lanes(q)], PRM3, 4 * j + q)
            joined = before + F[:, lanes(4 * j + q)].astype(F32)
            du = out_grad * gelu_slope(joined)
            DJ[rows, lanes(q)] = du
            MSG[X_THREE_BACK + j, q : q + 1, :] = jnp.sum(du, axis=0, keepdims=True)
            MSG[X_THREE_BACK + j, 4 + q : 5 + q, :] = jnp.sum(du * centred, axis=0, keepdims=True)
        announce(X_THREE_BACK + j)

    rows_arrived(1, gather_recv)
    rows_gather(2)
    pooled_arrived(2)
    pooled_gather(3, which=range(4))
    proto_own = proto_half(r)
    proto_swap.wait_recv()
    RC_P[...] += proto_own
    for strip in proto_strips:
        strip.start(0)

    @pl.loop(0, 4)
    def _(j):
        collect(X_THREE_BACK + j)
        whole_back(X_THREE_BACK + j, whole_rows, PRM3, 4 * j, 8 + 4 * j)
        rows = at(j * ROWS, ROWS)
        for q in range(4):
            centred, _ = norm_terms(C3[rows, lanes(q)], PRM3, 4 * j + q)
            COLS[:, lanes(4 * j + q)] = back_through(
                DJ[rows, lanes(q)], centred, RW[...], PRM3, 4 * j + q
            ).astype(BF)

    pl.semaphore_signal(free_sem, inc=1, device_id=(1 - r, d), device_id_type=MESH)
    centre = pl.ds(EDGE, ROWS)

    @pl.loop(0, 2)
    def _(h):
        APAD[centre, lanes(h, 256)] = mm_t(COLS[:, 0:DEPTH], WE[at(h * 256, 256), :])

    def through_gelu(values, prm, x):
        for q in range(4):
            centred, before = norm_terms(values[:, lanes(q)], prm, q)
            du = APAD[centre, lanes(q)] * gelu_slope(before) * RW[...]
            APAD[centre, lanes(q)] = du
            MSG[x, q : q + 1, :] = jnp.sum(du, axis=0, keepdims=True)
            MSG[x, 4 + q : 5 + q, :] = jnp.sum(du * centred, axis=0, keepdims=True)
        announce(x)

    through_gelu(C2, PRM2, X_TWO_BACK)

    @pl.loop(0, 4)
    def _(j):
        OUT[half_tile(j), :] = t_mm(A2[:, half_tile(1 - r)], COLS[:, lanes(j, WIDTH)])
        core_copy(OUT.at[half_tile(j), :], RC_E.at[half_tile(j), :], j, j).start()

    @pl.loop(0, 4)
    def _(j):
        own = t_mm(A2[:, half_tile(r)], COLS[:, lanes(j, WIDTH)])
        tile = RC_E.at[half_tile(j), :]
        core_copy(tile, tile, j, j).wait_recv()
        tile[...] += own

    for strip in expand_strips:
        strip.start(0)
    advance(wave(proto_strips, 0))
    collect(X_TWO_BACK)
    whole_back(X_TWO_BACK, whole_rows, PRM2, 0, 4)
    for q in range(4):
        centred, _ = norm_terms(C2[:, lanes(q)], PRM2, q)
        APAD[centre, lanes(q)] = back_through(APAD[centre, lanes(q)], centred, RW[...], PRM2, q)
    spread_taps(-1)

    @pl.loop(0, 2)
    def _(h):
        total = mm_t(COLS[:, 0:WIDTH], WS[at(h * 256, 256), :])
        for tap in range(1, 9):
            total += mm_t(
                COLS[:, tap * WIDTH : (tap + 1) * WIDTH], WS[at(tap * WIDTH + h * 256, 256), :]
            )
        APAD[centre, lanes(h, 256)] = total

    through_gelu(C1, PRM1, X_ONE_BACK)

    rows_arrived(2, gather_recv)
    rows_gather(3)
    pooled_gather(3, which=range(4, 8))

    def half_tap(which, m):
        g = 9 * which + m
        return mm(A1T[half_tile(lax.rem(g, 2)), :], COLS[:, lanes(g // 2, WIDTH)])

    pl.semaphore_wait(free_sem, 1)

    def ring(slot):
        tile = OUT.at[half_tile(slot), :]
        return tile, core_copy(tile, tile, slot, 0)

    def add_half_tap(m):
        own = half_tap(r, m)
        tile = C3.at[half_tile(m), :]
        core_copy(tile, tile, 0, 4 + m).wait_recv()
        tile[...] += own

    @pl.loop(0, 9)
    def _(m):
        slot = lax.rem(m, 4)
        tile, last = ring(slot)
        last.wait_send()
        tile[...] = half_tap(1 - r, m)
        core_copy(tile, C3.at[half_tile(m), :], slot, 4 + m).start()

        @pl.when(m >= 2)
        def _():
            add_half_tap(m - 2)

    add_half_tap(7)
    add_half_tap(8)
    for strip in spatial_strips:
        strip.start(0)

    collect(X_ONE_BACK)
    whole_back(X_ONE_BACK, whole_rows, PRM1, 0, 0)
    for q in range(4):
        centred, _ = norm_terms(C1[:, lanes(q)], PRM1, q)
        A2[:, lanes(q)] = back_through(APAD[centre, lanes(q)], centred, RW[...], PRM1, q).astype(BF)

    def reduce_tile(which, j):
        columns = pl.ds(pl.multiple_of(which * 1024 + j * 256, 256), 256)
        return t_mm(F[:, columns], A2[...])

    def reduce_rows(j):
        return C3.at[pl.ds(pl.multiple_of(SPATIAL_HALF + j * 256, 256), 256), :]

    @pl.loop(0, 4)
    def _(j):
        slot = lax.rem(j + 1, 4)
        tile, last = ring(slot)
        last.wait_send()
        tile[...] = reduce_tile(1 - r, j)
        core_copy(tile, reduce_rows(j), slot, 13 + j).start()

    @pl.loop(0, 4)
    def _(j):
        own = reduce_tile(r, j)
        tile = reduce_rows(j)
        core_copy(tile, tile, 0, 13 + j).wait_recv()
        tile[...] += own

    for strip in reduce_strips:
        strip.start(0)
    collect(X_EXTRA)
    extra = jnp.sum(RECV[X_EXTRA], axis=0)
    FAR[0, 88:96, :] = extra
    far = pltpu.make_async_remote_copy(
        FAR.at[0],
        FAR.at[1],
        far_sem.at[0],
        far_sem.at[1],
        device_id=(1 - r, d),
        device_id_type=MESH,
    )
    far.start()

    @pl.loop(0, 4)
    def _(j):
        rows = at(j * ROWS, ROWS)
        grad = mm_t(A2[...], WR[at(j * WIDTH, WIDTH), :])
        for q in range(4):
            DJ[rows, lanes(q)] = (DJ[rows, lanes(q)] + grad[:, lanes(q)]) * RW[...]
        pltpu.make_async_copy(
            DJ.at[rows, :], feature_out.at[0, :, lanes(j, WIDTH)], out_sem.at[0]
        ).start()

    advance(wave(proto_strips, 1))
    advance(wave(expand_strips, 0))
    HACC = HB.at[pl.ds(0, DEPTH), :]
    HREC = HB.at[pl.ds(DEPTH, 1024), :]

    unit_rows = pl.ds(pl.multiple_of(d * LANES, LANES), LANES)

    def hidden_gradient(depth):
        pooled_arrived(3)
        total = GROUP * depth
        pieces = [(c, j) for c in range(total // 256) for j in range(4)]

        def load(k):
            c, j = pieces[k]
            return pltpu.make_async_copy(
                PG.at[pl.ds(256 * c, 256), lanes(j, WIDTH)],
                STG.at[k % 2, pl.ds(0, 256), :],
                stage_sem.at[k % 2],
            )

        load(0).start()
        for k, (c, j) in enumerate(pieces):
            if k + 1 < len(pieces):
                load(k + 1).start()
            load(k).wait()
            COLS[
                256 * (c % 2) : 256 * (c % 2) + 256,
                DEPTH * (c // 2) + WIDTH * j : DEPTH * (c // 2) + WIDTH * j + WIDTH,
            ] = STG[k % 2, 0:256, :].astype(BF)
        for part in range((total + 511) // 512):
            count = min(512, total)
            pooled_all = COLS[0:count, DEPTH * part : DEPTH * part + DEPTH]
            head = mm(pooled_all, WHC[...])
            centred, earlier = norm_terms(head, PRM4, d)
            low_rows = D2A[512 * part : 512 * part + count, :].astype(BF)
            du = mm_t(low_rows, WP[unit_rows, :]) * gelu_slope(earlier)
            dh = back_through(du, centred, 1.0, PRM4, d).astype(BF)
            act = gelu(earlier).astype(BF)
            if part == 0:
                PACC[...] = t_mm(act, low_rows)
            else:
                PACC[...] += t_mm(act, low_rows)
            for j in range(4):
                columns = slice(DEPTH * part + WIDTH * j, DEPTH * part + WIDTH * j + WIDTH)
                rows = slice(WIDTH * j, WIDTH * j + WIDTH)
                if part == 0:
                    HACC[rows, :] = t_mm(COLS[0:count, columns], dh)
                else:
                    HACC[rows, :] += t_mm(COLS[0:count, columns], dh)

    loads[4].wait()
    rows_arrived(3, gather_recv)
    by_size(hidden_gradient)

    def hidden_half(which):
        return HB.at[pl.ds(pl.multiple_of(which * 1024, 1024), 1024), :]

    hidden_swap = core_copy(hidden_half(1 - r), HREC, 5, 18)
    hidden_swap.start()
    project_swap = core_copy(PACC, PREC, 6, 19)
    project_swap.start()
    advance(wave(spatial_strips, 0))
    advance(wave(proto_strips, 2))
    advance(wave(expand_strips, 1))
    hidden_swap.wait_recv()
    hidden_half(r)[...] += HREC[...]

    @pl.loop(1, GROUP)
    def _(k):
        to = lax.rem(d + k, GROUP)
        pltpu.make_async_remote_copy(
            HB.at[pl.ds(pl.multiple_of(r * 1024 + to * 64, 64), 64), :],
            HAL.at[d],
            row_sem.at[3],
            row_sem.at[4],
            device_id=(r, to),
            device_id_type=MESH,
        ).start()

    HAL[d] = HB[pl.ds(pl.multiple_of(r * 1024 + d * 64, 64), 64), :]

    project_swap.wait()
    PACC[...] = jnp.where(big, PACC[...], PREC[...]) + jnp.where(big, PREC[...], PACC[...])
    serves = (d // 8) == r
    first_owner = lax.rem(2 * d, GROUP)
    for half in range(2):
        owner = first_owner + half
        part = PACC.at[pl.ds(64 * half, 64), :]
        local = owner == d

        @pl.when(serves & jnp.logical_not(local))
        def _():
            pltpu.make_async_remote_copy(
                part, PIN, core_send.at[7 + half], row_sem.at[5],
                device_id=(r, owner), device_id_type=MESH,
            ).start()

        @pl.when(serves & local)
        def _():
            PIN[...] = part[...]

    chip_of_own = (r * GROUP + d) // 2
    from_self = chip_of_own == d

    advance(wave(reduce_strips, 0))
    advance(wave(proto_strips, 3))
    proto_own_rows = pl.ds(pl.multiple_of(r * PROTO_HALF + d * 96, 16), 96)
    TAB[proto_own_rows, :] = RC_P[pl.ds(pl.multiple_of(d * 96, 16), 96), :]
    proto_orders = ((8, 4, 1, 2), (8, 1, 2, 4), (8, 2, 4, 1))
    every_lane = slice(0, LANES)

    def proto_gather(stage):
        for p, order in enumerate(proto_orders):
            gather_start(
                TAB, r * PROTO_HALF + 32 * p, 96, 32, every_lane, order, stage, 3 + p
            )

    def proto_wait(stage, sems):
        for p in range(3):
            gather_wait(TAB, 32, every_lane, stage, 3 + p, sems)

    def proto_arrived(stage):
        proto_wait(stage, gather_recv)

    proto_gather(0)
    advance(wave(spatial_strips, 1))
    proto_arrived(0)
    proto_gather(1)
    advance(wave(reduce_strips, 1))
    advance(wave(expand_strips, 2))
    proto_arrived(1)
    proto_gather(2)
    advance(wave(spatial_strips, 2))
    advance(wave(expand_strips, 3))
    proto_arrived(2)
    proto_gather(3)
    advance(wave(reduce_strips, 2))
    for j in range(4):
        for q in range(4):
            expand_out[pl.ds(4 * j + q, 16, stride=16), :] = RC_E[
                pl.ds(pl.multiple_of(256 * j + d * 16, 16), 16), lanes(q)
            ]
    proto_arrived(3)
    proto_part = TAB.at[pl.ds(pl.multiple_of(r * PROTO_HALF, LANES), PROTO_HALF), :]
    proto_far = core_copy(proto_part, proto_part, 9, 20)
    proto_far.start()
    far.wait()
    both = jnp.where(big, FAR[0], FAR[1]) + jnp.where(big, FAR[1], FAR[0])
    gain_out[...] = both[0:40]
    shift_out[0:40, :] = both[48:88]
    shift_out[40:41, :] = both[88:89]
    loss_out[...] = both[89:90, 0:1] / float(GROUP * IMAGES)
    arrived = HAL.at[pl.ds(0, GROUP - 1)]
    pltpu.make_async_copy(arrived, arrived, row_sem.at[4]).wait()
    pltpu.make_async_copy(arrived, arrived, row_sem.at[3]).wait()
    for source in range(GROUP):
        hidden_out[pl.ds(source, 64, stride=16), :] = HAL[source]

    @pl.when(jnp.logical_not(from_self))
    def _():
        pltpu.make_async_copy(PIN, PIN, row_sem.at[5]).wait()

    project_out[...] = PIN[...]
    for half in range(2):

        @pl.when(serves & jnp.logical_not(first_owner + half == d))
        def _():
            pltpu.make_async_copy(PIN, PIN, core_send.at[7 + half]).wait()

    proto_far.wait()
    hidden_swap.wait_send()
    for stage in range(4):
        proto_wait(stage, gather_send)
    for c in range(PADDED // LANES):
        TAB[c * LANES : c * LANES + LANES, :] = TAB[c * LANES : c * LANES + LANES, :].T
    lane_row = lax.broadcasted_iota(jnp.int32, (8, LANES), 1)
    carry = jnp.zeros((8, LANES), F32)
    for b in range(16):
        offset = (PROTOS * b) % LANES
        first = (PROTOS * b) // LANES
        whole = (offset + PROTOS) // LANES
        for t in range(whole + 1):
            if t < PADDED // LANES:
                tile = TAB[pl.ds(LANES * t + b, 8, stride=16), :]
                turned = pltpu.roll(tile, offset, 1) if offset else tile
            else:
                turned = jnp.zeros((8, LANES), F32)
            line = jnp.where(lane_row < offset, carry, turned) if offset else turned
            if t < whole:
                HB[pl.ds(first + t, 8, stride=375), :] = line
                carry = turned
            else:
                carry = line
    flat_copy = pltpu.make_async_copy(HB.at[pl.ds(0, PROTOS), :], proto_out, out_sem.at[2])
    flat_copy.start()
    advance(wave(spatial_strips, 3))
    for q in range(4):
        spatial_out[pl.ds(q, 144, stride=4), :] = C3[
            pl.ds(pl.multiple_of(d * 144, 16), 144), lanes(q)
        ]
    advance(wave(reduce_strips, 3))
    for q in range(4):
        reduce_out[pl.ds(q, 64, stride=4), :] = C3[
            pl.ds(pl.multiple_of(SPATIAL_HALF + d * 64, 16), 64), lanes(q)
        ]


    @pl.when(big)
    def _():
        forward_units.wait_send()

    proto_swap.wait_send()
    for stage in range(4):

        def pooled_sent(depth):
            for number, (columns, _) in enumerate(pooled_parts):
                gather_wait(PG, depth, columns, stage, number, gather_send)

        by_size(pooled_sent)
        rows_arrived(stage, gather_send)
    for strip in spatial_strips + reduce_strips + expand_strips + proto_strips:
        strip.close()
    flat_copy.wait()
    for slot in range(4):
        ring(slot)[1].wait_send()
    pltpu.make_async_copy(feature_out.at[0], feature_out.at[0], out_sem.at[0]).wait()


def tower(
    features,
    crop_counts,
    crop_image,
    w_reduce,
    w_spatial,
    w_expand,
    w_hidden,
    w_project,
    prototypes,
    norm_gain,
    norm_shift,
):
    anywhere = pl.BlockSpec(memory_space=pl.ANY)
    inside = pl.BlockSpec(memory_space=pltpu.VMEM)
    in_hbm = pl.BlockSpec(memory_space=pltpu.HBM)

    def vm(*shape, dtype=F32):
        return pltpu.VMEM(shape, dtype)

    dma = pltpu.SemaphoreType.DMA

    def shaped(*shape):
        return jax.ShapeDtypeStruct(shape, F32)

    return pl.pallas_call(
        tower_kernel,
        out_shape=(
            shaped(1, 1),
            shaped(1, ROWS, DEPTH),
            shaped(256, LANES),
            shaped(576, LANES),
            shaped(256, LANES),
            shaped(1024, LANES),
            shaped(64, LANES),
            shaped(PROTOS, FEATS),
            shaped(40, LANES),
            shaped(41, LANES),
            shaped(GROUP * SLOTS, DEPTH),
            shaped(3, 15 * 48, WIDTH),
            shaped(3, 15 * 24, WIDTH),
            shaped(3, 15 * 24, WIDTH),
            shaped(3, 15 * 32, LANES),
        ),
        in_specs=[anywhere, inside, inside] + [anywhere] * 6 + [inside, inside],
        out_specs=(
            (inside, anywhere) + (inside,) * 5 + (anywhere, inside, inside) + (in_hbm,) * 5
        ),
        scratch_shapes=[
            vm(ROWS, DEPTH, dtype=BF),
            vm(DEPTH, WIDTH, dtype=BF),
            vm(9 * WIDTH, WIDTH, dtype=BF),
            vm(WIDTH, DEPTH, dtype=BF),
            vm(2, DEPTH, 256, dtype=BF),
            vm(DEPTH, LANES, dtype=BF),
            vm(HIDDEN, FEATS, dtype=BF),
            vm(PROTOS, FEATS, dtype=BF),
            vm(PADDED, FEATS, dtype=BF),
            vm(ROWS, WIDTH),
            vm(ROWS, WIDTH),
            vm(SPATIAL_HALF + 1024, WIDTH),
            vm(4 * ROWS, WIDTH),
            vm(ROWS + 2 * EDGE, WIDTH),
            vm(ROWS, 9 * WIDTH, dtype=BF),
            vm(ROWS, WIDTH, dtype=BF),
            vm(WIDTH, ROWS, dtype=BF),
            vm(SLOTS, DEPTH, dtype=BF),
            vm(4, SLOTS, WIDTH),
            vm(SLOTS, HIDDEN, dtype=BF),
            vm(4, SLOTS, WIDTH),
            vm(SLOTS, HIDDEN, dtype=BF),
            vm(SLOTS, PADDED, dtype=BF),
            vm(SLOTS, FEATS, dtype=BF),
            vm(SLOTS, FEATS),
            vm(GROUP * SLOTS, FEATS),
            vm(PADDED, GROUP * IMAGES),
            vm(2 * IMAGES, PADDED),
            vm(GROUP * IMAGES, LANES),
            vm(GROUP * IMAGES, LANES),
            vm(GROUP, 2 * IMAGES, FEATS),
            vm(2 * IMAGES, FEATS),
            vm(ROWS, LANES),
            vm(SLOTS, LANES),
            vm(ROWS, LANES),
            vm(ROWS, SLOTS, dtype=BF),
            vm(SLOTS, ROWS, dtype=BF),
            vm(4, 8, LANES),
            vm(4, 8, LANES),
            vm(16, 8, LANES),
            vm(16, 8, LANES),
            vm(EXCHANGES, 8, LANES),
            vm(EXCHANGES, GROUP, 8, LANES),
            vm(2, 96, LANES),
            vm(1024, WIDTH),
            vm(1024, WIDTH),
            vm(PROTO_HALF, LANES),
            vm(PROTO_HALF, LANES),
            vm(2, 8 * 48, WIDTH),
            vm(2, 8 * 32, LANES),
            vm(DEPTH + 1024, LANES),
            vm(GROUP, 64, LANES),
            vm(LANES, LANES),
            vm(LANES, LANES),
            vm(64, LANES),
            dma((7,)),
            dma((EXCHANGES,)),
            dma((EXCHANGES,)),
            dma((4,)),
            dma((4,)),
            dma((2,)),
            dma((2,)),
            dma((12, 4)),
            dma((12, 4)),
            dma((2,)),
            dma((7, 4)),
            dma((7, 4)),
            dma((10,)),
            dma((21,)),
            dma((6,)),
            pltpu.SemaphoreType.REGULAR,
        ],
        compiler_params=pltpu.CompilerParams(
            collective_id=0, has_side_effects=True, vmem_limit_bytes=63 << 20
        ),
    )(
        features,
        crop_image.reshape(1, SLOTS),
        crop_counts.reshape(1, IMAGES),
        w_reduce,
        w_spatial,
        w_expand,
        w_hidden,
        w_project,
        prototypes.T,
        norm_gain.reshape(40, LANES),
        norm_shift.reshape(41, LANES),
    )


FEATURE_PARTS = 7


def copy_kernel(count, *refs):
    sources, targets = refs[:count], refs[count : 2 * count]
    held = refs[2 * count : 3 * count]
    in_sem, out_sem = refs[3 * count :]
    depth = ROWS // FEATURE_PARTS
    triples = list(zip(sources[1:], held[1:], targets[1:]))
    for p in range(FEATURE_PARTS):
        rows = (0, pl.ds(p * depth, depth))
        triples.append((sources[0].at[rows], held[0].at[rows], targets[0].at[rows]))
    triples.sort(key=lambda t: -t[0].size)
    ins = [
        pltpu.make_async_copy(source, room, in_sem.at[k])
        for k, (source, room, _) in enumerate(triples)
    ]
    outs = [
        pltpu.make_async_copy(room, target, out_sem.at[k])
        for k, (_, room, target) in enumerate(triples)
    ]
    for copy in ins:
        copy.start()
    for copy, follow in zip(ins, outs):
        copy.wait()
        follow.start()
    for copy in outs:
        copy.wait()


def handed_on(arrays):
    count = len(arrays)
    anywhere = pl.BlockSpec(memory_space=pl.ANY)
    dma = pltpu.SemaphoreType.DMA
    return pl.pallas_call(
        functools.partial(copy_kernel, count),
        out_shape=tuple(jax.ShapeDtypeStruct(a.shape, a.dtype) for a in arrays),
        in_specs=[anywhere] * count,
        out_specs=(anywhere,) * count,
        scratch_shapes=[pltpu.VMEM(a.shape, a.dtype) for a in arrays]
        + [dma((count - 1 + FEATURE_PARTS,)), dma((count - 1 + FEATURE_PARTS,))],
        compiler_params=pltpu.CompilerParams(vmem_limit_bytes=62 << 20),
    )(*arrays)


def fused_body(*arrays):
    loss, *results = tower(*arrays)[:10]
    feature, *flats, loss = handed_on(results + [loss])
    return (loss.reshape(()), feature) + tuple(a.reshape(-1) for a in flats)


def solution(mesh):
    return jax.shard_map(
        fused_body if mesh.shape["dp"] == GROUP else body,
        mesh=mesh,
        in_specs=(P("res", "dp", None), P("dp"), P("dp"), P(), P(), P(), P(), P(), P(), P(), P()),
        out_specs=(
            P(),
            P("res", "dp", None),
            P(("res", "dp")),
            P(("res", "dp")),
            P(("res", "dp")),
            P(("res", "dp")),
            P(("res", "dp")),
            P(),
            P(),
            P(),
        ),
        check_vma=False,
    )
```
